512 devices in a mesh: ctx: 32 (over x_hi, z), head: 8 (over y, x_lo), dp: 2 (over core).
Axes of the slice: x: 4 (x_hi: 2, x_lo: 2; x = x_hi * 2 + x_lo), y: 4, z: 16, core: 2. Of those that a mesh axis runs over, the one named last changes fastest.
Arguments:
- queries: bfloat16 [8192, 3072], P(('dp', 'ctx'), 'head'), parts along dimension 0, may hold values from -5.5 to 5.5
- keys: bfloat16 [8192, 3072], P(('dp', 'ctx'), 'head'), parts along dimension 0, may hold values from -5.5 to 5.5
- values: bfloat16 [8192, 3072], P(('dp', 'ctx'), 'head'), parts along dimension 0, may hold values from -6 to 6
- tan_queries: bfloat16 [8192, 3072], P(('dp', 'ctx'), 'head'), parts along dimension 0, may hold values from -6 to 6
- tan_keys: bfloat16 [8192, 3072], P(('dp', 'ctx'), 'head'), parts along dimension 0, may hold values from -6 to 6
- tan_values: bfloat16 [8192, 3072], P(('dp', 'ctx'), 'head'), parts along dimension 0, may hold values from -6 to 6
- out_weight: bfloat16 [3072, 5120], P('head'), may hold values from -0.15625 to 0.15625
- clip_lengths: int32 [32], P('dp'), parts along dimension 0, may hold values from 1 to 1024, 4096 in all
- stretch_order: int32 [128], P('dp'), parts along dimension 0, may hold values from 0 to 63, each once
Outputs:
- attended: bfloat16 [8192, 5120], P(('dp', 'ctx'), 'head'), parts along dimension 0
- tan_attended: bfloat16 [8192, 5120], P(('dp', 'ctx'), 'head'), parts along dimension 0
The draws below stay inside these ranges and needn't reach their ends.
There are 2 independent parts, one for each index of `dp`. The reference program is written for one: setup_inputs(seed, part) draws one part's arguments, and reference() takes and returns one part's arrays. A program takes and returns all parts, laid end to end along the dimension named above; an argument that names none is the same for every part. Nothing has to cross between parts.
Inputs may be any that keep to these rules, and one draw needn't show every extreme that they name: `stretch_order`: each is a permutation. `clip_lengths`: they sum to 4096; the longest is 1024.
All inputs are finite; a program needn't handle non-finite values.
Results may differ from the reference program's by a relative error of at most 0.02.
Values may be sent and summed in bfloat16 or wider, within the bound.
A program may use at most 64 MiB of HBM per device.

```python
import math
import jax
import jax.numpy as jnp
import numpy as np
from jax import lax

D = 5120
HDIM = 128
HEADS = 24
CLIPS = 16
SEQ = 4096
HALF = 64
MOST = 1024
N_CTX = 32
N_HEAD = 8


def draw_queries(key, part):
    key = jax.random.fold_in(key, 5)
    result = jnp.clip(jax.random.normal(key, (SEQ, HEADS * HDIM), jnp.float32), -4.0, 4.0)
    return result.astype(jnp.bfloat16)


def draw_keys(key, part):
    key = jax.random.fold_in(key, 7)
    result = jnp.clip(jax.random.normal(key, (SEQ, HEADS * HDIM), jnp.float32), -4.0, 4.0)
    return result.astype(jnp.bfloat16)


def strengthened(drawn, stream_key, source, target, blocks, factor):
    def block_of(axis_at):
        return (jnp.arange(drawn.shape[axis_at]) // (drawn.shape[axis_at] // blocks)).reshape((-1,) + (1,) * (drawn.ndim - 1 - axis_at))

    near = jax.random.permutation(stream_key, blocks)[block_of(target)]
    other_side = (block_of(target) + blocks // 2) % blocks
    return jnp.where((block_of(source) == near) | (block_of(source) == other_side), factor * drawn, drawn)


def levels(own_key, extent, shards, least, high):
    factor_of, own = 1.0, jax.random.fold_in(own_key, 6)
    for axis_at, shards_of in shards:
        heights = jnp.exp(jax.random.uniform(jax.random.fold_in(own, axis_at), (shards_of,), jnp.float32, least / len(shards), high / len(shards)))
        factor_of = factor_of * jnp.repeat(heights, extent[axis_at] // shards_of).reshape([-1 if axis == axis_at else 1 for axis in range(len(extent))])
    return factor_of


def length_profile(number_of, total, reach, lean):
    portions = [(1 << 20) // math.isqrt(rank ** lean) + 1 for rank in range(2, number_of + 1)]
    rest, given = total - reach - (number_of - 1), [1] * (number_of - 1)
    while rest > 0:
        free = [i for i in range(number_of - 1) if given[i] < reach]
        mass, left = sum([portions[i] for i in free]), rest
        for i in free:
            addition = min(reach - given[i], max(1, left * portions[i] // mass), rest)
            given[i] = given[i] + addition
            rest = rest - addition
    return np.array([reach] + given)


def ragged_sizes(stream_key, amount, total, reach, slope):
    if amount == 2:
        one = jax.random.randint(stream_key, (), max(1, total - reach), min(reach, total - 1) + 1)
        return jnp.stack([one, total - one])
    sizes = jnp.asarray(length_profile(amount, total, reach, slope), jnp.int32)
    twos = (amount - 1) // 2
    source_of, sink = sizes[1:1 + 2 * twos:2], sizes[2:2 + 2 * twos:2]
    margin = jnp.minimum(source_of - 1, reach - sink)
    moved = jax.random.randint(jax.random.fold_in(stream_key, 1), (twos,), 0, 1 << 20) % (margin + 1)
    sizes = sizes.at[1:1 + 2 * twos:2].set(source_of - moved).at[2:2 + 2 * twos:2].set(sink + moved)
    return sizes[jax.random.permutation(jax.random.fold_in(stream_key, 2), amount)]


def centred(key, dims, deviation, reach, split=(), kind=jnp.bfloat16):
    gain = levels(key, dims, split, -0.22, 0.18) if split else 1.0
    values = jax.random.normal(key, dims, jnp.float32) * deviation * gain
    return jnp.minimum(jnp.maximum(values, -reach), reach).astype(kind)


def gaussian_with(key, shape, scale, most, pieces, heavy, kind=jnp.bfloat16):
    values = scale * jax.random.normal(key, shape, jnp.float32)
    if pieces:
        values = values * levels(key, shape, pieces, -0.22, 0.18)
    return jnp.clip(strengthened(values, jax.random.fold_in(key, 3), *heavy), -most, most).astype(kind)


def setup_inputs(seed: int = 0, part: int = 0) -> dict:
    streams_of = jax.random.split(jax.random.key(seed), 10)
    own_keys = jax.random.split(jax.random.fold_in(streams_of[9], part), 10)
    queries = draw_queries(jax.random.fold_in(jax.random.fold_in(streams_of[9], part), 71), part)
    keys = draw_keys(jax.random.fold_in(jax.random.fold_in(streams_of[9], part), 71), part)
    values = centred(own_keys[2], (SEQ, HEADS * HDIM), 1.0, 6.0, ((0, 32), (1, 8)))
    tan_queries = centred(own_keys[3], (SEQ, HEADS * HDIM), 1.0, 6.0, ((0, 32), (1, 8)))
    tan_keys = centred(own_keys[4], (SEQ, HEADS * HDIM), 1.0, 6.0, ((0, 32), (1, 8)))
    tan_values = centred(own_keys[5], (SEQ, HEADS * HDIM), 1.0, 6.0, ((0, 32), (1, 8)))
    out_weight = gaussian_with(streams_of[6], (HEADS * HDIM, D), (HEADS * HDIM) ** -0.5, 0.15625, ((0, 8),), (0, 1, 8, 2.0))
    clip_lengths = ragged_sizes(own_keys[7], CLIPS, SEQ, MOST, 2).astype(jnp.int32)
    stretch_order = jax.random.permutation(own_keys[8], 2 * N_CTX).astype(jnp.int32)
    return dict(queries=queries, keys=keys, values=values, tan_queries=tan_queries, tan_keys=tan_keys, tan_values=tan_values, out_weight=out_weight, clip_lengths=clip_lengths, stretch_order=stretch_order)


def segment_ids(row_ids, stretch_order, clip_ends, half_rows):
    stretch = row_ids // half_rows
    table = stretch[:, None] == jnp.arange(stretch_order.shape[0], dtype=jnp.int32)[None, :]
    anchor = jnp.sum(jnp.where(table, stretch_order[None, :], 0), axis=1).astype(jnp.int32) * half_rows + row_ids % half_rows
    return jnp.sum((clip_ends[None, :] <= anchor[:, None]).astype(jnp.int32), axis=1)


def head_attention(blocks, allowed):
    query, key_rows, value, tan_query, tan_key, tan_value = blocks
    score_scale = 1.0 / (HDIM ** 0.5)
    scores = jnp.dot(query, key_rows.T, preferred_element_type=jnp.float32) * score_scale
    tan_scores = (jnp.dot(tan_query, key_rows.T, preferred_element_type=jnp.float32)
                  + jnp.dot(query, tan_key.T, preferred_element_type=jnp.float32)) * score_scale
    masked = jnp.where(allowed, scores, -1e30)
    peak = jnp.max(masked, axis=1, keepdims=True)
    weights = jnp.where(allowed, jnp.exp(masked - peak), 0.0)
    total = jnp.sum(weights, axis=1, keepdims=True)
    products = weights * tan_scores
    tan_total = jnp.sum(products, axis=1, keepdims=True)
    weights_b = weights.astype(jnp.bfloat16)
    products_b = products.astype(jnp.bfloat16)
    primal = jnp.dot(weights_b, value, preferred_element_type=jnp.float32) / total
    tangent = (jnp.dot(products_b, value, preferred_element_type=jnp.float32)
               + jnp.dot(weights_b, tan_value, preferred_element_type=jnp.float32)) / total - (tan_total / total) * primal
    return primal, tangent


def reference(queries, keys, values, tan_queries, tan_keys, tan_values, out_weight, clip_lengths, stretch_order):
    clip_ends = jnp.cumsum(clip_lengths).astype(jnp.int32)
    row_ids = jnp.arange(SEQ, dtype=jnp.int32)
    seg = segment_ids(row_ids, stretch_order.astype(jnp.int32), clip_ends, HALF)
    allowed = seg[:, None] == seg[None, :]

    def split_heads(array):
        return array.reshape(SEQ, HEADS, HDIM).transpose(1, 0, 2)

    stacked = tuple(split_heads(a) for a in (queries, keys, values, tan_queries, tan_keys, tan_values))
    primal, tangent = lax.map(lambda blocks: head_attention(blocks, allowed), stacked)
    heads_out = primal.transpose(1, 0, 2).reshape(SEQ, HEADS * HDIM).astype(jnp.bfloat16)
    tan_heads_out = tangent.transpose(1, 0, 2).reshape(SEQ, HEADS * HDIM).astype(jnp.bfloat16)
    group_width = HEADS * HDIM // N_HEAD
    attended = jnp.zeros((SEQ, D), jnp.float32)
    tan_attended = jnp.zeros((SEQ, D), jnp.float32)
    for group in range(N_HEAD):
        lower = group * group_width
        weight_rows = out_weight[lower:lower + group_width]
        term = jnp.dot(heads_out[:, lower:lower + group_width], weight_rows, preferred_element_type=jnp.float32).astype(jnp.bfloat16)
        tan_term = jnp.dot(tan_heads_out[:, lower:lower + group_width], weight_rows, preferred_element_type=jnp.float32).astype(jnp.bfloat16)
        term = lax.optimization_barrier(term)
        tan_term = lax.optimization_barrier(tan_term)
        attended = attended + term.astype(jnp.float32)
        tan_attended = tan_attended + tan_term.astype(jnp.float32)
    return attended.astype(jnp.bfloat16), tan_attended.astype(jnp.bfloat16)
```

```python
import functools

import jax
import jax.numpy as jnp
from jax import lax
from jax.experimental import pallas as pl
from jax.experimental.pallas import tpu as pltpu
from jax.sharding import PartitionSpec as P

HDIM = 128
PIECES = 4
NONE_SEEN = -1e29
MASKED = -1e30


def dot(a, b):
    return lax.dot_general(a, b, (((1,), (0,)), ((), ())), preferred_element_type=jnp.float32)


def dot_nt(a, b):
    return lax.dot_general(a, b, (((1,), (1,)), ((), ())), preferred_element_type=jnp.float32)


def kernel(
    nz,
    n_head,
    q_in,
    k_in,
    v_in,
    tq_in,
    tk_in,
    tv_in,
    w_in,
    lengths,
    order,
    out,
    tan_out,
    stage,
    qbuf,
    kbuf,
    vbuf,
    wbuf,
    bounds,
    stats,
    acc,
    own_o,
    own_stats,
    o_send,
    s_send,
    o_recv,
    s_recv,
    gbuf,
    total,
    stage_sem,
    ring_send,
    ring_recv,
    q_sem,
    w_sem,
    w_own_sem,
    o_sem,
    s_sem,
    g_send,
    g_recv,
):
    rows = q_in.shape[0]
    heads = q_in.shape[1] // HDIM
    half = rows // 2
    clips = lengths.shape[0]
    depth = nz // 2
    ncol = wbuf.shape[2]
    scale = 1.0 / HDIM**0.5

    ctx = lax.axis_index("ctx")
    hd = lax.axis_index("head")
    column = ctx // nz
    z = ctx % nz
    right = column * nz + (z + 1) % nz
    left = column * nz + (z + nz - 1) % nz
    partner = (ctx + nz) % (2 * nz)

    stages = [
        pltpu.make_async_copy(ref, stage.at[i], stage_sem.at[i])
        for i, ref in enumerate((k_in, tk_in, v_in, tv_in, q_in, tq_in))
    ]
    for copy in stages:
        copy.start()
    own_w = pltpu.make_async_copy(
        w_in.at[:, :, pl.ds(pl.multiple_of(hd * ncol, 128), ncol)],
        wbuf.at[:, pl.ds(pl.multiple_of(hd * HDIM, HDIM), HDIM), :],
        w_own_sem,
    )
    own_w.start()

    barrier = pltpu.get_barrier_semaphore()
    for other in (right, left, partner):
        pl.semaphore_signal(barrier, inc=1, device_id={"ctx": other})
    for i in range(1, n_head):
        pl.semaphore_signal(barrier, inc=1, device_id={"head": (hd + i) % n_head})

    ends = []
    running = jnp.int32(0)
    for c in range(clips):
        running = running + lengths[c]
        ends.append(running)
    lane = lax.broadcasted_iota(jnp.int32, (1, rows), 1)
    for slot, index in enumerate((ctx, partner)):
        anchor = jnp.where(
            lane < half,
            order[2 * index] * half + lane,
            order[2 * index + 1] * half + lane - half,
        )
        low = jnp.zeros_like(anchor)
        high = jnp.full_like(anchor, rows * nz * 2)
        for end in ends:
            low = jnp.where(end <= anchor, jnp.maximum(low, end), low)
            high = jnp.where(end > anchor, jnp.minimum(high, end), high)
        bounds[0:1, slot * rows : (slot + 1) * rows] = low
        bounds[1:2, slot * rows : (slot + 1) * rows] = high

    for copy in stages:
        copy.wait()
    for h in range(heads):
        cols = slice(h * HDIM, (h + 1) * HDIM)
        kbuf[h, z, :, 0:HDIM] = stage[0, :, cols]
        kbuf[h, z, :, HDIM : 2 * HDIM] = stage[1, :, cols]
        vbuf[h, z, 0:HDIM, :] = stage[2, :, cols].astype(jnp.float32).T.astype(jnp.bfloat16)
        vbuf[h, z, HDIM : 2 * HDIM, :] = stage[3, :, cols].astype(jnp.float32).T.astype(jnp.bfloat16)
        qbuf[0, h, :, HDIM : 2 * HDIM] = stage[4, :, cols]
        qbuf[0, h, :, 0:HDIM] = stage[5, :, cols]

    def ring_copy(h, hop, piece, side):
        source = (z + nz - hop) % nz if side == 0 else (z + hop) % nz
        step = h * depth + hop
        buf = kbuf if piece < 2 else vbuf
        size = buf.shape[2] // 2
        ref = buf.at[h, source, pl.ds((piece % 2) * size, size), :]
        return pltpu.make_async_remote_copy(
            src_ref=ref,
            dst_ref=ref,
            send_sem=ring_send.at[side, piece, step % 2],
            recv_sem=ring_recv.at[side, piece, step],
            device_id={"ctx": right if side == 0 else left},
        )

    def q_copy(h):
        return pltpu.make_async_remote_copy(
            src_ref=qbuf.at[0, h],
            dst_ref=qbuf.at[1, h],
            send_sem=q_sem.at[0, h],
            recv_sem=q_sem.at[1, h],
            device_id={"ctx": partner},
        )

    def w_copy(i):
        other = (hd + i) % n_head
        return pltpu.make_async_remote_copy(
            src_ref=w_in.at[:, :, pl.ds(pl.multiple_of(other * ncol, 128), ncol)],
            dst_ref=wbuf.at[:, pl.ds(pl.multiple_of(hd * HDIM, HDIM), HDIM), :],
            send_sem=w_sem.at[0, i - 1],
            recv_sem=w_sem.at[1, i - 1],
            device_id={"head": other},
        )

    def o_copies(h):
        return [
            pltpu.make_async_remote_copy(
                src_ref=src.at[h],
                dst_ref=dst.at[h],
                send_sem=sem.at[0, h],
                recv_sem=sem.at[1, h],
                device_id={"ctx": partner},
            )
            for src, dst, sem in ((s_send, s_recv, s_sem), (o_send, o_recv, o_sem))
        ]

    def g_copy(h, i):
        return pltpu.make_async_remote_copy(
            src_ref=gbuf.at[h, hd],
            dst_ref=gbuf.at[h, hd],
            send_sem=g_send.at[h, i - 1],
            recv_sem=g_recv.at[h, i - 1],
            device_id={"head": (hd + i) % n_head},
        )

    pl.semaphore_wait(barrier, 2 + n_head)
    for piece in range(PIECES):
        for side in range(2):
            ring_copy(0, 0, piece, side).start()
    for h in range(heads):
        q_copy(h).start()
    for i in range(1, n_head):
        w_copy(i).start()
    total[...] = jnp.zeros_like(total)
    s_send[...] = jnp.zeros_like(s_send)

    def allowed_keys(source):
        low, high = bounds[0:1, :], bounds[1:2, :]
        index = column * nz + source
        position = lax.broadcasted_iota(jnp.int32, (half, 2 * rows), 0)
        parts = []
        for part in range(2):
            first = order[2 * index + part] * half
            parts.append(jnp.logical_and(position >= low - first, position < high - first))
        return parts

    def attend(h, first, second):
        key = jnp.concatenate([kbuf[h, first], kbuf[h, second]], axis=0)
        query = jnp.concatenate([qbuf[0, h], qbuf[1, h]], axis=0)
        scores = dot_nt(key[:, :HDIM], query[:, HDIM:]) * scale
        tan_scores = dot_nt(key, query) * scale
        masks = allowed_keys(first) + allowed_keys(second)
        masked = jnp.concatenate(
            [
                jnp.where(mask, scores[i * half : (i + 1) * half], MASKED)
                for i, mask in enumerate(masks)
            ],
            axis=0,
        )
        peak = stats[0:1, :]
        new_peak = jnp.maximum(peak, jnp.max(masked, axis=0, keepdims=True))
        weights = jnp.exp(masked - new_peak)
        rescale = jnp.exp(peak - new_peak)
        products = weights * tan_scores
        stats[0:1, :] = new_peak
        stats[1:2, :] = rescale * stats[1:2, :] + jnp.sum(weights, axis=0, keepdims=True)
        stats[2:3, :] = rescale * stats[2:3, :] + jnp.sum(products, axis=0, keepdims=True)
        value = jnp.concatenate([vbuf[h, first], vbuf[h, second]], axis=1)
        weights_b = weights.astype(jnp.bfloat16)
        both = dot(value, weights_b)
        moved = dot(value[:HDIM], products.astype(jnp.bfloat16))
        acc[0:HDIM, :] = rescale * acc[0:HDIM, :] + both[:HDIM]
        acc[HDIM:, :] = rescale * acc[HDIM:, :] + both[HDIM:] + moved

    def finish(h):
        sums = stats[1:2, :]
        inverse = jnp.where(sums > 0.0, 1.0 / jnp.where(sums > 0.0, sums, 1.0), 0.0)
        mean = stats[2:3, :] * inverse
        primal = acc[0:HDIM, :] * inverse
        tangent = acc[HDIM:, :] * inverse - mean * primal
        own_o[h, 0:HDIM, :] = primal[:, :rows]
        own_o[h, HDIM:, :] = tangent[:, :rows]
        o_send[h, 0:HDIM, :] = primal[:, rows:].astype(jnp.bfloat16)
        o_send[h, HDIM:, :] = tangent[:, rows:].astype(jnp.bfloat16)
        for i, row in enumerate((stats[0:1, :], sums, mean)):
            own_stats[h, i : i + 1, :] = row[:, :rows]
            s_send[h, i : i + 1, :] = row[:, rows:]
        for copy in o_copies(h):
            copy.start()

    def merge(h):
        for copy in o_copies(h):
            copy.wait()
        peaks, sums, means = [], [], []
        for ref in (own_stats, s_recv):
            peaks.append(ref[h, 0:1, :])
            sums.append(ref[h, 1:2, :])
            means.append(ref[h, 2:3, :])
        peak = jnp.maximum(peaks[0], peaks[1])
        shares = [sums[i] * jnp.exp(peaks[i] - peak) for i in range(2)]
        inverse = 1.0 / (shares[0] + shares[1])
        shares = [share * inverse for share in shares]
        mean = shares[0] * means[0] + shares[1] * means[1]
        primals = [own_o[h, 0:HDIM, :], o_recv[h, 0:HDIM, :].astype(jnp.float32)]
        tangents = [own_o[h, HDIM:, :], o_recv[h, HDIM:, :].astype(jnp.float32)]
        primal = shares[0] * primals[0] + shares[1] * primals[1]
        tangent = sum(
            shares[i] * (tangents[i] + (means[i] - mean) * primals[i]) for i in range(2)
        )
        gbuf[h, hd, 0:rows, :] = primal.T.astype(jnp.bfloat16)
        gbuf[h, hd, rows:, :] = tangent.T.astype(jnp.bfloat16)
        for i in range(1, n_head):
            g_copy(h, i).start()

    def project(h):
        for i in range(1, n_head):
            g_copy(h, i).wait()
        features = jnp.concatenate([gbuf[h, g] for g in range(n_head)], axis=1)
        total[...] += dot(features, wbuf[h])

    def step(index, carry):
        h = index // depth
        d = index % depth + 1

        for piece in range(PIECES):
            for side in range(2):
                crosses = (piece < 2) == (side == 0)

                def take(piece=piece, side=side, crosses=crosses):
                    arrived = ring_copy(h, d - 1, piece, side)
                    arrived.wait_recv()

                    @pl.when(d < depth if crosses else d < depth - 1)
                    def _():
                        ring_copy(h, d, piece, side).start()

                    arrived.wait_send()

                if crosses:
                    take()
                else:
                    pl.when(d < depth)(take)

        @pl.when(jnp.logical_and(d == depth - 1, h < heads - 1))
        def _():
            for piece in range(PIECES):
                for side in range(2):
                    ring_copy(h + 1, 0, piece, side).start()

        @pl.when(d == 1)
        def _():
            stats[0:1, :] = jnp.full((1, 2 * rows), NONE_SEEN, jnp.float32)
            stats[1:3, :] = jnp.zeros((2, 2 * rows), jnp.float32)
            acc[...] = jnp.zeros_like(acc)
            q_copy(h).wait()

        attend(h, (z + nz - d) % nz, (z + d % depth) % nz)

        @pl.when(jnp.logical_and(d == 2, h >= 1))
        def _():
            merge(h - 1)

        @pl.when(jnp.logical_and(d == depth // 2, h == heads - 1))
        def _():
            own_w.wait()
            for i in range(1, n_head):
                w_copy(i).wait()

        for early in range(heads - 1):

            @pl.when(jnp.logical_and(d == depth // 2 + early, h == heads - 1))
            def _(early=early):
                project(early)

        @pl.when(d == depth)
        def _():
            finish(h)

        return carry

    lax.fori_loop(0, heads * depth, step, 0)
    merge(heads - 1)
    project(heads - 1)
    out[...] = total[0:rows, :].astype(out.dtype)
    tan_out[...] = total[rows:, :].astype(tan_out.dtype)


def local(
    queries,
    keys,
    values,
    tan_queries,
    tan_keys,
    tan_values,
    out_weight,
    clip_lengths,
    stretch_order,
):
    rows, width = queries.shape
    heads = width // HDIM
    n_head = lax.axis_size("head")
    nz = lax.axis_size("ctx") // 2
    depth = nz // 2
    ncol = out_weight.shape[1] // n_head
    bf16, f32 = jnp.bfloat16, jnp.float32
    weight = out_weight.reshape(heads, HDIM, out_weight.shape[1])
    dma = pltpu.SemaphoreType.DMA
    anywhere = pl.BlockSpec(memory_space=pl.ANY)
    in_smem = pl.BlockSpec(memory_space=pltpu.SMEM)
    in_vmem = pl.BlockSpec(memory_space=pltpu.VMEM)
    return pl.pallas_call(
        functools.partial(kernel, nz, n_head),
        out_shape=(
            jax.ShapeDtypeStruct((rows, ncol), bf16),
            jax.ShapeDtypeStruct((rows, ncol), bf16),
        ),
        in_specs=[anywhere] * 7 + [in_smem] * 2,
        out_specs=(in_vmem, in_vmem),
        scratch_shapes=[
            pltpu.VMEM((6, rows, width), bf16),
            pltpu.VMEM((2, heads, rows, 2 * HDIM), bf16),
            pltpu.VMEM((heads, nz, rows, 2 * HDIM), bf16),
            pltpu.VMEM((heads, nz, 2 * HDIM, rows), bf16),
            pltpu.VMEM((heads, n_head * HDIM, ncol), bf16),
            pltpu.VMEM((8, 2 * rows), jnp.int32),
            pltpu.VMEM((8, 2 * rows), f32),
            pltpu.VMEM((2 * HDIM, 2 * rows), f32),
            pltpu.VMEM((heads, 2 * HDIM, rows), f32),
            pltpu.VMEM((heads, 8, rows), f32),
            pltpu.VMEM((heads, 2 * HDIM, rows), bf16),
            pltpu.VMEM((heads, 8, rows), f32),
            pltpu.VMEM((heads, 2 * HDIM, rows), bf16),
            pltpu.VMEM((heads, 8, rows), f32),
            pltpu.VMEM((heads, n_head, 2 * rows, HDIM), bf16),
            pltpu.VMEM((2 * rows, ncol), f32),
            dma((6,)),
            dma((2, PIECES, 2)),
            dma((2, PIECES, heads * depth)),
            dma((2, heads)),
            dma((2, n_head - 1)),
            dma,
            dma((2, heads)),
            dma((2, heads)),
            dma((heads, n_head - 1)),
            dma((heads, n_head - 1)),
        ],
        compiler_params=pltpu.CompilerParams(
            collective_id=0,
            has_side_effects=True,
            vmem_limit_bytes=40 * 1024 * 1024,
        ),
        cost_estimate=pl.CostEstimate(
            flops=2 * 6 * 2 * rows * nz * rows * width + 4 * rows * n_head * width * ncol,
            bytes_accessed=8 * 1024 * 1024,
            transcendentals=2 * rows * nz * rows * heads,
        ),
    )(
        queries,
        keys,
        values,
        tan_queries,
        tan_keys,
        tan_values,
        weight,
        clip_lengths,
        stretch_order,
    )


def solution(mesh):
    placed = P(("dp", "ctx"), "head")
    return jax.shard_map(
        local,
        mesh=mesh,
        in_specs=(placed,) * 6 + (P("head", None), P("dp"), P("dp")),
        out_specs=(placed, placed),
        check_vma=False,
    )
```

```python
import functools

import jax
import jax.numpy as jnp
from jax import lax
from jax.experimental import pallas as pl
from jax.experimental.pallas import tpu as pltpu
from jax.sharding import PartitionSpec as P

HDIM = 128
PIECES = 4
NONE_SEEN = -1e29
MASKED = -1e30


def dot(a, b):
    return lax.dot_general(a, b, (((1,), (0,)), ((), ())), preferred_element_type=jnp.float32)


def dot_nt(a, b):
    return lax.dot_general(a, b, (((1,), (1,)), ((), ())), preferred_element_type=jnp.float32)


def kernel(
    nz,
    n_head,
    q_in,
    k_in,
    v_in,
    tq_in,
    tk_in,
    tv_in,
    w_in,
    lengths,
    order,
    out,
    tan_out,
    stage,
    qbuf,
    kbuf,
    vbuf,
    wbuf,
    bounds,
    stats,
    acc,
    factors,
    own_o,
    own_stats,
    o_send,
    s_send,
    o_recv,
    s_recv,
    gbuf,
    total,
    stage_sem,
    ring_send,
    ring_recv,
    q_sem,
    w_sem,
    w_own_sem,
    o_sem,
    s_sem,
    g_send,
    g_recv,
):
    rows = q_in.shape[0]
    heads = q_in.shape[1] // HDIM
    half = rows // 2
    clips = lengths.shape[0]
    depth = nz // 2
    ncol = wbuf.shape[2]
    scale = 1.0 / HDIM**0.5

    ctx = lax.axis_index("ctx")
    hd = lax.axis_index("head")
    column = ctx // nz
    z = ctx % nz
    right = column * nz + (z + 1) % nz
    left = column * nz + (z + nz - 1) % nz
    partner = (ctx + nz) % (2 * nz)

    stages = [
        pltpu.make_async_copy(ref, stage.at[i], stage_sem.at[i])
        for i, ref in enumerate((k_in, tk_in, v_in, tv_in, q_in, tq_in))
    ]
    for copy in stages:
        copy.start()
    own_w = pltpu.make_async_copy(
        w_in.at[:, :, pl.ds(pl.multiple_of(hd * ncol, 128), ncol)],
        wbuf.at[:, pl.ds(pl.multiple_of(hd * HDIM, HDIM), HDIM), :],
        w_own_sem,
    )
    own_w.start()

    barrier = pltpu.get_barrier_semaphore()
    for other in (right, left, partner):
        pl.semaphore_signal(barrier, inc=1, device_id={"ctx": other})
    for i in range(1, n_head):
        pl.semaphore_signal(barrier, inc=1, device_id={"head": (hd + i) % n_head})

    ends = []
    running = jnp.int32(0)
    for c in range(clips):
        running = running + lengths[c]
        ends.append(running)
    lane = lax.broadcasted_iota(jnp.int32, (1, rows), 1)
    for slot, index in enumerate((ctx, partner)):
        anchor = jnp.where(
            lane < half,
            order[2 * index] * half + lane,
            order[2 * index + 1] * half + lane - half,
        )
        low = jnp.zeros_like(anchor)
        high = jnp.full_like(anchor, rows * nz * 2)
        for end in ends:
            low = jnp.where(end <= anchor, jnp.maximum(low, end), low)
            high = jnp.where(end > anchor, jnp.minimum(high, end), high)
        bounds[0:1, slot * rows : (slot + 1) * rows] = low
        bounds[1:2, slot * rows : (slot + 1) * rows] = high

    for copy in stages:
        copy.wait()
    for h in range(heads):
        cols = slice(h * HDIM, (h + 1) * HDIM)
        kbuf[h, z, :, 0:HDIM] = stage[0, :, cols]
        kbuf[h, z, :, HDIM : 2 * HDIM] = stage[1, :, cols]
        vbuf[h, z, 0:HDIM, :] = stage[2, :, cols].astype(jnp.float32).T.astype(jnp.bfloat16)
        vbuf[h, z, HDIM : 2 * HDIM, :] = stage[3, :, cols].astype(jnp.float32).T.astype(jnp.bfloat16)
        qbuf[0, h, :, HDIM : 2 * HDIM] = stage[4, :, cols]
        qbuf[0, h, :, 0:HDIM] = stage[5, :, cols]

    def ring_copy(h, hop, piece, side):
        source = (z + nz - hop) % nz if side == 0 else (z + hop) % nz
        step = h * depth + hop
        buf = kbuf if piece < 2 else vbuf
        size = buf.shape[2] // 2
        ref = buf.at[h, source, pl.ds((piece % 2) * size, size), :]
        return pltpu.make_async_remote_copy(
            src_ref=ref,
            dst_ref=ref,
            send_sem=ring_send.at[side, piece, h * 2 + hop % 2],
            recv_sem=ring_recv.at[side, piece, step],
            device_id={"ctx": right if side == 0 else left},
        )

    def send_own(h):
        for piece in range(PIECES):
            for side in range(2):
                ring_copy(h, 0, piece, side).start()

    def q_copy(h):
        return pltpu.make_async_remote_copy(
            src_ref=qbuf.at[0, h],
            dst_ref=qbuf.at[1, h],
            send_sem=q_sem.at[0, h],
            recv_sem=q_sem.at[1, h],
            device_id={"ctx": partner},
        )

    def w_copy(i):
        other = (hd + i) % n_head
        return pltpu.make_async_remote_copy(
            src_ref=w_in.at[:, :, pl.ds(pl.multiple_of(other * ncol, 128), ncol)],
            dst_ref=wbuf.at[:, pl.ds(pl.multiple_of(hd * HDIM, HDIM), HDIM), :],
            send_sem=w_sem.at[0, i - 1],
            recv_sem=w_sem.at[1, i - 1],
            device_id={"head": other},
        )

    def o_copies(h):
        return [
            pltpu.make_async_remote_copy(
                src_ref=src.at[h],
                dst_ref=dst.at[h],
                send_sem=sem.at[0, h],
                recv_sem=sem.at[1, h],
                device_id={"ctx": partner},
            )
            for src, dst, sem in ((s_send, s_recv, s_sem), (o_send, o_recv, o_sem))
        ]

    def g_copy(h, i):
        return pltpu.make_async_remote_copy(
            src_ref=gbuf.at[h, hd],
            dst_ref=gbuf.at[h, hd],
            send_sem=g_send.at[h, i - 1],
            recv_sem=g_recv.at[h, i - 1],
            device_id={"head": (hd + i) % n_head},
        )

    pl.semaphore_wait(barrier, 2 + n_head)
    for h in range(heads - 1):
        send_own(h)
    for h in range(heads):
        q_copy(h).start()
    for i in range(1, n_head):
        w_copy(i).start()
    total[...] = jnp.zeros_like(total)
    s_send[...] = jnp.zeros_like(s_send)

    def allowed_keys(source):
        low, high = bounds[0:1, :], bounds[1:2, :]
        index = column * nz + source
        position = lax.broadcasted_iota(jnp.int32, (half, 2 * rows), 0)
        parts = []
        for part in range(2):
            first = order[2 * index + part] * half
            parts.append(jnp.logical_and(position >= low - first, position < high - first))
        return parts

    def score(h, first, second):
        key = jnp.concatenate([kbuf[h, first], kbuf[h, second]], axis=0)
        query = jnp.concatenate([qbuf[0, h], qbuf[1, h]], axis=0)
        scores = dot_nt(key[:, :HDIM], query[:, HDIM:]) * scale
        tan_scores = dot_nt(key, query) * scale
        masks = allowed_keys(first) + allowed_keys(second)
        masked = jnp.concatenate(
            [
                jnp.where(mask, scores[i * half : (i + 1) * half], MASKED)
                for i, mask in enumerate(masks)
            ],
            axis=0,
        )
        peak = stats[h, 0:1, :]
        new_peak = jnp.maximum(peak, jnp.max(masked, axis=0, keepdims=True))
        weights = jnp.exp(masked - new_peak)
        rescale = jnp.exp(peak - new_peak)
        products = weights * tan_scores
        stats[h, 0:1, :] = new_peak
        stats[h, 1:2, :] = rescale * stats[h, 1:2, :] + jnp.sum(weights, axis=0, keepdims=True)
        stats[h, 2:3, :] = rescale * stats[h, 2:3, :] + jnp.sum(products, axis=0, keepdims=True)
        stats[h, 3:4, :] = rescale
        factors[0] = weights.astype(jnp.bfloat16)
        factors[1] = products.astype(jnp.bfloat16)

    def apply(h, first, second):
        value = jnp.concatenate([vbuf[h, first], vbuf[h, second]], axis=1)
        both = dot(value, factors[0])
        moved = dot(value[:HDIM], factors[1])
        rescale = stats[h, 3:4, :]
        acc[h, 0:HDIM, :] = rescale * acc[h, 0:HDIM, :] + both[:HDIM]
        acc[h, HDIM:, :] = rescale * acc[h, HDIM:, :] + both[HDIM:] + moved

    def finish(h):
        sums = stats[h, 1:2, :]
        inverse = jnp.where(sums > 0.0, 1.0 / jnp.where(sums > 0.0, sums, 1.0), 0.0)
        mean = stats[h, 2:3, :] * inverse
        primal = acc[h, 0:HDIM, :] * inverse
        tangent = acc[h, HDIM:, :] * inverse - mean * primal
        own_o[h, 0:HDIM, :] = primal[:, :rows]
        own_o[h, HDIM:, :] = tangent[:, :rows]
        o_send[h, 0:HDIM, :] = primal[:, rows:].astype(jnp.bfloat16)
        o_send[h, HDIM:, :] = tangent[:, rows:].astype(jnp.bfloat16)
        for i, row in enumerate((stats[h, 0:1, :], sums, mean)):
            own_stats[h, i : i + 1, :] = row[:, :rows]
            s_send[h, i : i + 1, :] = row[:, rows:]
        for copy in o_copies(h):
            copy.start()

    def merge(h):
        for copy in o_copies(h):
            copy.wait()
        peaks, sums, means = [], [], []
        for ref in (own_stats, s_recv):
            peaks.append(ref[h, 0:1, :])
            sums.append(ref[h, 1:2, :])
            means.append(ref[h, 2:3, :])
        peak = jnp.maximum(peaks[0], peaks[1])
        shares = [sums[i] * jnp.exp(peaks[i] - peak) for i in range(2)]
        inverse = 1.0 / (shares[0] + shares[1])
        shares = [share * inverse for share in shares]
        mean = shares[0] * means[0] + shares[1] * means[1]
        primals = [own_o[h, 0:HDIM, :], o_recv[h, 0:HDIM, :].astype(jnp.float32)]
        tangents = [own_o[h, HDIM:, :], o_recv[h, HDIM:, :].astype(jnp.float32)]
        primal = shares[0] * primals[0] + shares[1] * primals[1]
        tangent = sum(
            shares[i] * (tangents[i] + (means[i] - mean) * primals[i]) for i in range(2)
        )
        gbuf[h, hd, 0:rows, :] = primal.T.astype(jnp.bfloat16)
        gbuf[h, hd, rows:, :] = tangent.T.astype(jnp.bfloat16)
        for i in range(1, n_head):
            g_copy(h, i).start()

    def project(h):
        for i in range(1, n_head):
            g_copy(h, i).wait()
        features = jnp.concatenate([gbuf[h, g] for g in range(n_head)], axis=1)
        total[...] += dot(features, wbuf[h])

    first_part = (heads - 1) * depth
    steps = heads * depth

    def place(index):
        late = index // first_part
        h = (1 - late) * (index % (heads - 1)) + late * (heads - 1)
        d = (1 - late) * (index // (heads - 1)) + late * (index - first_part) + 1
        return h, d

    def forward(h, d, piece):
        for side in range(2):
            crosses = (piece < 2) == (side == 0)

            def take(side=side, crosses=crosses):
                arrived = ring_copy(h, d - 1, piece, side)
                arrived.wait_recv()

                @pl.when(d < depth if crosses else d < depth - 1)
                def _():
                    ring_copy(h, d, piece, side).start()

                arrived.wait_send()

            if crosses:
                take()
            else:
                pl.when(d < depth)(take)

    def step(index, carry):
        h, d = place(index)
        old_h, old_d = place(jnp.maximum(index - 1, 0))
        first, second = (z + nz - old_d) % nz, (z + old_d % depth) % nz
        live = index < steps

        @pl.when(live)
        def _():
            forward(h, d, 0)

        @pl.when(index > 0)
        def _():
            @pl.when(old_d == 1)
            def _():
                stats[old_h, 0:1, :] = jnp.full((1, 2 * rows), NONE_SEEN, jnp.float32)
                stats[old_h, 1:3, :] = jnp.zeros((2, 2 * rows), jnp.float32)
                acc[old_h] = jnp.zeros((2 * HDIM, 2 * rows), jnp.float32)
                q_copy(old_h).wait()

            score(old_h, first, second)

        @pl.when(live)
        def _():
            forward(h, d, 1)

        @pl.when(index > 0)
        def _():
            apply(old_h, first, second)

            @pl.when(old_d == depth)
            def _():
                finish(old_h)

        @pl.when(live)
        def _():
            for piece in range(2, PIECES):
                forward(h, d, piece)

        @pl.when(jnp.logical_and(d == depth - 1, h == heads - 2))
        def _():
            send_own(heads - 1)

        @pl.when(jnp.logical_and(index > first_part, index < first_part + heads))
        def _():
            merge(index - first_part - 1)

        return carry

    lax.fori_loop(0, steps + 1, step, 0)
    own_w.wait()
    for i in range(1, n_head):
        w_copy(i).wait()
    project(0)
    merge(heads - 1)
    for h in range(1, heads):
        project(h)
    out[...] = total[0:rows, :].astype(out.dtype)
    tan_out[...] = total[rows:, :].astype(tan_out.dtype)


def local(
    queries,
    keys,
    values,
    tan_queries,
    tan_keys,
    tan_values,
    out_weight,
    clip_lengths,
    stretch_order,
):
    rows, width = queries.shape
    heads = width // HDIM
    n_head = lax.axis_size("head")
    nz = lax.axis_size("ctx") // 2
    depth = nz // 2
    ncol = out_weight.shape[1] // n_head
    bf16, f32 = jnp.bfloat16, jnp.float32
    weight = out_weight.reshape(heads, HDIM, out_weight.shape[1])
    dma = pltpu.SemaphoreType.DMA
    anywhere = pl.BlockSpec(memory_space=pl.ANY)
    in_smem = pl.BlockSpec(memory_space=pltpu.SMEM)
    in_vmem = pl.BlockSpec(memory_space=pltpu.VMEM)
    return pl.pallas_call(
        functools.partial(kernel, nz, n_head),
        out_shape=(
            jax.ShapeDtypeStruct((rows, ncol), bf16),
            jax.ShapeDtypeStruct((rows, ncol), bf16),
        ),
        in_specs=[anywhere] * 7 + [in_smem] * 2,
        out_specs=(in_vmem, in_vmem),
        scratch_shapes=[
            pltpu.VMEM((6, rows, width), bf16),
            pltpu.VMEM((2, heads, rows, 2 * HDIM), bf16),
            pltpu.VMEM((heads, nz, rows, 2 * HDIM), bf16),
            pltpu.VMEM((heads, nz, 2 * HDIM, rows), bf16),
            pltpu.VMEM((heads, n_head * HDIM, ncol), bf16),
            pltpu.VMEM((8, 2 * rows), jnp.int32),
            pltpu.VMEM((heads, 8, 2 * rows), f32),
            pltpu.VMEM((heads, 2 * HDIM, 2 * rows), f32),
            pltpu.VMEM((2, 2 * rows, 2 * rows), bf16),
            pltpu.VMEM((heads, 2 * HDIM, rows), f32),
            pltpu.VMEM((heads, 8, rows), f32),
            pltpu.VMEM((heads, 2 * HDIM, rows), bf16),
            pltpu.VMEM((heads, 8, rows), f32),
            pltpu.VMEM((heads, 2 * HDIM, rows), bf16),
            pltpu.VMEM((heads, 8, rows), f32),
            pltpu.VMEM((heads, n_head, 2 * rows, HDIM), bf16),
            pltpu.VMEM((2 * rows, ncol), f32),
            dma((6,)),
            dma((2, PIECES, 2 * heads)),
            dma((2, PIECES, heads * depth)),
            dma((2, heads)),
            dma((2, n_head - 1)),
            dma,
            dma((2, heads)),
            dma((2, heads)),
            dma((heads, n_head - 1)),
            dma((heads, n_head - 1)),
        ],
        compiler_params=pltpu.CompilerParams(
            collective_id=0,
            has_side_effects=True,
            vmem_limit_bytes=60 * 1024 * 1024,
        ),
        cost_estimate=pl.CostEstimate(
            flops=2 * 6 * 2 * rows * nz * rows * width + 4 * rows * n_head * width * ncol,
            bytes_accessed=8 * 1024 * 1024,
            transcendentals=2 * rows * nz * rows * heads,
        ),
    )(
        queries,
        keys,
        values,
        tan_queries,
        tan_keys,
        tan_values,
        weight,
        clip_lengths,
        stretch_order,
    )


def solution(mesh):
    placed = P(("dp", "ctx"), "head")
    return jax.shard_map(
        local,
        mesh=mesh,
        in_specs=(placed,) * 6 + (P("head", None), P("dp"), P("dp")),
        out_specs=(placed, placed),
        check_vma=False,
    )
```

```python
import functools

import jax
import jax.numpy as jnp
from jax import lax
from jax.experimental import pallas as pl
from jax.experimental.pallas import tpu as pltpu
from jax.sharding import PartitionSpec as P

HDIM = 128
PIECES = 4
NONE_SEEN = -1e29
MASKED = -1e30


def dot(a, b):
    return lax.dot_general(a, b, (((1,), (0,)), ((), ())), preferred_element_type=jnp.float32)


def dot_nt(a, b):
    return lax.dot_general(a, b, (((1,), (1,)), ((), ())), preferred_element_type=jnp.float32)


def kernel(
    nz,
    n_head,
    q_in,
    k_in,
    v_in,
    tq_in,
    tk_in,
    tv_in,
    w_in,
    lengths,
    order,
    out,
    stage,
    qbuf,
    kbuf,
    vbuf,
    wbuf,
    bounds,
    stats,
    acc,
    factors,
    own_o,
    own_stats,
    o_send,
    s_send,
    o_recv,
    s_recv,
    gbuf,
    total,
    stage_sem,
    ring_send,
    ring_recv,
    q_sem,
    w_sem,
    w_own_sem,
    o_sem,
    s_sem,
    g_send,
    g_recv,
):
    rows = q_in.shape[0]
    heads = q_in.shape[1] // HDIM
    half = rows // 2
    clips = lengths.shape[0]
    depth = nz // 2
    ncol = wbuf.shape[2]
    scale = 1.0 / HDIM**0.5

    ctx = lax.axis_index("ctx")
    hd = lax.axis_index("head")
    column = ctx // nz
    z = ctx % nz
    right = column * nz + (z + 1) % nz
    left = column * nz + (z + nz - 1) % nz
    partner = (ctx + nz) % (2 * nz)

    stages = [
        pltpu.make_async_copy(ref, stage.at[i], stage_sem.at[i])
        for i, ref in enumerate((k_in, tk_in, v_in, tv_in, q_in, tq_in))
    ]
    for copy in stages:
        copy.start()
    own_w = pltpu.make_async_copy(
        w_in.at[:, :, pl.ds(pl.multiple_of(hd * ncol, 128), ncol)],
        wbuf.at[:, pl.ds(pl.multiple_of(hd * HDIM, HDIM), HDIM), :],
        w_own_sem,
    )
    own_w.start()

    barrier = pltpu.get_barrier_semaphore()
    for other in (right, left, partner):
        pl.semaphore_signal(barrier, inc=1, device_id={"ctx": other})
    for i in range(1, n_head):
        pl.semaphore_signal(barrier, inc=1, device_id={"head": (hd + i) % n_head})

    ends = []
    running = jnp.int32(0)
    for c in range(clips):
        running = running + lengths[c]
        ends.append(running)
    lane = lax.broadcasted_iota(jnp.int32, (1, rows), 1)
    for slot, index in enumerate((ctx, partner)):
        anchor = jnp.where(
            lane < half,
            order[2 * index] * half + lane,
            order[2 * index + 1] * half + lane - half,
        )
        low = jnp.zeros_like(anchor)
        high = jnp.full_like(anchor, rows * nz * 2)
        for end in ends:
            low = jnp.where(end <= anchor, jnp.maximum(low, end), low)
            high = jnp.where(end > anchor, jnp.minimum(high, end), high)
        bounds[0:1, slot * rows : (slot + 1) * rows] = low
        bounds[1:2, slot * rows : (slot + 1) * rows] = high

    for copy in stages:
        copy.wait()
    for h in range(heads):
        cols = slice(h * HDIM, (h + 1) * HDIM)
        kbuf[h, z, :, 0:HDIM] = stage[0, :, cols]
        kbuf[h, z, :, HDIM : 2 * HDIM] = stage[1, :, cols]
        vbuf[h, z, 0:HDIM, :] = stage[2, :, cols].astype(jnp.float32).T.astype(jnp.bfloat16)
        vbuf[h, z, HDIM : 2 * HDIM, :] = stage[3, :, cols].astype(jnp.float32).T.astype(jnp.bfloat16)
        qbuf[0, h, :, HDIM : 2 * HDIM] = stage[4, :, cols]
        qbuf[0, h, :, 0:HDIM] = stage[5, :, cols]

    def ring_copy(h, hop, piece, side):
        source = (z + nz - hop) % nz if side == 0 else (z + hop) % nz
        step = h * depth + hop
        buf = kbuf if piece < 2 else vbuf
        size = buf.shape[2] // 2
        ref = buf.at[h, source, pl.ds((piece % 2) * size, size), :]
        return pltpu.make_async_remote_copy(
            src_ref=ref,
            dst_ref=ref,
            send_sem=ring_send.at[side, piece, h * 2 + hop % 2],
            recv_sem=ring_recv.at[side, piece, step],
            device_id={"ctx": right if side == 0 else left},
        )

    def send_own(h):
        for piece in range(PIECES):
            for side in range(2):
                ring_copy(h, 0, piece, side).start()

    def q_copy(h):
        return pltpu.make_async_remote_copy(
            src_ref=qbuf.at[0, h],
            dst_ref=qbuf.at[1, h],
            send_sem=q_sem.at[0, h],
            recv_sem=q_sem.at[1, h],
            device_id={"ctx": partner},
        )

    def w_copy(h, i):
        other = (hd + i) % n_head
        return pltpu.make_async_remote_copy(
            src_ref=w_in.at[h, :, pl.ds(pl.multiple_of(other * ncol, 128), ncol)],
            dst_ref=wbuf.at[h, pl.ds(pl.multiple_of(hd * HDIM, HDIM), HDIM), :],
            send_sem=w_sem.at[0, h, i - 1],
            recv_sem=w_sem.at[1, h, i - 1],
            device_id={"head": other},
        )

    def o_copies(h):
        return [
            pltpu.make_async_remote_copy(
                src_ref=src.at[h],
                dst_ref=dst.at[h],
                send_sem=sem.at[0, h],
                recv_sem=sem.at[1, h],
                device_id={"ctx": partner},
            )
            for src, dst, sem in ((s_send, s_recv, s_sem), (o_send, o_recv, o_sem))
        ]

    def g_copy(h, i):
        return pltpu.make_async_remote_copy(
            src_ref=gbuf.at[h, hd],
            dst_ref=gbuf.at[h, hd],
            send_sem=g_send.at[h, i - 1],
            recv_sem=g_recv.at[h, i - 1],
            device_id={"head": (hd + i) % n_head},
        )

    pl.semaphore_wait(barrier, 2 + n_head)
    for h in range(heads - 1):
        send_own(h)
    for h in range(heads):
        q_copy(h).start()
    total[...] = jnp.zeros_like(total)
    s_send[...] = jnp.zeros_like(s_send)

    def allowed_keys(source):
        low, high = bounds[0:1, :], bounds[1:2, :]
        index = column * nz + source
        position = lax.broadcasted_iota(jnp.int32, (half, 2 * rows), 0)
        parts = []
        for part in range(2):
            first = order[2 * index + part] * half
            parts.append(jnp.logical_and(position >= low - first, position < high - first))
        return parts

    def score(h, first, second):
        key = jnp.concatenate([kbuf[h, first], kbuf[h, second]], axis=0)
        query = jnp.concatenate([qbuf[0, h], qbuf[1, h]], axis=0)
        scores = dot_nt(key[:, :HDIM], query[:, HDIM:]) * scale
        tan_scores = dot_nt(key, query) * scale
        masks = allowed_keys(first) + allowed_keys(second)
        masked = jnp.concatenate(
            [
                jnp.where(mask, scores[i * half : (i + 1) * half], MASKED)
                for i, mask in enumerate(masks)
            ],
            axis=0,
        )
        peak = stats[h, 0:1, :]
        new_peak = jnp.maximum(peak, jnp.max(masked, axis=0, keepdims=True))
        weights = jnp.exp(masked - new_peak)
        rescale = jnp.exp(peak - new_peak)
        products = weights * tan_scores
        stats[h, 0:1, :] = new_peak
        stats[h, 1:2, :] = rescale * stats[h, 1:2, :] + jnp.sum(weights, axis=0, keepdims=True)
        stats[h, 2:3, :] = rescale * stats[h, 2:3, :] + jnp.sum(products, axis=0, keepdims=True)
        stats[h, 3:4, :] = rescale
        factors[0] = weights.astype(jnp.bfloat16)
        factors[1] = products.astype(jnp.bfloat16)

    def apply(h, first, second):
        value = jnp.concatenate([vbuf[h, first], vbuf[h, second]], axis=1)
        both = dot(value, factors[0])
        moved = dot(value[:HDIM], factors[1])
        rescale = stats[h, 3:4, :]
        acc[h, 0:HDIM, :] = rescale * acc[h, 0:HDIM, :] + both[:HDIM]
        acc[h, HDIM:, :] = rescale * acc[h, HDIM:, :] + both[HDIM:] + moved

    def finish(h):
        sums = stats[h, 1:2, :]
        inverse = jnp.where(sums > 0.0, 1.0 / jnp.where(sums > 0.0, sums, 1.0), 0.0)
        mean = stats[h, 2:3, :] * inverse
        primal = acc[h, 0:HDIM, :] * inverse
        tangent = acc[h, HDIM:, :] * inverse - mean * primal
        own_o[h, 0:HDIM, :] = primal[:, :rows]
        own_o[h, HDIM:, :] = tangent[:, :rows]
        o_send[h, 0:HDIM, :] = primal[:, rows:].astype(jnp.bfloat16)
        o_send[h, HDIM:, :] = tangent[:, rows:].astype(jnp.bfloat16)
        for i, row in enumerate((stats[h, 0:1, :], sums, mean)):
            own_stats[h, i : i + 1, :] = row[:, :rows]
            s_send[h, i : i + 1, :] = row[:, rows:]
        for copy in o_copies(h):
            copy.start()

    def merge(h):
        for copy in o_copies(h):
            copy.wait()
        peaks, sums, means = [], [], []
        for ref in (own_stats, s_recv):
            peaks.append(ref[h, 0:1, :])
            sums.append(ref[h, 1:2, :])
            means.append(ref[h, 2:3, :])
        peak = jnp.maximum(peaks[0], peaks[1])
        shares = [sums[i] * jnp.exp(peaks[i] - peak) for i in range(2)]
        inverse = 1.0 / (shares[0] + shares[1])
        shares = [share * inverse for share in shares]
        mean = shares[0] * means[0] + shares[1] * means[1]
        primals = [own_o[h, 0:HDIM, :], o_recv[h, 0:HDIM, :].astype(jnp.float32)]
        tangents = [own_o[h, HDIM:, :], o_recv[h, HDIM:, :].astype(jnp.float32)]
        primal = shares[0] * primals[0] + shares[1] * primals[1]
        tangent = sum(
            shares[i] * (tangents[i] + (means[i] - mean) * primals[i]) for i in range(2)
        )
        gbuf[h, hd, 0:rows, :] = primal.T.astype(jnp.bfloat16)
        gbuf[h, hd, rows:, :] = tangent.T.astype(jnp.bfloat16)
        for i in range(1, n_head):
            g_copy(h, i).start()

    def project(h):
        for i in range(1, n_head):
            w_copy(h, i).wait()
            g_copy(h, i).wait()
        features = jnp.concatenate([gbuf[h, g] for g in range(n_head)], axis=1)
        total[...] += dot(features, wbuf[h])

    first_part = (heads - 1) * depth
    steps = heads * depth

    def place(index):
        late = index // first_part
        h = (1 - late) * (index % (heads - 1)) + late * (heads - 1)
        d = (1 - late) * (index // (heads - 1)) + late * (index - first_part) + 1
        return h, d

    def forward(h, d, piece):
        for side in range(2):
            crosses = (piece < 2) == (side == 0)

            def take(side=side, crosses=crosses):
                arrived = ring_copy(h, d - 1, piece, side)
                arrived.wait_recv()

                @pl.when(d < depth if crosses else d < depth - 1)
                def _():
                    ring_copy(h, d, piece, side).start()

                arrived.wait_send()

            if crosses:
                take()
            else:
                pl.when(d < depth)(take)

    def step(index, carry):
        h, d = place(index)
        old_h, old_d = place(jnp.maximum(index - 1, 0))
        first, second = (z + nz - old_d) % nz, (z + old_d % depth) % nz
        live = index < steps

        @pl.when(live)
        def _():
            forward(h, d, 0)

        @pl.when(index > 0)
        def _():
            @pl.when(old_d == 1)
            def _():
                stats[old_h, 0:1, :] = jnp.full((1, 2 * rows), NONE_SEEN, jnp.float32)
                stats[old_h, 1:3, :] = jnp.zeros((2, 2 * rows), jnp.float32)
                acc[old_h] = jnp.zeros((2 * HDIM, 2 * rows), jnp.float32)
                q_copy(old_h).wait()

            score(old_h, first, second)

        @pl.when(live)
        def _():
            forward(h, d, 1)

        @pl.when(index > 0)
        def _():
            apply(old_h, first, second)

            @pl.when(old_d == depth)
            def _():
                finish(old_h)

        @pl.when(live)
        def _():
            for piece in range(2, PIECES):
                forward(h, d, piece)

        @pl.when(index < heads * (n_head - 1))
        def _():
            w_copy(index // (n_head - 1), index % (n_head - 1) + 1).start()

        @pl.when(jnp.logical_and(d == depth - 1, h == heads - 2))
        def _():
            send_own(heads - 1)

        @pl.when(jnp.logical_and(index > first_part, index < first_part + heads))
        def _():
            merge(index - first_part - 1)

        return carry

    lax.fori_loop(0, steps + 1, step, 0)
    own_w.wait()
    project(0)
    merge(heads - 1)
    for h in range(1, heads):
        project(h)
    out[...] = total[...].astype(out.dtype)


def local(
    queries,
    keys,
    values,
    tan_queries,
    tan_keys,
    tan_values,
    out_weight,
    clip_lengths,
    stretch_order,
):
    rows, width = queries.shape
    heads = width // HDIM
    n_head = lax.axis_size("head")
    nz = lax.axis_size("ctx") // 2
    depth = nz // 2
    ncol = out_weight.shape[1] // n_head
    bf16, f32 = jnp.bfloat16, jnp.float32
    weight = out_weight.reshape(heads, HDIM, out_weight.shape[1])
    dma = pltpu.SemaphoreType.DMA
    anywhere = pl.BlockSpec(memory_space=pl.ANY)
    in_smem = pl.BlockSpec(memory_space=pltpu.SMEM)
    in_vmem = pl.BlockSpec(memory_space=pltpu.VMEM)
    both = pl.pallas_call(
        functools.partial(kernel, nz, n_head),
        out_shape=jax.ShapeDtypeStruct((2 * rows, ncol), bf16),
        in_specs=[anywhere] * 7 + [in_smem] * 2,
        out_specs=in_vmem,
        scratch_shapes=[
            pltpu.VMEM((6, rows, width), bf16),
            pltpu.VMEM((2, heads, rows, 2 * HDIM), bf16),
            pltpu.VMEM((heads, nz, rows, 2 * HDIM), bf16),
            pltpu.VMEM((heads, nz, 2 * HDIM, rows), bf16),
            pltpu.VMEM((heads, n_head * HDIM, ncol), bf16),
            pltpu.VMEM((8, 2 * rows), jnp.int32),
            pltpu.VMEM((heads, 8, 2 * rows), f32),
            pltpu.VMEM((heads, 2 * HDIM, 2 * rows), f32),
            pltpu.VMEM((2, 2 * rows, 2 * rows), bf16),
            pltpu.VMEM((heads, 2 * HDIM, rows), f32),
            pltpu.VMEM((heads, 8, rows), f32),
            pltpu.VMEM((heads, 2 * HDIM, rows), bf16),
            pltpu.VMEM((heads, 8, rows), f32),
            pltpu.VMEM((heads, 2 * HDIM, rows), bf16),
            pltpu.VMEM((heads, 8, rows), f32),
            pltpu.VMEM((heads, n_head, 2 * rows, HDIM), bf16),
            pltpu.VMEM((2 * rows, ncol), f32),
            dma((6,)),
            dma((2, PIECES, 2 * heads)),
            dma((2, PIECES, heads * depth)),
            dma((2, heads)),
            dma((2, heads, n_head - 1)),
            dma,
            dma((2, heads)),
            dma((2, heads)),
            dma((heads, n_head - 1)),
            dma((heads, n_head - 1)),
        ],
        compiler_params=pltpu.CompilerParams(
            collective_id=0,
            has_side_effects=True,
            vmem_limit_bytes=60 * 1024 * 1024,
        ),
        cost_estimate=pl.CostEstimate(
            flops=2 * 6 * 2 * rows * nz * rows * width + 4 * rows * n_head * width * ncol,
            bytes_accessed=8 * 1024 * 1024,
            transcendentals=2 * rows * nz * rows * heads,
        ),
    )(
        queries,
        keys,
        values,
        tan_queries,
        tan_keys,
        tan_values,
        weight,
        clip_lengths,
        stretch_order,
    )
    return both[:rows], both[rows:]


def solution(mesh):
    placed = P(("dp", "ctx"), "head")
    return jax.shard_map(
        local,
        mesh=mesh,
        in_specs=(placed,) * 6 + (P("head", None), P("dp"), P("dp")),
        out_specs=(placed, placed),
        check_vma=False,
    )
```

```python
import functools

import jax
import jax.numpy as jnp
from jax import lax
from jax.experimental import pallas as pl
from jax.experimental.pallas import tpu as pltpu
from jax.sharding import PartitionSpec as P

HDIM = 128
PIECES = 4
NONE_SEEN = -1e29
MASKED = -1e30


def dot(a, b):
    return lax.dot_general(a, b, (((1,), (0,)), ((), ())), preferred_element_type=jnp.float32)


def dot_nt(a, b):
    return lax.dot_general(a, b, (((1,), (1,)), ((), ())), preferred_element_type=jnp.float32)


def kernel(
    nz,
    n_head,
    q_in,
    k_in,
    v_in,
    tq_in,
    tk_in,
    tv_in,
    w_in,
    lengths,
    order,
    out,
    stage,
    qbuf,
    kbuf,
    vbuf,
    wbuf,
    bounds,
    stats,
    acc,
    factors,
    own_o,
    own_stats,
    o_send,
    s_send,
    o_recv,
    s_recv,
    gbuf,
    total,
    stage_sem,
    ring_send,
    ring_recv,
    q_sem,
    w_sem,
    w_own_sem,
    o_sem,
    s_sem,
    g_send,
    g_recv,
):
    rows = q_in.shape[0]
    heads = q_in.shape[1] // HDIM
    half = rows // 2
    clips = lengths.shape[0]
    depth = nz // 2
    ncol = wbuf.shape[2]
    w_half = HDIM // 2
    scale = 1.0 / HDIM**0.5

    ctx = lax.axis_index("ctx")
    hd = lax.axis_index("head")
    core = lax.axis_index("dp")
    column = ctx // nz
    z = ctx % nz
    right = column * nz + (z + 1) % nz
    left = column * nz + (z + nz - 1) % nz
    partner = (ctx + nz) % (2 * nz)

    stages = [
        pltpu.make_async_copy(ref, stage.at[i], stage_sem.at[i])
        for i, ref in enumerate((k_in, tk_in, v_in, tv_in, q_in, tq_in))
    ]
    for copy in stages:
        copy.start()
    own_w = pltpu.make_async_copy(
        w_in.at[:, :, pl.ds(pl.multiple_of(hd * ncol, 128), ncol)],
        wbuf.at[:, pl.ds(pl.multiple_of(hd * HDIM, HDIM), HDIM), :],
        w_own_sem,
    )
    own_w.start()

    barrier = pltpu.get_barrier_semaphore()
    for other in (right, left, partner):
        pl.semaphore_signal(barrier, inc=1, device_id={"ctx": other})
    for i in range(1, n_head):
        pl.semaphore_signal(barrier, inc=1, device_id={"head": (hd + i) % n_head})
    pl.semaphore_signal(barrier, inc=1, device_id={"dp": 1 - core})

    ends = []
    running = jnp.int32(0)
    for c in range(clips):
        running = running + lengths[c]
        ends.append(running)
    lane = lax.broadcasted_iota(jnp.int32, (1, rows), 1)
    for slot, index in enumerate((ctx, partner)):
        anchor = jnp.where(
            lane < half,
            order[2 * index] * half + lane,
            order[2 * index + 1] * half + lane - half,
        )
        low = jnp.zeros_like(anchor)
        high = jnp.full_like(anchor, rows * nz * 2)
        for end in ends:
            low = jnp.where(end <= anchor, jnp.maximum(low, end), low)
            high = jnp.where(end > anchor, jnp.minimum(high, end), high)
        bounds[0:1, slot * rows : (slot + 1) * rows] = low
        bounds[1:2, slot * rows : (slot + 1) * rows] = high

    def ring_copy(h, hop, piece, side):
        source = (z + nz - hop) % nz if side == 0 else (z + hop) % nz
        step = h * depth + hop
        buf = kbuf if piece < 2 else vbuf
        size = buf.shape[2] // 2
        ref = buf.at[h, source, pl.ds((piece % 2) * size, size), :]
        return pltpu.make_async_remote_copy(
            src_ref=ref,
            dst_ref=ref,
            send_sem=ring_send.at[side, piece, h * 2 + hop % 2],
            recv_sem=ring_recv.at[side, piece, step],
            device_id={"ctx": right if side == 0 else left},
        )

    def send_own(h, pieces):
        for piece in pieces:
            for side in range(2):
                ring_copy(h, 0, piece, side).start()

    def q_copy(h):
        return pltpu.make_async_remote_copy(
            src_ref=qbuf.at[0, h],
            dst_ref=qbuf.at[1, h],
            send_sem=q_sem.at[0, h],
            recv_sem=q_sem.at[1, h],
            device_id={"ctx": partner},
        )

    def w_copy(i):
        other = (hd + i) % n_head
        return pltpu.make_async_remote_copy(
            src_ref=w_in.at[
                :,
                pl.ds(pl.multiple_of(core * w_half, w_half), w_half),
                pl.ds(pl.multiple_of(other * ncol, 128), ncol),
            ],
            dst_ref=wbuf.at[:, pl.ds(pl.multiple_of(hd * HDIM + core * w_half, w_half), w_half), :],
            send_sem=w_sem.at[0, i - 1],
            recv_sem=w_sem.at[1, i - 1],
            device_id={"head": other},
        )

    def w_share(i):
        source = (hd + n_head - i) % n_head
        ref = wbuf.at[:, pl.ds(pl.multiple_of(source * HDIM + core * w_half, w_half), w_half), :]
        return pltpu.make_async_remote_copy(
            src_ref=ref,
            dst_ref=ref,
            send_sem=w_sem.at[2, i - 1],
            recv_sem=w_sem.at[3, i - 1],
            device_id={"dp": 1 - core},
        )

    def o_copies(h):
        return [
            pltpu.make_async_remote_copy(
                src_ref=src.at[h],
                dst_ref=dst.at[h],
                send_sem=sem.at[0, h],
                recv_sem=sem.at[1, h],
                device_id={"ctx": partner},
            )
            for src, dst, sem in ((s_send, s_recv, s_sem), (o_send, o_recv, o_sem))
        ]

    def g_copy(h, i):
        return pltpu.make_async_remote_copy(
            src_ref=gbuf.at[h, hd],
            dst_ref=gbuf.at[h, hd],
            send_sem=g_send.at[h, i - 1],
            recv_sem=g_recv.at[h, i - 1],
            device_id={"head": (hd + i) % n_head},
        )

    columns = [slice(h * HDIM, (h + 1) * HDIM) for h in range(heads)]
    for copy in stages[:2]:
        copy.wait()
    for h, cols in enumerate(columns):
        kbuf[h, z, :, 0:HDIM] = stage[0, :, cols]
        kbuf[h, z, :, HDIM : 2 * HDIM] = stage[1, :, cols]
    pl.semaphore_wait(barrier, 3 + n_head)
    send_own(0, range(2))
    for copy in stages[2:4]:
        copy.wait()
    for h, cols in enumerate(columns):
        vbuf[h, z, 0:HDIM, :] = stage[2, :, cols].astype(jnp.float32).T.astype(jnp.bfloat16)
        vbuf[h, z, HDIM : 2 * HDIM, :] = stage[3, :, cols].astype(jnp.float32).T.astype(jnp.bfloat16)
    send_own(0, range(2, PIECES))
    for h in range(1, heads - 1):
        send_own(h, range(PIECES))
    for copy in stages[4:]:
        copy.wait()
    for h, cols in enumerate(columns):
        qbuf[0, h, :, HDIM : 2 * HDIM] = stage[4, :, cols]
        qbuf[0, h, :, 0:HDIM] = stage[5, :, cols]
        q_copy(h).start()
    for i in range(1, n_head):
        w_copy(i).start()
    total[...] = jnp.zeros_like(total)
    s_send[...] = jnp.zeros_like(s_send)

    def allowed_keys(source):
        low, high = bounds[0:1, :], bounds[1:2, :]
        index = column * nz + source
        position = lax.broadcasted_iota(jnp.int32, (half, 2 * rows), 0)
        parts = []
        for part in range(2):
            first = order[2 * index + part] * half
            parts.append(jnp.logical_and(position >= low - first, position < high - first))
        return parts

    def score(h, first, second):
        key = jnp.concatenate([kbuf[h, first], kbuf[h, second]], axis=0)
        query = jnp.concatenate([qbuf[0, h], qbuf[1, h]], axis=0)
        scores = dot_nt(key[:, :HDIM], query[:, HDIM:]) * scale
        tan_scores = dot_nt(key, query) * scale
        masks = allowed_keys(first) + allowed_keys(second)
        masked = jnp.concatenate(
            [
                jnp.where(mask, scores[i * half : (i + 1) * half], MASKED)
                for i, mask in enumerate(masks)
            ],
            axis=0,
        )
        peak = stats[h, 0:1, :]
        new_peak = jnp.maximum(peak, jnp.max(masked, axis=0, keepdims=True))
        weights = jnp.exp(masked - new_peak)
        rescale = jnp.exp(peak - new_peak)
        products = weights * tan_scores
        stats[h, 0:1, :] = new_peak
        stats[h, 1:2, :] = rescale * stats[h, 1:2, :] + jnp.sum(weights, axis=0, keepdims=True)
        stats[h, 2:3, :] = rescale * stats[h, 2:3, :] + jnp.sum(products, axis=0, keepdims=True)
        stats[h, 3:4, :] = rescale
        factors[0] = weights.astype(jnp.bfloat16)
        factors[1] = products.astype(jnp.bfloat16)

    def apply(h, first, second):
        value = jnp.concatenate([vbuf[h, first], vbuf[h, second]], axis=1)
        both = dot(value, factors[0])
        moved = dot(value[:HDIM], factors[1])
        rescale = stats[h, 3:4, :]
        acc[h, 0:HDIM, :] = rescale * acc[h, 0:HDIM, :] + both[:HDIM]
        acc[h, HDIM:, :] = rescale * acc[h, HDIM:, :] + both[HDIM:] + moved

    def finish(h):
        sums = stats[h, 1:2, :]
        inverse = jnp.where(sums > 0.0, 1.0 / jnp.where(sums > 0.0, sums, 1.0), 0.0)
        mean = stats[h, 2:3, :] * inverse
        primal = acc[h, 0:HDIM, :] * inverse
        tangent = acc[h, HDIM:, :] * inverse - mean * primal
        own_o[h, 0:HDIM, :] = primal[:, :rows]
        own_o[h, HDIM:, :] = tangent[:, :rows]
        o_send[h, 0:HDIM, :] = primal[:, rows:].astype(jnp.bfloat16)
        o_send[h, HDIM:, :] = tangent[:, rows:].astype(jnp.bfloat16)
        for i, row in enumerate((stats[h, 0:1, :], sums, mean)):
            own_stats[h, i : i + 1, :] = row[:, :rows]
            s_send[h, i : i + 1, :] = row[:, rows:]
        for copy in o_copies(h):
            copy.start()

    def merge(h):
        for copy in o_copies(h):
            copy.wait()
        peaks, sums, means = [], [], []
        for ref in (own_stats, s_recv):
            peaks.append(ref[h, 0:1, :])
            sums.append(ref[h, 1:2, :])
            means.append(ref[h, 2:3, :])
        peak = jnp.maximum(peaks[0], peaks[1])
        shares = [sums[i] * jnp.exp(peaks[i] - peak) for i in range(2)]
        inverse = 1.0 / (shares[0] + shares[1])
        shares = [share * inverse for share in shares]
        mean = shares[0] * means[0] + shares[1] * means[1]
        primals = [own_o[h, 0:HDIM, :], o_recv[h, 0:HDIM, :].astype(jnp.float32)]
        tangents = [own_o[h, HDIM:, :], o_recv[h, HDIM:, :].astype(jnp.float32)]
        primal = shares[0] * primals[0] + shares[1] * primals[1]
        tangent = sum(
            shares[i] * (tangents[i] + (means[i] - mean) * primals[i]) for i in range(2)
        )
        gbuf[h, hd, 0:rows, :] = primal.T.astype(jnp.bfloat16)
        gbuf[h, hd, rows:, :] = tangent.T.astype(jnp.bfloat16)
        for i in range(1, n_head):
            g_copy(h, i).start()

    def project(h):
        for i in range(1, n_head):
            g_copy(h, i).wait()
        features = jnp.concatenate([gbuf[h, g] for g in range(n_head)], axis=1)
        total[...] += dot(features, wbuf[h])

    first_part = (heads - 1) * depth
    steps = heads * depth

    def place(index):
        late = index // first_part
        h = (1 - late) * (index % (heads - 1)) + late * (heads - 1)
        d = (1 - late) * (index // (heads - 1)) + late * (index - first_part) + 1
        return h, d

    def forward(h, d, piece):
        for side in range(2):
            crosses = (piece < 2) == (side == 0)

            def take(side=side, crosses=crosses):
                arrived = ring_copy(h, d - 1, piece, side)
                arrived.wait_recv()

                @pl.when(d < depth if crosses else d < depth - 1)
                def _():
                    ring_copy(h, d, piece, side).start()

                arrived.wait_send()

            if crosses:
                take()
            else:
                pl.when(d < depth)(take)

    def step(index, carry):
        h, d = place(index)
        old_h, old_d = place(jnp.maximum(index - 1, 0))
        first, second = (z + nz - old_d) % nz, (z + old_d % depth) % nz
        live = index < steps

        @pl.when(live)
        def _():
            forward(h, d, 0)

        @pl.when(index > 0)
        def _():
            @pl.when(old_d == 1)
            def _():
                stats[old_h, 0:1, :] = jnp.full((1, 2 * rows), NONE_SEEN, jnp.float32)
                stats[old_h, 1:3, :] = jnp.zeros((2, 2 * rows), jnp.float32)
                acc[old_h] = jnp.zeros((2 * HDIM, 2 * rows), jnp.float32)
                q_copy(old_h).wait()

            score(old_h, first, second)

        @pl.when(live)
        def _():
            forward(h, d, 1)

        @pl.when(index > 0)
        def _():
            apply(old_h, first, second)

            @pl.when(old_d == depth)
            def _():
                finish(old_h)

        @pl.when(live)
        def _():
            for piece in range(2, PIECES):
                forward(h, d, piece)

        @pl.when(index == first_part)
        def _():
            for i in range(1, n_head):
                w_copy(i).wait()
                w_share(i).start()

        @pl.when(jnp.logical_and(d == depth - 1, h == heads - 2))
        def _():
            send_own(heads - 1, range(PIECES))

        @pl.when(jnp.logical_and(index > first_part, index < first_part + heads))
        def _():
            merge(index - first_part - 1)

        return carry

    lax.fori_loop(0, steps + 1, step, 0)
    own_w.wait()
    for i in range(1, n_head):
        w_share(i).wait()
    project(0)
    merge(heads - 1)
    for h in range(1, heads):
        project(h)
    out[...] = total[...].astype(out.dtype)


def local(
    queries,
    keys,
    values,
    tan_queries,
    tan_keys,
    tan_values,
    out_weight,
    clip_lengths,
    stretch_order,
):
    rows, width = queries.shape
    heads = width // HDIM
    n_head = lax.axis_size("head")
    nz = lax.axis_size("ctx") // 2
    depth = nz // 2
    ncol = out_weight.shape[1] // n_head
    bf16, f32 = jnp.bfloat16, jnp.float32
    weight = out_weight.reshape(heads, HDIM, out_weight.shape[1])
    dma = pltpu.SemaphoreType.DMA
    anywhere = pl.BlockSpec(memory_space=pl.ANY)
    in_smem = pl.BlockSpec(memory_space=pltpu.SMEM)
    in_vmem = pl.BlockSpec(memory_space=pltpu.VMEM)
    both = pl.pallas_call(
        functools.partial(kernel, nz, n_head),
        out_shape=jax.ShapeDtypeStruct((2 * rows, ncol), bf16),
        in_specs=[anywhere] * 7 + [in_smem] * 2,
        out_specs=in_vmem,
        scratch_shapes=[
            pltpu.VMEM((6, rows, width), bf16),
            pltpu.VMEM((2, heads, rows, 2 * HDIM), bf16),
            pltpu.VMEM((heads, nz, rows, 2 * HDIM), bf16),
            pltpu.VMEM((heads, nz, 2 * HDIM, rows), bf16),
            pltpu.VMEM((heads, n_head * HDIM, ncol), bf16),
            pltpu.VMEM((8, 2 * rows), jnp.int32),
            pltpu.VMEM((heads, 8, 2 * rows), f32),
            pltpu.VMEM((heads, 2 * HDIM, 2 * rows), f32),
            pltpu.VMEM((2, 2 * rows, 2 * rows), bf16),
            pltpu.VMEM((heads, 2 * HDIM, rows), f32),
            pltpu.VMEM((heads, 8, rows), f32),
            pltpu.VMEM((heads, 2 * HDIM, rows), bf16),
            pltpu.VMEM((heads, 8, rows), f32),
            pltpu.VMEM((heads, 2 * HDIM, rows), bf16),
            pltpu.VMEM((heads, 8, rows), f32),
            pltpu.VMEM((heads, n_head, 2 * rows, HDIM), bf16),
            pltpu.VMEM((2 * rows, ncol), f32),
            dma((6,)),
            dma((2, PIECES, 2 * heads)),
            dma((2, PIECES, heads * depth)),
            dma((2, heads)),
            dma((4, n_head - 1)),
            dma,
            dma((2, heads)),
            dma((2, heads)),
            dma((heads, n_head - 1)),
            dma((heads, n_head - 1)),
        ],
        compiler_params=pltpu.CompilerParams(
            collective_id=0,
            has_side_effects=True,
            vmem_limit_bytes=60 * 1024 * 1024,
        ),
        cost_estimate=pl.CostEstimate(
            flops=2 * 6 * 2 * rows * nz * rows * width + 4 * rows * n_head * width * ncol,
            bytes_accessed=8 * 1024 * 1024,
            transcendentals=2 * rows * nz * rows * heads,
        ),
    )(
        queries,
        keys,
        values,
        tan_queries,
        tan_keys,
        tan_values,
        weight,
        clip_lengths,
        stretch_order,
    )
    return both[:rows], both[rows:]


def solution(mesh):
    placed = P(("dp", "ctx"), "head")
    return jax.shard_map(
        local,
        mesh=mesh,
        in_specs=(placed,) * 6 + (P("head", None), P("dp"), P("dp")),
        out_specs=(placed, placed),
        check_vma=False,
    )
```

```python
import functools

import jax
import jax.numpy as jnp
from jax import lax
from jax.experimental import pallas as pl
from jax.experimental.pallas import tpu as pltpu
from jax.sharding import PartitionSpec as P

HDIM = 128
PIECES = 4
NONE_SEEN = -1e29
MASKED = -1e30


def dot(a, b):
    return lax.dot_general(a, b, (((1,), (0,)), ((), ())), preferred_element_type=jnp.float32)


def dot_nt(a, b):
    return lax.dot_general(a, b, (((1,), (1,)), ((), ())), preferred_element_type=jnp.float32)


def kernel(
    nz,
    n_head,
    q_in,
    k_in,
    v_in,
    tq_in,
    tk_in,
    tv_in,
    w_in,
    lengths_in,
    order_in,
    out,
    lengths,
    order,
    stage,
    qbuf,
    kbuf,
    vbuf,
    wbuf,
    bounds,
    stats,
    acc,
    factors,
    own_o,
    own_stats,
    o_send,
    s_send,
    o_recv,
    s_recv,
    gbuf,
    total,
    stage_sem,
    ring_send,
    ring_recv,
    q_sem,
    w_sem,
    w_own_sem,
    o_sem,
    s_sem,
    g_send,
    g_recv,
):
    rows = q_in.shape[0]
    heads = q_in.shape[1] // HDIM
    half = rows // 2
    clips = lengths.shape[0]
    depth = nz // 2
    ncol = wbuf.shape[2]
    w_half = HDIM // 2
    scale = 1.0 / HDIM**0.5

    ctx = lax.axis_index("ctx")
    hd = lax.axis_index("head")
    core = lax.axis_index("dp")
    column = ctx // nz
    z = ctx % nz
    right = column * nz + (z + 1) % nz
    left = column * nz + (z + nz - 1) % nz
    partner = (ctx + nz) % (2 * nz)

    stages = [
        pltpu.make_async_copy(ref, stage.at[i], stage_sem.at[i])
        for i, ref in enumerate((k_in, tk_in, v_in, tv_in, q_in, tq_in))
    ]
    tables = [
        pltpu.make_async_copy(src, dst, stage_sem.at[6 + i])
        for i, (src, dst) in enumerate(((lengths_in, lengths), (order_in, order)))
    ]
    for copy in stages + tables:
        copy.start()
    own_w = pltpu.make_async_copy(
        w_in.at[:, :, pl.ds(pl.multiple_of(hd * ncol, 128), ncol)],
        wbuf.at[:, pl.ds(pl.multiple_of(hd * HDIM, HDIM), HDIM), :],
        w_own_sem,
    )
    own_w.start()

    barrier = pltpu.get_barrier_semaphore()
    for other in (right, left, partner):
        pl.semaphore_signal(barrier, inc=1, device_id={"ctx": other})
    for i in range(1, n_head):
        pl.semaphore_signal(barrier, inc=1, device_id={"head": (hd + i) % n_head})
    pl.semaphore_signal(barrier, inc=1, device_id={"dp": 1 - core})

    for copy in tables:
        copy.wait()
    ends = []
    running = jnp.int32(0)
    for c in range(clips):
        running = running + lengths[c]
        ends.append(running)
    lane = lax.broadcasted_iota(jnp.int32, (1, rows), 1)
    for slot, index in enumerate((ctx, partner)):
        anchor = jnp.where(
            lane < half,
            order[2 * index] * half + lane,
            order[2 * index + 1] * half + lane - half,
        )
        low = jnp.zeros_like(anchor)
        high = jnp.full_like(anchor, rows * nz * 2)
        for end in ends:
            low = jnp.where(end <= anchor, jnp.maximum(low, end), low)
            high = jnp.where(end > anchor, jnp.minimum(high, end), high)
        bounds[0:1, slot * rows : (slot + 1) * rows] = low
        bounds[1:2, slot * rows : (slot + 1) * rows] = high

    def ring_copy(h, hop, piece, side):
        source = (z + nz - hop) % nz if side == 0 else (z + hop) % nz
        step = h * depth + hop
        buf = kbuf if piece < 2 else vbuf
        size = buf.shape[2] // 2
        ref = buf.at[h, source, pl.ds((piece % 2) * size, size), :]
        return pltpu.make_async_remote_copy(
            src_ref=ref,
            dst_ref=ref,
            send_sem=ring_send.at[side, piece, h * 2 + hop % 2],
            recv_sem=ring_recv.at[side, piece, step],
            device_id={"ctx": right if side == 0 else left},
        )

    def send_own(h, pieces):
        for piece in pieces:
            for side in range(2):
                ring_copy(h, 0, piece, side).start()

    def q_copy(h):
        return pltpu.make_async_remote_copy(
            src_ref=qbuf.at[0, h],
            dst_ref=qbuf.at[1, h],
            send_sem=q_sem.at[0, h],
            recv_sem=q_sem.at[1, h],
            device_id={"ctx": partner},
        )

    def w_copy(i):
        other = (hd + i) % n_head
        return pltpu.make_async_remote_copy(
            src_ref=w_in.at[
                :,
                pl.ds(pl.multiple_of(core * w_half, w_half), w_half),
                pl.ds(pl.multiple_of(other * ncol, 128), ncol),
            ],
            dst_ref=wbuf.at[:, pl.ds(pl.multiple_of(hd * HDIM + core * w_half, w_half), w_half), :],
            send_sem=w_sem.at[0, i - 1],
            recv_sem=w_sem.at[1, i - 1],
            device_id={"head": other},
        )

    def w_share(i):
        source = (hd + n_head - i) % n_head
        ref = wbuf.at[:, pl.ds(pl.multiple_of(source * HDIM + core * w_half, w_half), w_half), :]
        return pltpu.make_async_remote_copy(
            src_ref=ref,
            dst_ref=ref,
            send_sem=w_sem.at[2, i - 1],
            recv_sem=w_sem.at[3, i - 1],
            device_id={"dp": 1 - core},
        )

    def o_copies(h):
        return [
            pltpu.make_async_remote_copy(
                src_ref=src.at[h],
                dst_ref=dst.at[h],
                send_sem=sem.at[0, h],
                recv_sem=sem.at[1, h],
                device_id={"ctx": partner},
            )
            for src, dst, sem in ((s_send, s_recv, s_sem), (o_send, o_recv, o_sem))
        ]

    def g_copy(h, i):
        return pltpu.make_async_remote_copy(
            src_ref=gbuf.at[h, hd],
            dst_ref=gbuf.at[h, hd],
            send_sem=g_send.at[h, i - 1],
            recv_sem=g_recv.at[h, i - 1],
            device_id={"head": (hd + i) % n_head},
        )

    columns = [slice(h * HDIM, (h + 1) * HDIM) for h in range(heads)]
    for copy in stages[:2]:
        copy.wait()
    for h, cols in enumerate(columns):
        kbuf[h, z, :, 0:HDIM] = stage[0, :, cols]
        kbuf[h, z, :, HDIM : 2 * HDIM] = stage[1, :, cols]
    pl.semaphore_wait(barrier, 3 + n_head)
    send_own(0, range(2))
    for copy in stages[2:4]:
        copy.wait()
    for h, cols in enumerate(columns):
        vbuf[h, z, 0:HDIM, :] = stage[2, :, cols].astype(jnp.float32).T.astype(jnp.bfloat16)
        vbuf[h, z, HDIM : 2 * HDIM, :] = stage[3, :, cols].astype(jnp.float32).T.astype(jnp.bfloat16)
    send_own(0, range(2, PIECES))
    for h in range(1, heads - 1):
        send_own(h, range(PIECES))
    for copy in stages[4:]:
        copy.wait()
    for h, cols in enumerate(columns):
        qbuf[0, h, :, HDIM : 2 * HDIM] = stage[4, :, cols]
        qbuf[0, h, :, 0:HDIM] = stage[5, :, cols]
        q_copy(h).start()
    for i in range(1, n_head):
        w_copy(i).start()
    total[...] = jnp.zeros_like(total)
    s_send[...] = jnp.zeros_like(s_send)

    def allowed_keys(source):
        low, high = bounds[0:1, :], bounds[1:2, :]
        index = column * nz + source
        position = lax.broadcasted_iota(jnp.int32, (half, 2 * rows), 0)
        parts = []
        for part in range(2):
            first = order[2 * index + part] * half
            parts.append(jnp.logical_and(position >= low - first, position < high - first))
        return parts

    def score(h, first, second):
        key = jnp.concatenate([kbuf[h, first], kbuf[h, second]], axis=0)
        query = jnp.concatenate([qbuf[0, h], qbuf[1, h]], axis=0)
        scores = dot_nt(key[:, :HDIM], query[:, HDIM:]) * scale
        tan_scores = dot_nt(key, query) * scale
        masks = allowed_keys(first) + allowed_keys(second)
        masked = jnp.concatenate(
            [
                jnp.where(mask, scores[i * half : (i + 1) * half], MASKED)
                for i, mask in enumerate(masks)
            ],
            axis=0,
        )
        peak = stats[h, 0:1, :]
        new_peak = jnp.maximum(peak, jnp.max(masked, axis=0, keepdims=True))
        weights = jnp.exp(masked - new_peak)
        rescale = jnp.exp(peak - new_peak)
        products = weights * tan_scores
        stats[h, 0:1, :] = new_peak
        stats[h, 1:2, :] = rescale * stats[h, 1:2, :] + jnp.sum(weights, axis=0, keepdims=True)
        stats[h, 2:3, :] = rescale * stats[h, 2:3, :] + jnp.sum(products, axis=0, keepdims=True)
        stats[h, 3:4, :] = rescale
        factors[0] = weights.astype(jnp.bfloat16)
        factors[1] = products.astype(jnp.bfloat16)

    def apply(h, first, second):
        value = jnp.concatenate([vbuf[h, first], vbuf[h, second]], axis=1)
        both = dot(value, factors[0])
        moved = dot(value[:HDIM], factors[1])
        rescale = stats[h, 3:4, :]
        acc[h, 0:HDIM, :] = rescale * acc[h, 0:HDIM, :] + both[:HDIM]
        acc[h, HDIM:, :] = rescale * acc[h, HDIM:, :] + both[HDIM:] + moved

    def finish(h):
        sums = stats[h, 1:2, :]
        inverse = jnp.where(sums > 0.0, 1.0 / jnp.where(sums > 0.0, sums, 1.0), 0.0)
        mean = stats[h, 2:3, :] * inverse
        primal = acc[h, 0:HDIM, :] * inverse
        tangent = acc[h, HDIM:, :] * inverse - mean * primal
        own_o[h, 0:HDIM, :] = primal[:, :rows]
        own_o[h, HDIM:, :] = tangent[:, :rows]
        o_send[h, 0:HDIM, :] = primal[:, rows:].astype(jnp.bfloat16)
        o_send[h, HDIM:, :] = tangent[:, rows:].astype(jnp.bfloat16)
        for i, row in enumerate((stats[h, 0:1, :], sums, mean)):
            own_stats[h, i : i + 1, :] = row[:, :rows]
            s_send[h, i : i + 1, :] = row[:, rows:]
        for copy in o_copies(h):
            copy.start()

    def merge(h):
        for copy in o_copies(h):
            copy.wait()
        peaks, sums, means = [], [], []
        for ref in (own_stats, s_recv):
            peaks.append(ref[h, 0:1, :])
            sums.append(ref[h, 1:2, :])
            means.append(ref[h, 2:3, :])
        peak = jnp.maximum(peaks[0], peaks[1])
        shares = [sums[i] * jnp.exp(peaks[i] - peak) for i in range(2)]
        inverse = 1.0 / (shares[0] + shares[1])
        shares = [share * inverse for share in shares]
        mean = shares[0] * means[0] + shares[1] * means[1]
        primals = [own_o[h, 0:HDIM, :], o_recv[h, 0:HDIM, :].astype(jnp.float32)]
        tangents = [own_o[h, HDIM:, :], o_recv[h, HDIM:, :].astype(jnp.float32)]
        primal = shares[0] * primals[0] + shares[1] * primals[1]
        tangent = sum(
            shares[i] * (tangents[i] + (means[i] - mean) * primals[i]) for i in range(2)
        )
        gbuf[h, hd, 0:rows, :] = primal.T.astype(jnp.bfloat16)
        gbuf[h, hd, rows:, :] = tangent.T.astype(jnp.bfloat16)
        for i in range(1, n_head):
            g_copy(h, i).start()

    def project(h):
        for i in range(1, n_head):
            g_copy(h, i).wait()
        features = jnp.concatenate([gbuf[h, g] for g in range(n_head)], axis=1)
        total[...] += dot(features, wbuf[h])

    mid = 3 * depth // 2
    late = mid + depth
    steps = heads * depth

    def place(index):
        group, turn = index // 3, index % 3
        slow = turn % 2
        h_a = slow
        d_a = (1 - slow) * (2 * group + turn // 2 + 1) + slow * (group + 1)
        pair, new = (index - mid) // 2, (index - mid) % 2
        h_b = 1 + new
        d_b = pair + 1 + (1 - new) * (depth // 2)
        d_c = depth // 2 + index - late + 1
        past_mid = jnp.minimum(index // mid, 1)
        past_late = jnp.minimum(index // late, 1)
        h = (1 - past_mid) * h_a + (past_mid - past_late) * h_b + past_late * 2
        d = (1 - past_mid) * d_a + (past_mid - past_late) * d_b + past_late * d_c
        return h, d

    def forward(h, d, piece):
        for side in range(2):
            crosses = (piece < 2) == (side == 0)

            def take(side=side, crosses=crosses):
                arrived = ring_copy(h, d - 1, piece, side)
                arrived.wait_recv()

                @pl.when(d < depth if crosses else d < depth - 1)
                def _():
                    ring_copy(h, d, piece, side).start()

                arrived.wait_send()

            if crosses:
                take()
            else:
                pl.when(d < depth)(take)

    def step(index, carry):
        h, d = place(index)
        old_h, old_d = place(jnp.maximum(index - 1, 0))
        first, second = (z + nz - old_d) % nz, (z + old_d % depth) % nz
        live = index < steps

        @pl.when(live)
        def _():
            forward(h, d, 0)

        @pl.when(index > 0)
        def _():
            @pl.when(old_d == 1)
            def _():
                stats[old_h, 0:1, :] = jnp.full((1, 2 * rows), NONE_SEEN, jnp.float32)
                stats[old_h, 1:3, :] = jnp.zeros((2, 2 * rows), jnp.float32)
                acc[old_h] = jnp.zeros((2 * HDIM, 2 * rows), jnp.float32)
                q_copy(old_h).wait()

            score(old_h, first, second)

        @pl.when(live)
        def _():
            forward(h, d, 1)

        @pl.when(index > 0)
        def _():
            apply(old_h, first, second)

            @pl.when(old_d == depth)
            def _():
                finish(old_h)

        @pl.when(live)
        def _():
            for piece in range(2, PIECES):
                forward(h, d, piece)

        @pl.when(index == late - 2)
        def _():
            for i in range(1, n_head):
                w_copy(i).wait()
                w_share(i).start()

        @pl.when(jnp.logical_and(d == depth - 1, h == 0))
        def _():
            send_own(heads - 1, range(PIECES))

        for early, when in ((0, mid + 2), (1, late + 1)):

            @pl.when(index == when)
            def _(early=early):
                merge(early)

        return carry

    lax.fori_loop(0, steps + 1, step, 0)
    own_w.wait()
    for i in range(1, n_head):
        w_share(i).wait()
    project(0)
    merge(heads - 1)
    for h in range(1, heads):
        project(h)
    out[...] = total[...].astype(out.dtype)


def local(
    queries,
    keys,
    values,
    tan_queries,
    tan_keys,
    tan_values,
    out_weight,
    clip_lengths,
    stretch_order,
):
    rows, width = queries.shape
    heads = width // HDIM
    n_head = lax.axis_size("head")
    nz = lax.axis_size("ctx") // 2
    depth = nz // 2
    ncol = out_weight.shape[1] // n_head
    bf16, f32 = jnp.bfloat16, jnp.float32
    weight = out_weight.reshape(heads, HDIM, out_weight.shape[1])
    dma = pltpu.SemaphoreType.DMA
    anywhere = pl.BlockSpec(memory_space=pl.ANY)
    in_vmem = pl.BlockSpec(memory_space=pltpu.VMEM)
    both = pl.pallas_call(
        functools.partial(kernel, nz, n_head),
        out_shape=jax.ShapeDtypeStruct((2 * rows, ncol), bf16),
        in_specs=[anywhere] * 9,
        out_specs=in_vmem,
        scratch_shapes=[
            pltpu.SMEM(clip_lengths.shape, jnp.int32),
            pltpu.SMEM(stretch_order.shape, jnp.int32),
            pltpu.VMEM((6, rows, width), bf16),
            pltpu.VMEM((2, heads, rows, 2 * HDIM), bf16),
            pltpu.VMEM((heads, nz, rows, 2 * HDIM), bf16),
            pltpu.VMEM((heads, nz, 2 * HDIM, rows), bf16),
            pltpu.VMEM((heads, n_head * HDIM, ncol), bf16),
            pltpu.VMEM((8, 2 * rows), jnp.int32),
            pltpu.VMEM((heads, 8, 2 * rows), f32),
            pltpu.VMEM((heads, 2 * HDIM, 2 * rows), f32),
            pltpu.VMEM((2, 2 * rows, 2 * rows), bf16),
            pltpu.VMEM((heads, 2 * HDIM, rows), f32),
            pltpu.VMEM((heads, 8, rows), f32),
            pltpu.VMEM((heads, 2 * HDIM, rows), bf16),
            pltpu.VMEM((heads, 8, rows), f32),
            pltpu.VMEM((heads, 2 * HDIM, rows), bf16),
            pltpu.VMEM((heads, 8, rows), f32),
            pltpu.VMEM((heads, n_head, 2 * rows, HDIM), bf16),
            pltpu.VMEM((2 * rows, ncol), f32),
            dma((8,)),
            dma((2, PIECES, 2 * heads)),
            dma((2, PIECES, heads * depth)),
            dma((2, heads)),
            dma((4, n_head - 1)),
            dma,
            dma((2, heads)),
            dma((2, heads)),
            dma((heads, n_head - 1)),
            dma((heads, n_head - 1)),
        ],
        compiler_params=pltpu.CompilerParams(
            collective_id=0,
            has_side_effects=True,
            vmem_limit_bytes=60 * 1024 * 1024,
        ),
        cost_estimate=pl.CostEstimate(
            flops=2 * 6 * 2 * rows * nz * rows * width + 4 * rows * n_head * width * ncol,
            bytes_accessed=8 * 1024 * 1024,
            transcendentals=2 * rows * nz * rows * heads,
        ),
    )(
        queries,
        keys,
        values,
        tan_queries,
        tan_keys,
        tan_values,
        weight,
        clip_lengths,
        stretch_order,
    )
    return both[:rows], both[rows:]


def solution(mesh):
    placed = P(("dp", "ctx"), "head")
    return jax.shard_map(
        local,
        mesh=mesh,
        in_specs=(placed,) * 6 + (P("head", None), P("dp"), P("dp")),
        out_specs=(placed, placed),
        check_vma=False,
    )
```

```python
import functools

import jax
import jax.numpy as jnp
from jax import lax
from jax.experimental import pallas as pl
from jax.experimental.pallas import tpu as pltpu
from jax.sharding import PartitionSpec as P

HDIM = 128
PIECES = 2
NONE_SEEN = -1e29
MASKED = -1e30


def dot(a, b):
    return lax.dot_general(a, b, (((1,), (0,)), ((), ())), preferred_element_type=jnp.float32)


def dot_nt(a, b):
    return lax.dot_general(a, b, (((1,), (1,)), ((), ())), preferred_element_type=jnp.float32)


def kernel(
    nz,
    n_head,
    q_in,
    k_in,
    v_in,
    tq_in,
    tk_in,
    tv_in,
    w_in,
    lengths_in,
    order_in,
    out,
    lengths,
    order,
    stage,
    qbuf,
    kbuf,
    vbuf,
    wbuf,
    bounds,
    stats,
    acc,
    factors,
    own_o,
    own_stats,
    o_send,
    s_send,
    o_recv,
    s_recv,
    gbuf,
    total,
    stage_sem,
    ring_send,
    ring_recv,
    q_sem,
    w_sem,
    w_own_sem,
    o_sem,
    s_sem,
    g_send,
    g_recv,
):
    rows = q_in.shape[0]
    heads = q_in.shape[1] // HDIM
    half = rows // 2
    clips = lengths.shape[0]
    depth = nz // 2
    ncol = wbuf.shape[2]
    w_half = HDIM // 2
    scale = 1.0 / HDIM**0.5

    ctx = lax.axis_index("ctx")
    hd = lax.axis_index("head")
    core = lax.axis_index("dp")
    column = ctx // nz
    z = ctx % nz
    right = column * nz + (z + 1) % nz
    left = column * nz + (z + nz - 1) % nz
    partner = (ctx + nz) % (2 * nz)

    stages = [
        pltpu.make_async_copy(ref, stage.at[i], stage_sem.at[i])
        for i, ref in enumerate((k_in, tk_in, v_in, tv_in, q_in, tq_in))
    ]
    tables = [
        pltpu.make_async_copy(src, dst, stage_sem.at[6 + i])
        for i, (src, dst) in enumerate(((lengths_in, lengths), (order_in, order)))
    ]
    for copy in stages + tables:
        copy.start()
    own_w = pltpu.make_async_copy(
        w_in.at[:, :, pl.ds(pl.multiple_of(hd * ncol, 128), ncol)],
        wbuf.at[:, pl.ds(pl.multiple_of(hd * HDIM, HDIM), HDIM), :],
        w_own_sem,
    )
    own_w.start()

    barrier = pltpu.get_barrier_semaphore()
    for other in (right, left, partner):
        pl.semaphore_signal(barrier, inc=1, device_id={"ctx": other})
    for i in range(1, n_head):
        pl.semaphore_signal(barrier, inc=1, device_id={"head": (hd + i) % n_head})
    pl.semaphore_signal(barrier, inc=1, device_id={"dp": 1 - core})

    for copy in tables:
        copy.wait()
    ends = []
    running = jnp.int32(0)
    for c in range(clips):
        running = running + lengths[c]
        ends.append(running)
    lane = lax.broadcasted_iota(jnp.int32, (1, rows), 1)
    for slot, index in enumerate((ctx, partner)):
        anchor = jnp.where(
            lane < half,
            order[2 * index] * half + lane,
            order[2 * index + 1] * half + lane - half,
        )
        low = jnp.zeros_like(anchor)
        high = jnp.full_like(anchor, rows * nz * 2)
        for end in ends:
            low = jnp.where(end <= anchor, jnp.maximum(low, end), low)
            high = jnp.where(end > anchor, jnp.minimum(high, end), high)
        bounds[0:1, slot * rows : (slot + 1) * rows] = low
        bounds[1:2, slot * rows : (slot + 1) * rows] = high

    def ring_copy(h, hop, piece, side):
        source = (z + nz - hop) % nz if side == 0 else (z + hop) % nz
        step = h * depth + hop
        ref = (kbuf, vbuf)[piece].at[h, source]
        return pltpu.make_async_remote_copy(
            src_ref=ref,
            dst_ref=ref,
            send_sem=ring_send.at[side, piece, h * 2 + hop % 2],
            recv_sem=ring_recv.at[side, piece, step],
            device_id={"ctx": right if side == 0 else left},
        )

    def send_own(h, pieces):
        for piece in pieces:
            for side in range(2):
                ring_copy(h, 0, piece, side).start()

    def q_copy(h):
        return pltpu.make_async_remote_copy(
            src_ref=qbuf.at[0, h],
            dst_ref=qbuf.at[1, h],
            send_sem=q_sem.at[0, h],
            recv_sem=q_sem.at[1, h],
            device_id={"ctx": partner},
        )

    def w_copy(i):
        other = (hd + i) % n_head
        return pltpu.make_async_remote_copy(
            src_ref=w_in.at[
                :,
                pl.ds(pl.multiple_of(core * w_half, w_half), w_half),
                pl.ds(pl.multiple_of(other * ncol, 128), ncol),
            ],
            dst_ref=wbuf.at[:, pl.ds(pl.multiple_of(hd * HDIM + core * w_half, w_half), w_half), :],
            send_sem=w_sem.at[0, i - 1],
            recv_sem=w_sem.at[1, i - 1],
            device_id={"head": other},
        )

    def w_share(i):
        source = (hd + n_head - i) % n_head
        ref = wbuf.at[:, pl.ds(pl.multiple_of(source * HDIM + core * w_half, w_half), w_half), :]
        return pltpu.make_async_remote_copy(
            src_ref=ref,
            dst_ref=ref,
            send_sem=w_sem.at[2, i - 1],
            recv_sem=w_sem.at[3, i - 1],
            device_id={"dp": 1 - core},
        )

    def o_copies(h):
        return [
            pltpu.make_async_remote_copy(
                src_ref=src.at[h],
                dst_ref=dst.at[h],
                send_sem=sem.at[0, h],
                recv_sem=sem.at[1, h],
                device_id={"ctx": partner},
            )
            for src, dst, sem in ((s_send, s_recv, s_sem), (o_send, o_recv, o_sem))
        ]

    def g_copy(h, i):
        return pltpu.make_async_remote_copy(
            src_ref=gbuf.at[h, hd],
            dst_ref=gbuf.at[h, hd],
            send_sem=g_send.at[h, i - 1],
            recv_sem=g_recv.at[h, i - 1],
            device_id={"head": (hd + i) % n_head},
        )

    columns = [slice(h * HDIM, (h + 1) * HDIM) for h in range(heads)]
    for copy in stages[:2]:
        copy.wait()
    for h, cols in enumerate(columns):
        kbuf[h, z, :, 0:HDIM] = stage[0, :, cols]
        kbuf[h, z, :, HDIM : 2 * HDIM] = stage[1, :, cols]
    pl.semaphore_wait(barrier, 3 + n_head)
    send_own(0, [0])
    for copy in stages[2:4]:
        copy.wait()
    for h, cols in enumerate(columns):
        vbuf[h, z, 0:HDIM, :] = stage[2, :, cols].astype(jnp.float32).T.astype(jnp.bfloat16)
        vbuf[h, z, HDIM : 2 * HDIM, :] = stage[3, :, cols].astype(jnp.float32).T.astype(jnp.bfloat16)
    send_own(0, [1])
    for h in range(1, heads - 1):
        send_own(h, range(PIECES))
    for copy in stages[4:]:
        copy.wait()
    for h, cols in enumerate(columns):
        qbuf[0, h, :, HDIM : 2 * HDIM] = stage[4, :, cols]
        qbuf[0, h, :, 0:HDIM] = stage[5, :, cols]
        q_copy(h).start()
    for i in range(1, n_head):
        w_copy(i).start()
    total[...] = jnp.zeros_like(total)
    s_send[...] = jnp.zeros_like(s_send)

    def allowed_keys(source):
        low, high = bounds[0:1, :], bounds[1:2, :]
        index = column * nz + source
        position = lax.broadcasted_iota(jnp.int32, (half, 2 * rows), 0)
        parts = []
        for part in range(2):
            first = order[2 * index + part] * half
            parts.append(jnp.logical_and(position >= low - first, position < high - first))
        return parts

    def score(h, first, second):
        key = jnp.concatenate([kbuf[h, first], kbuf[h, second]], axis=0)
        query = jnp.concatenate([qbuf[0, h], qbuf[1, h]], axis=0)
        scores = dot_nt(key[:, :HDIM], query[:, HDIM:]) * scale
        tan_scores = dot_nt(key, query) * scale
        masks = allowed_keys(first) + allowed_keys(second)
        masked = jnp.concatenate(
            [
                jnp.where(mask, scores[i * half : (i + 1) * half], MASKED)
                for i, mask in enumerate(masks)
            ],
            axis=0,
        )
        peak = stats[h, 0:1, :]
        new_peak = jnp.maximum(peak, jnp.max(masked, axis=0, keepdims=True))
        weights = jnp.exp(masked - new_peak)
        rescale = jnp.exp(peak - new_peak)
        products = weights * tan_scores
        stats[h, 0:1, :] = new_peak
        stats[h, 1:2, :] = rescale * stats[h, 1:2, :] + jnp.sum(weights, axis=0, keepdims=True)
        stats[h, 2:3, :] = rescale * stats[h, 2:3, :] + jnp.sum(products, axis=0, keepdims=True)
        stats[h, 3:4, :] = rescale
        factors[0] = weights.astype(jnp.bfloat16)
        factors[1] = products.astype(jnp.bfloat16)

    def apply(h, first, second):
        value = jnp.concatenate([vbuf[h, first], vbuf[h, second]], axis=1)
        both = dot(value, factors[0])
        moved = dot(value[:HDIM], factors[1])
        rescale = stats[h, 3:4, :]
        acc[h, 0:HDIM, :] = rescale * acc[h, 0:HDIM, :] + both[:HDIM]
        acc[h, HDIM:, :] = rescale * acc[h, HDIM:, :] + both[HDIM:] + moved

    def finish(h):
        for slot in (1, 0):
            lanes = slice(slot * rows, (slot + 1) * rows)
            sums = stats[h, 1:2, lanes]
            inverse = jnp.where(sums > 0.0, 1.0 / jnp.where(sums > 0.0, sums, 1.0), 0.0)
            mean = stats[h, 2:3, lanes] * inverse
            primal = acc[h, 0:HDIM, lanes] * inverse
            tangent = acc[h, HDIM:, lanes] * inverse - mean * primal
            out_ref, stats_ref = ((own_o, own_stats), (o_send, s_send))[slot]
            out_ref[h, 0:HDIM, :] = primal.astype(out_ref.dtype)
            out_ref[h, HDIM:, :] = tangent.astype(out_ref.dtype)
            for i, row in enumerate((stats[h, 0:1, lanes], sums, mean)):
                stats_ref[h, i : i + 1, :] = row
            if slot == 1:
                for copy in o_copies(h):
                    copy.start()

    def merge(h):
        for copy in o_copies(h):
            copy.wait()
        peaks, sums, means = [], [], []
        for ref in (own_stats, s_recv):
            peaks.append(ref[h, 0:1, :])
            sums.append(ref[h, 1:2, :])
            means.append(ref[h, 2:3, :])
        peak = jnp.maximum(peaks[0], peaks[1])
        shares = [sums[i] * jnp.exp(peaks[i] - peak) for i in range(2)]
        inverse = 1.0 / (shares[0] + shares[1])
        shares = [share * inverse for share in shares]
        mean = shares[0] * means[0] + shares[1] * means[1]
        primals = [own_o[h, 0:HDIM, :], o_recv[h, 0:HDIM, :].astype(jnp.float32)]
        tangents = [own_o[h, HDIM:, :], o_recv[h, HDIM:, :].astype(jnp.float32)]
        primal = shares[0] * primals[0] + shares[1] * primals[1]
        tangent = sum(
            shares[i] * (tangents[i] + (means[i] - mean) * primals[i]) for i in range(2)
        )
        gbuf[h, hd, 0:rows, :] = primal.T.astype(jnp.bfloat16)
        gbuf[h, hd, rows:, :] = tangent.T.astype(jnp.bfloat16)
        for i in range(1, n_head):
            g_copy(h, i).start()

    def project(h):
        for i in range(1, n_head):
            g_copy(h, i).wait()
        features = jnp.concatenate([gbuf[h, g] for g in range(n_head)], axis=1)
        total[...] += dot(features, wbuf[h])

    mid = 3 * depth // 2
    late = mid + depth
    steps = heads * depth

    def place(index):
        group, turn = index // 3, index % 3
        slow = turn % 2
        h_a = slow
        d_a = (1 - slow) * (2 * group + turn // 2 + 1) + slow * (group + 1)
        pair, new = (index - mid) // 2, (index - mid) % 2
        h_b = 1 + new
        d_b = pair + 1 + (1 - new) * (depth // 2)
        d_c = depth // 2 + index - late + 1
        past_mid = jnp.minimum(index // mid, 1)
        past_late = jnp.minimum(index // late, 1)
        h = (1 - past_mid) * h_a + (past_mid - past_late) * h_b + past_late * 2
        d = (1 - past_mid) * d_a + (past_mid - past_late) * d_b + past_late * d_c
        return h, d

    def forward(h, d, piece):
        for side in range(2):
            crosses = piece == side

            def take(side=side, crosses=crosses):
                arrived = ring_copy(h, d - 1, piece, side)
                arrived.wait_recv()

                @pl.when(d < depth if crosses else d < depth - 1)
                def _():
                    ring_copy(h, d, piece, side).start()

                arrived.wait_send()

            if crosses:
                take()
            else:
                pl.when(d < depth)(take)

    def step(index, carry):
        h, d = place(index)
        old_h, old_d = place(jnp.maximum(index - 1, 0))
        first, second = (z + nz - old_d) % nz, (z + old_d % depth) % nz
        live = index < steps

        @pl.when(live)
        def _():
            forward(h, d, 0)

        @pl.when(index > 0)
        def _():
            @pl.when(old_d == 1)
            def _():
                stats[old_h, 0:1, :] = jnp.full((1, 2 * rows), NONE_SEEN, jnp.float32)
                stats[old_h, 1:3, :] = jnp.zeros((2, 2 * rows), jnp.float32)
                acc[old_h] = jnp.zeros((2 * HDIM, 2 * rows), jnp.float32)
                q_copy(old_h).wait()

            score(old_h, first, second)

        @pl.when(live)
        def _():
            forward(h, d, 1)

        @pl.when(index > 0)
        def _():
            apply(old_h, first, second)

            @pl.when(old_d == depth)
            def _():
                finish(old_h)

        @pl.when(index == late - 2)
        def _():
            for i in range(1, n_head):
                w_copy(i).wait()
                w_share(i).start()

        @pl.when(jnp.logical_and(d == depth - 1, h == 0))
        def _():
            send_own(heads - 1, range(PIECES))

        for early, when in ((0, mid + 2), (1, late + 1)):

            @pl.when(index == when)
            def _(early=early):
                merge(early)

        return carry

    lax.fori_loop(0, steps + 1, step, 0)
    own_w.wait()
    for i in range(1, n_head):
        w_share(i).wait()
    project(0)
    merge(heads - 1)
    for h in range(1, heads):
        project(h)
    out[...] = total[...].astype(out.dtype)


def local(
    queries,
    keys,
    values,
    tan_queries,
    tan_keys,
    tan_values,
    out_weight,
    clip_lengths,
    stretch_order,
):
    rows, width = queries.shape
    heads = width // HDIM
    n_head = lax.axis_size("head")
    nz = lax.axis_size("ctx") // 2
    depth = nz // 2
    ncol = out_weight.shape[1] // n_head
    bf16, f32 = jnp.bfloat16, jnp.float32
    weight = out_weight.reshape(heads, HDIM, out_weight.shape[1])
    dma = pltpu.SemaphoreType.DMA
    anywhere = pl.BlockSpec(memory_space=pl.ANY)
    in_vmem = pl.BlockSpec(memory_space=pltpu.VMEM)
    both = pl.pallas_call(
        functools.partial(kernel, nz, n_head),
        out_shape=jax.ShapeDtypeStruct((2 * rows, ncol), bf16),
        in_specs=[anywhere] * 9,
        out_specs=in_vmem,
        scratch_shapes=[
            pltpu.SMEM(clip_lengths.shape, jnp.int32),
            pltpu.SMEM(stretch_order.shape, jnp.int32),
            pltpu.VMEM((6, rows, width), bf16),
            pltpu.VMEM((2, heads, rows, 2 * HDIM), bf16),
            pltpu.VMEM((heads, nz, rows, 2 * HDIM), bf16),
            pltpu.VMEM((heads, nz, 2 * HDIM, rows), bf16),
            pltpu.VMEM((heads, n_head * HDIM, ncol), bf16),
            pltpu.VMEM((8, 2 * rows), jnp.int32),
            pltpu.VMEM((heads, 8, 2 * rows), f32),
            pltpu.VMEM((heads, 2 * HDIM, 2 * rows), f32),
            pltpu.VMEM((2, 2 * rows, 2 * rows), bf16),
            pltpu.VMEM((heads, 2 * HDIM, rows), f32),
            pltpu.VMEM((heads, 8, rows), f32),
            pltpu.VMEM((heads, 2 * HDIM, rows), bf16),
            pltpu.VMEM((heads, 8, rows), f32),
            pltpu.VMEM((heads, 2 * HDIM, rows), bf16),
            pltpu.VMEM((heads, 8, rows), f32),
            pltpu.VMEM((heads, n_head, 2 * rows, HDIM), bf16),
            pltpu.VMEM((2 * rows, ncol), f32),
            dma((8,)),
            dma((2, PIECES, 2 * heads)),
            dma((2, PIECES, heads * depth)),
            dma((2, heads)),
            dma((4, n_head - 1)),
            dma,
            dma((2, heads)),
            dma((2, heads)),
            dma((heads, n_head - 1)),
            dma((heads, n_head - 1)),
        ],
        compiler_params=pltpu.CompilerParams(
            collective_id=0,
            has_side_effects=True,
            vmem_limit_bytes=60 * 1024 * 1024,
        ),
        cost_estimate=pl.CostEstimate(
            flops=2 * 6 * 2 * rows * nz * rows * width + 4 * rows * n_head * width * ncol,
            bytes_accessed=8 * 1024 * 1024,
            transcendentals=2 * rows * nz * rows * heads,
        ),
    )(
        queries,
        keys,
        values,
        tan_queries,
        tan_keys,
        tan_values,
        weight,
        clip_lengths,
        stretch_order,
    )
    return both[:rows], both[rows:]


def solution(mesh):
    placed = P(("dp", "ctx"), "head")
    return jax.shard_map(
        local,
        mesh=mesh,
        in_specs=(placed,) * 6 + (P("head", None), P("dp"), P("dp")),
        out_specs=(placed, placed),
        check_vma=False,
    )
```

```python
import functools
import math

import jax
import jax.numpy as jnp
from jax import lax
from jax.experimental import pallas as pl
from jax.experimental.pallas import tpu as pltpu
from jax.sharding import PartitionSpec as P

HDIM = 128
PIECES = 4
NONE_SEEN = -1e29
MASKED = -1e30


def dot(a, b):
    return lax.dot_general(a, b, (((1,), (0,)), ((), ())), preferred_element_type=jnp.float32)


def turned(block):
    return block.astype(jnp.float32).T.astype(jnp.bfloat16)


def schedule(heads, depth):
    if heads != 3 or depth != 8:
        return [(h, d) for d in range(1, depth + 1) for h in range(heads)]
    turns = [0, 1, 0, 2] * 3 + [0, 1] * 2 + [2, 1] * 3 + [2, 2]
    return [(h, turns[: i + 1].count(h)) for i, h in enumerate(turns)]


def kernel(
    nz,
    n_head,
    q_in,
    k_in,
    v_in,
    tq_in,
    tk_in,
    tv_in,
    w_in,
    lengths_in,
    order_in,
    out,
    lengths,
    order,
    stage,
    qbuf,
    kbuf,
    vbuf,
    wbuf,
    bounds,
    stats,
    acc,
    factors,
    own_o,
    own_stats,
    o_send,
    s_send,
    o_recv,
    s_recv,
    gbuf,
    total,
    stage_sem,
    ring_send,
    ring_recv,
    q_sem,
    w_sem,
    w_own_sem,
    o_sem,
    s_sem,
    g_send,
    g_recv,
):
    rows = q_in.shape[0]
    heads = q_in.shape[1] // HDIM
    half = rows // 2
    clips = lengths.shape[0]
    depth = nz // 2
    ncol = wbuf.shape[2]
    w_half = HDIM // 2
    scale = 1.0 / HDIM**0.5

    ctx = lax.axis_index("ctx")
    hd = lax.axis_index("head")
    core = lax.axis_index("dp")
    column = ctx // nz
    z = ctx % nz
    right = column * nz + (z + 1) % nz
    left = column * nz + (z + nz - 1) % nz
    partner = (ctx + nz) % (2 * nz)

    stages = [
        pltpu.make_async_copy(ref, stage.at[i], stage_sem.at[i])
        for i, ref in enumerate((k_in, tk_in, v_in, tv_in, q_in, tq_in))
    ]
    tables = [
        pltpu.make_async_copy(src, dst, stage_sem.at[6 + i])
        for i, (src, dst) in enumerate(((lengths_in, lengths), (order_in, order)))
    ]
    for copy in stages + tables:
        copy.start()
    own_w = pltpu.make_async_copy(
        w_in.at[:, :, pl.ds(pl.multiple_of(hd * ncol, 128), ncol)],
        wbuf.at[:, pl.ds(pl.multiple_of(hd * HDIM, HDIM), HDIM), :],
        w_own_sem,
    )
    own_w.start()

    barrier = pltpu.get_barrier_semaphore()
    for other in (right, left, partner):
        pl.semaphore_signal(barrier, inc=1, device_id={"ctx": other})
    for i in range(1, n_head):
        pl.semaphore_signal(barrier, inc=1, device_id={"head": (hd + i) % n_head})
    pl.semaphore_signal(barrier, inc=1, device_id={"dp": 1 - core})

    for copy in tables:
        copy.wait()
    ends = []
    running = jnp.int32(0)
    for c in range(clips):
        running = running + lengths[c]
        ends.append(running)
    lane = lax.broadcasted_iota(jnp.int32, (1, rows), 1)
    for slot, index in enumerate((ctx, partner)):
        anchor = jnp.where(
            lane < half,
            order[2 * index] * half + lane,
            order[2 * index + 1] * half + lane - half,
        )
        low = jnp.zeros_like(anchor)
        high = jnp.full_like(anchor, rows * nz * 2)
        for end in ends:
            low = jnp.where(end <= anchor, jnp.maximum(low, end), low)
            high = jnp.where(end > anchor, jnp.minimum(high, end), high)
        bounds[0:1, slot * rows : (slot + 1) * rows] = low
        bounds[1:2, slot * rows : (slot + 1) * rows] = high

    def ring_copy(h, hop, piece, side):
        source = (z + nz - hop) % nz if side == 0 else (z + hop) % nz
        step = h * depth + hop
        buf = kbuf if piece < 2 else vbuf
        size = buf.shape[2] // 2
        ref = buf.at[h, source, pl.ds((piece % 2) * size, size), :]
        return pltpu.make_async_remote_copy(
            src_ref=ref,
            dst_ref=ref,
            send_sem=ring_send.at[side, piece, h * 2 + hop % 2],
            recv_sem=ring_recv.at[side, piece, step],
            device_id={"ctx": right if side == 0 else left},
        )

    def send_own(h, pieces):
        for piece in pieces:
            for side in range(2):
                ring_copy(h, 0, piece, side).start()

    def q_copy(h):
        return pltpu.make_async_remote_copy(
            src_ref=qbuf.at[0, h],
            dst_ref=qbuf.at[1, h],
            send_sem=q_sem.at[0, h],
            recv_sem=q_sem.at[1, h],
            device_id={"ctx": partner},
        )

    def w_copy(i):
        other = (hd + i) % n_head
        return pltpu.make_async_remote_copy(
            src_ref=w_in.at[
                :,
                pl.ds(pl.multiple_of(core * w_half, w_half), w_half),
                pl.ds(pl.multiple_of(other * ncol, 128), ncol),
            ],
            dst_ref=wbuf.at[:, pl.ds(pl.multiple_of(hd * HDIM + core * w_half, w_half), w_half), :],
            send_sem=w_sem.at[0, i - 1],
            recv_sem=w_sem.at[1, i - 1],
            device_id={"head": other},
        )

    def w_share(i):
        source = (hd + n_head - i) % n_head
        ref = wbuf.at[:, pl.ds(pl.multiple_of(source * HDIM + core * w_half, w_half), w_half), :]
        return pltpu.make_async_remote_copy(
            src_ref=ref,
            dst_ref=ref,
            send_sem=w_sem.at[2, i - 1],
            recv_sem=w_sem.at[3, i - 1],
            device_id={"dp": 1 - core},
        )

    def o_copies(h):
        return [
            pltpu.make_async_remote_copy(
                src_ref=src.at[h],
                dst_ref=dst.at[h],
                send_sem=sem.at[0, h],
                recv_sem=sem.at[1, h],
                device_id={"ctx": partner},
            )
            for src, dst, sem in ((s_send, s_recv, s_sem), (o_send, o_recv, o_sem))
        ]

    def g_copy(h, i):
        return pltpu.make_async_remote_copy(
            src_ref=gbuf.at[h, hd],
            dst_ref=gbuf.at[h, hd],
            send_sem=g_send.at[h, i - 1],
            recv_sem=g_recv.at[h, i - 1],
            device_id={"head": (hd + i) % n_head},
        )

    columns = [slice(h * HDIM, (h + 1) * HDIM) for h in range(heads)]
    for copy in stages[:2]:
        copy.wait()
    for h, cols in enumerate(columns):
        kbuf[h, z, :, 0:HDIM] = stage[0, :, cols]
        kbuf[h, z, :, HDIM : 2 * HDIM] = stage[1, :, cols]
    pl.semaphore_wait(barrier, 3 + n_head)
    send_own(0, range(2))
    for copy in stages[2:4]:
        copy.wait()
    for h, cols in enumerate(columns):
        vbuf[h, z, 0:HDIM, :] = turned(stage[2, :, cols])
        vbuf[h, z, HDIM : 2 * HDIM, :] = turned(stage[3, :, cols])
    send_own(0, range(2, PIECES))
    for h in range(1, heads):
        send_own(h, range(PIECES))
    for copy in stages[4:]:
        copy.wait()
    for h, cols in enumerate(columns):
        qbuf[0, h, 0:HDIM, :] = turned(stage[5, :, cols])
        qbuf[0, h, HDIM : 2 * HDIM, :] = turned(stage[4, :, cols])
        q_copy(h).start()
    for i in range(1, n_head):
        w_copy(i).start()
    total[...] = jnp.zeros_like(total)
    s_send[...] = jnp.zeros_like(s_send)

    def allowed_keys(source):
        low, high = bounds[0:1, :], bounds[1:2, :]
        index = column * nz + source
        position = lax.broadcasted_iota(jnp.int32, (half, 2 * rows), 0)
        parts = []
        for part in range(2):
            first = order[2 * index + part] * half
            parts.append(jnp.logical_and(position >= low - first, position < high - first))
        return parts

    def score(h, first, second):
        key = jnp.concatenate([kbuf[h, first], kbuf[h, second]], axis=0)
        query = jnp.concatenate([qbuf[0, h], qbuf[1, h]], axis=1)
        scores = dot(key[:, :HDIM], query[HDIM:]) * (scale * math.log2(math.e))
        tan_scores = dot(key, query)
        masks = allowed_keys(first) + allowed_keys(second)
        masked = jnp.concatenate(
            [
                jnp.where(mask, scores[i * half : (i + 1) * half], MASKED)
                for i, mask in enumerate(masks)
            ],
            axis=0,
        )
        peak = stats[h, 0:1, :]
        new_peak = jnp.maximum(peak, jnp.max(masked, axis=0, keepdims=True))
        weights = jnp.exp2(masked - new_peak)
        rescale = jnp.exp2(peak - new_peak)
        products = weights * tan_scores
        stats[h, 0:1, :] = new_peak
        stats[h, 1:2, :] = rescale * stats[h, 1:2, :] + jnp.sum(weights, axis=0, keepdims=True)
        stats[h, 2:3, :] = rescale * stats[h, 2:3, :] + scale * jnp.sum(
            products, axis=0, keepdims=True
        )
        stats[h, 3:4, :] = rescale
        factors[0] = weights.astype(jnp.bfloat16)
        factors[1] = products.astype(jnp.bfloat16)

    def apply(h, first, second):
        value = jnp.concatenate([vbuf[h, first], vbuf[h, second]], axis=1)
        both = dot(value, factors[0])
        moved = dot(value[:HDIM], factors[1])
        rescale = stats[h, 3:4, :]
        acc[h, 0:HDIM, :] = rescale * acc[h, 0:HDIM, :] + both[:HDIM]
        acc[h, HDIM:, :] = rescale * acc[h, HDIM:, :] + both[HDIM:] + scale * moved

    def finish(h):
        for slot in (1, 0):
            lanes = slice(slot * rows, (slot + 1) * rows)
            sums = stats[h, 1:2, lanes]
            inverse = jnp.where(sums > 0.0, 1.0 / jnp.where(sums > 0.0, sums, 1.0), 0.0)
            mean = stats[h, 2:3, lanes] * inverse
            primal = acc[h, 0:HDIM, lanes] * inverse
            tangent = acc[h, HDIM:, lanes] * inverse - mean * primal
            out_ref, stats_ref = ((own_o, own_stats), (o_send, s_send))[slot]
            out_ref[h, 0:HDIM, :] = primal.astype(out_ref.dtype)
            out_ref[h, HDIM:, :] = tangent.astype(out_ref.dtype)
            for i, row in enumerate((stats[h, 0:1, lanes], sums, mean)):
                stats_ref[h, i : i + 1, :] = row
            if slot == 1:
                for copy in o_copies(h):
                    copy.start()

    def merge(h):
        for copy in o_copies(h):
            copy.wait()
        peaks, sums, means = [], [], []
        for ref in (own_stats, s_recv):
            peaks.append(ref[h, 0:1, :])
            sums.append(ref[h, 1:2, :])
            means.append(ref[h, 2:3, :])
        peak = jnp.maximum(peaks[0], peaks[1])
        shares = [sums[i] * jnp.exp2(peaks[i] - peak) for i in range(2)]
        inverse = 1.0 / (shares[0] + shares[1])
        shares = [share * inverse for share in shares]
        mean = shares[0] * means[0] + shares[1] * means[1]
        primals = [own_o[h, 0:HDIM, :], o_recv[h, 0:HDIM, :].astype(jnp.float32)]
        tangents = [own_o[h, HDIM:, :], o_recv[h, HDIM:, :].astype(jnp.float32)]
        primal = shares[0] * primals[0] + shares[1] * primals[1]
        tangent = sum(
            shares[i] * (tangents[i] + (means[i] - mean) * primals[i]) for i in range(2)
        )
        gbuf[h, hd, 0:rows, :] = primal.T.astype(jnp.bfloat16)
        gbuf[h, hd, rows:, :] = tangent.T.astype(jnp.bfloat16)
        for i in range(1, n_head):
            g_copy(h, i).start()

    def project(h):
        for first in range(0, n_head, 2):
            sources = [(hd + n_head - i) % n_head for i in (first, first + 1)]
            for i in (first, first + 1):
                if i > 0:
                    g_copy(h, i).wait()
            features = jnp.concatenate([gbuf[h, source] for source in sources], axis=1)
            weight = jnp.concatenate(
                [
                    wbuf[h, pl.ds(pl.multiple_of(source * HDIM, HDIM), HDIM), :]
                    for source in sources
                ],
                axis=0,
            )
            total[...] += dot(features, weight)

    order_of = schedule(heads, depth)
    steps = len(order_of)
    finished = [order_of.index((h, depth)) for h in range(heads)]

    def place(index):
        h = d = 0
        for i, (head_at, hop_at) in enumerate(order_of):
            h = h + jnp.where(index == i, head_at, 0)
            d = d + jnp.where(index == i, hop_at, 0)
        return h, d

    def forward(h, d, piece):
        for side in range(2):
            crosses = (piece < 2) == (side == 0)

            def take(side=side, crosses=crosses):
                arrived = ring_copy(h, d - 1, piece, side)
                arrived.wait_recv()

                @pl.when(d < depth if crosses else d < depth - 1)
                def _():
                    ring_copy(h, d, piece, side).start()

                arrived.wait_send()

            if crosses:
                take()
            else:
                pl.when(d < depth)(take)

    def step(index, carry):
        h, d = place(index)
        old_h, old_d = carry
        first, second = (z + nz - old_d) % nz, (z + old_d % depth) % nz
        live = index < steps

        @pl.when(live)
        def _():
            forward(h, d, 0)

        @pl.when(index > 0)
        def _():
            @pl.when(old_d == 1)
            def _():
                stats[old_h, 0:1, :] = jnp.full((1, 2 * rows), NONE_SEEN, jnp.float32)
                stats[old_h, 1:3, :] = jnp.zeros((2, 2 * rows), jnp.float32)
                acc[old_h] = jnp.zeros((2 * HDIM, 2 * rows), jnp.float32)
                q_copy(old_h).wait()

            score(old_h, first, second)

        @pl.when(live)
        def _():
            forward(h, d, 1)

        @pl.when(index > 0)
        def _():
            apply(old_h, first, second)

            @pl.when(old_d == depth)
            def _():
                finish(old_h)

        @pl.when(live)
        def _():
            for piece in range(2, PIECES):
                forward(h, d, piece)

        @pl.when(index == min(finished[0] + 2, steps))
        def _():
            for i in range(1, n_head):
                w_copy(i).wait()
                w_share(i).start()

        for early in range(heads - 1):

            @pl.when(index == min(finished[early] + 3, steps))
            def _(early=early):
                merge(early)

        return h, d

    lax.fori_loop(0, steps + 1, step, (jnp.int32(0), jnp.int32(1)))
    own_w.wait()
    for i in range(1, n_head):
        w_share(i).wait()
    project(0)
    merge(heads - 1)
    for h in range(1, heads):
        project(h)
    out[...] = total[...].astype(out.dtype)


def local(
    queries,
    keys,
    values,
    tan_queries,
    tan_keys,
    tan_values,
    out_weight,
    clip_lengths,
    stretch_order,
):
    rows, width = queries.shape
    heads = width // HDIM
    n_head = lax.axis_size("head")
    nz = lax.axis_size("ctx") // 2
    depth = nz // 2
    ncol = out_weight.shape[1] // n_head
    bf16, f32 = jnp.bfloat16, jnp.float32
    weight = out_weight.reshape(heads, HDIM, out_weight.shape[1])
    dma = pltpu.SemaphoreType.DMA
    anywhere = pl.BlockSpec(memory_space=pl.ANY)
    in_vmem = pl.BlockSpec(memory_space=pltpu.VMEM)
    both = pl.pallas_call(
        functools.partial(kernel, nz, n_head),
        out_shape=jax.ShapeDtypeStruct((2 * rows, ncol), bf16),
        in_specs=[anywhere] * 9,
        out_specs=in_vmem,
        scratch_shapes=[
            pltpu.SMEM(clip_lengths.shape, jnp.int32),
            pltpu.SMEM(stretch_order.shape, jnp.int32),
            pltpu.VMEM((6, rows, width), bf16),
            pltpu.VMEM((2, heads, 2 * HDIM, rows), bf16),
            pltpu.VMEM((heads, nz, rows, 2 * HDIM), bf16),
            pltpu.VMEM((heads, nz, 2 * HDIM, rows), bf16),
            pltpu.VMEM((heads, n_head * HDIM, ncol), bf16),
            pltpu.VMEM((8, 2 * rows), jnp.int32),
            pltpu.VMEM((heads, 8, 2 * rows), f32),
            pltpu.VMEM((heads, 2 * HDIM, 2 * rows), f32),
            pltpu.VMEM((2, 2 * rows, 2 * rows), bf16),
            pltpu.VMEM((heads, 2 * HDIM, rows), f32),
            pltpu.VMEM((heads, 8, rows), f32),
            pltpu.VMEM((heads, 2 * HDIM, rows), bf16),
            pltpu.VMEM((heads, 8, rows), f32),
            pltpu.VMEM((heads, 2 * HDIM, rows), bf16),
            pltpu.VMEM((heads, 8, rows), f32),
            pltpu.VMEM((heads, n_head, 2 * rows, HDIM), bf16),
            pltpu.VMEM((2 * rows, ncol), f32),
            dma((8,)),
            dma((2, PIECES, 2 * heads)),
            dma((2, PIECES, heads * depth)),
            dma((2, heads)),
            dma((4, n_head - 1)),
            dma,
            dma((2, heads)),
            dma((2, heads)),
            dma((heads, n_head - 1)),
            dma((heads, n_head - 1)),
        ],
        compiler_params=pltpu.CompilerParams(
            collective_id=0,
            has_side_effects=True,
            vmem_limit_bytes=60 * 1024 * 1024,
        ),
        cost_estimate=pl.CostEstimate(
            flops=2 * 6 * 2 * rows * nz * rows * width + 4 * rows * n_head * width * ncol,
            bytes_accessed=8 * 1024 * 1024,
            transcendentals=2 * rows * nz * rows * heads,
        ),
    )(
        queries,
        keys,
        values,
        tan_queries,
        tan_keys,
        tan_values,
        weight,
        clip_lengths,
        stretch_order,
    )
    return both[:rows], both[rows:]


def solution(mesh):
    placed = P(("dp", "ctx"), "head")
    return jax.shard_map(
        local,
        mesh=mesh,
        in_specs=(placed,) * 6 + (P("head", None), P("dp"), P("dp")),
        out_specs=(placed, placed),
        check_vma=False,
    )
```

```python
import functools
import math

import jax
import jax.numpy as jnp
from jax import lax
from jax.experimental import pallas as pl
from jax.experimental.pallas import tpu as pltpu
from jax.sharding import PartitionSpec as P

HDIM = 128
PIECES = 4
NONE_SEEN = -1e29
MASKED = -1e30


def dot(a, b):
    return lax.dot_general(a, b, (((1,), (0,)), ((), ())), preferred_element_type=jnp.float32)


def turned(block):
    return block.astype(jnp.float32).T.astype(jnp.bfloat16)


def schedule(heads, depth):
    if heads != 3 or depth != 8:
        return [(h, d) for d in range(1, depth + 1) for h in range(heads)]
    turns = [0, 1, 0, 2] * 3 + [0, 1] * 2 + [1, 2] * 3 + [2, 2]
    return [(h, turns[: i + 1].count(h)) for i, h in enumerate(turns)]


def kernel(
    nz,
    n_head,
    q_in,
    k_in,
    v_in,
    tq_in,
    tk_in,
    tv_in,
    w_in,
    lengths_in,
    order_in,
    out,
    lengths,
    order,
    stage,
    qbuf,
    kbuf,
    vbuf,
    wbuf,
    bounds,
    stats,
    acc,
    factors,
    own_o,
    own_stats,
    o_send,
    s_send,
    o_recv,
    s_recv,
    gbuf,
    total,
    stage_sem,
    ring_send,
    ring_recv,
    q_sem,
    w_sem,
    w_own_sem,
    o_sem,
    s_sem,
    g_send,
    g_recv,
):
    rows = q_in.shape[0]
    heads = q_in.shape[1] // HDIM
    half = rows // 2
    clips = lengths.shape[0]
    depth = nz // 2
    ncol = wbuf.shape[2]
    w_half = HDIM // 2
    scale = 1.0 / HDIM**0.5

    ctx = lax.axis_index("ctx")
    hd = lax.axis_index("head")
    core = lax.axis_index("dp")
    column = ctx // nz
    z = ctx % nz
    right = column * nz + (z + 1) % nz
    left = column * nz + (z + nz - 1) % nz
    partner = (ctx + nz) % (2 * nz)

    stages = [
        pltpu.make_async_copy(ref, stage.at[i], stage_sem.at[i])
        for i, ref in enumerate((k_in, tk_in, v_in, tv_in, q_in, tq_in))
    ]
    tables = [
        pltpu.make_async_copy(src, dst, stage_sem.at[6 + i])
        for i, (src, dst) in enumerate(((lengths_in, lengths), (order_in, order)))
    ]
    for copy in stages + tables:
        copy.start()
    own_w = pltpu.make_async_copy(
        w_in.at[:, :, pl.ds(pl.multiple_of(hd * ncol, 128), ncol)],
        wbuf.at[:, pl.ds(pl.multiple_of(hd * HDIM, HDIM), HDIM), :],
        w_own_sem,
    )
    own_w.start()

    barrier = pltpu.get_barrier_semaphore()
    for other in (right, left, partner):
        pl.semaphore_signal(barrier, inc=1, device_id={"ctx": other})
    for i in range(1, n_head):
        pl.semaphore_signal(barrier, inc=1, device_id={"head": (hd + i) % n_head})
    pl.semaphore_signal(barrier, inc=1, device_id={"dp": 1 - core})

    for copy in tables:
        copy.wait()
    ends = []
    running = jnp.int32(0)
    for c in range(clips):
        running = running + lengths[c]
        ends.append(running)
    lane = lax.broadcasted_iota(jnp.int32, (1, rows), 1)
    for slot, index in enumerate((ctx, partner)):
        anchor = jnp.where(
            lane < half,
            order[2 * index] * half + lane,
            order[2 * index + 1] * half + lane - half,
        )
        low = jnp.zeros_like(anchor)
        high = jnp.full_like(anchor, rows * nz * 2)
        for end in ends:
            low = jnp.where(end <= anchor, jnp.maximum(low, end), low)
            high = jnp.where(end > anchor, jnp.minimum(high, end), high)
        bounds[0:1, slot * rows : (slot + 1) * rows] = low
        bounds[1:2, slot * rows : (slot + 1) * rows] = high

    def ring_copy(h, hop, piece, side):
        source = (z + nz - hop) % nz if side == 0 else (z + hop) % nz
        step = h * depth + hop
        buf = kbuf if piece < 2 else vbuf
        size = buf.shape[2] // 2
        ref = buf.at[h, source, pl.ds((piece % 2) * size, size), :]
        return pltpu.make_async_remote_copy(
            src_ref=ref,
            dst_ref=ref,
            send_sem=ring_send.at[side, piece, h * 2 + hop % 2],
            recv_sem=ring_recv.at[side, piece, step],
            device_id={"ctx": right if side == 0 else left},
        )

    def send_own(h, pieces):
        for piece in pieces:
            for side in range(2):
                ring_copy(h, 0, piece, side).start()

    def q_copy(h):
        return pltpu.make_async_remote_copy(
            src_ref=qbuf.at[0, h],
            dst_ref=qbuf.at[1, h],
            send_sem=q_sem.at[0, h],
            recv_sem=q_sem.at[1, h],
            device_id={"ctx": partner},
        )

    def w_copy(i):
        other = (hd + i) % n_head
        return pltpu.make_async_remote_copy(
            src_ref=w_in.at[
                :,
                pl.ds(pl.multiple_of(core * w_half, w_half), w_half),
                pl.ds(pl.multiple_of(other * ncol, 128), ncol),
            ],
            dst_ref=wbuf.at[:, pl.ds(pl.multiple_of(hd * HDIM + core * w_half, w_half), w_half), :],
            send_sem=w_sem.at[0, i - 1],
            recv_sem=w_sem.at[1, i - 1],
            device_id={"head": other},
        )

    def w_share(i):
        source = (hd + n_head - i) % n_head
        ref = wbuf.at[:, pl.ds(pl.multiple_of(source * HDIM + core * w_half, w_half), w_half), :]
        return pltpu.make_async_remote_copy(
            src_ref=ref,
            dst_ref=ref,
            send_sem=w_sem.at[2, i - 1],
            recv_sem=w_sem.at[3, i - 1],
            device_id={"dp": 1 - core},
        )

    def o_copies(h):
        return [
            pltpu.make_async_remote_copy(
                src_ref=src.at[h],
                dst_ref=dst.at[h],
                send_sem=sem.at[0, h],
                recv_sem=sem.at[1, h],
                device_id={"ctx": partner},
            )
            for src, dst, sem in ((s_send, s_recv, s_sem), (o_send, o_recv, o_sem))
        ]

    def g_copy(h, i):
        return pltpu.make_async_remote_copy(
            src_ref=gbuf.at[h, hd],
            dst_ref=gbuf.at[h, hd],
            send_sem=g_send.at[h, i - 1],
            recv_sem=g_recv.at[h, i - 1],
            device_id={"head": (hd + i) % n_head},
        )

    columns = [slice(h * HDIM, (h + 1) * HDIM) for h in range(heads)]
    for copy in stages[:2]:
        copy.wait()
    for h, cols in enumerate(columns):
        kbuf[h, z, :, 0:HDIM] = stage[0, :, cols]
        kbuf[h, z, :, HDIM : 2 * HDIM] = stage[1, :, cols]
    pl.semaphore_wait(barrier, 3 + n_head)
    send_own(0, range(2))
    for copy in stages[2:4]:
        copy.wait()
    for h, cols in enumerate(columns):
        vbuf[h, z, 0:HDIM, :] = turned(stage[2, :, cols])
        vbuf[h, z, HDIM : 2 * HDIM, :] = turned(stage[3, :, cols])
    send_own(0, range(2, PIECES))
    for h in range(1, heads):
        send_own(h, range(PIECES))
    for copy in stages[4:]:
        copy.wait()
    for h, cols in enumerate(columns):
        qbuf[0, h, 0:HDIM, :] = turned(stage[5, :, cols])
        qbuf[0, h, HDIM : 2 * HDIM, :] = turned(stage[4, :, cols])
        q_copy(h).start()
    for i in range(1, n_head):
        w_copy(i).start()
    total[...] = jnp.zeros_like(total)
    s_send[...] = jnp.zeros_like(s_send)

    def allowed_keys(source):
        low, high = bounds[0:1, :], bounds[1:2, :]
        index = column * nz + source
        position = lax.broadcasted_iota(jnp.int32, (half, 2 * rows), 0)
        parts = []
        for part in range(2):
            first = order[2 * index + part] * half
            parts.append(jnp.logical_and(position >= low - first, position < high - first))
        return parts

    def score(h, sources):
        key = jnp.concatenate([kbuf[h, source] for source in sources], axis=0)
        query = jnp.concatenate([qbuf[0, h], qbuf[1, h]], axis=1)
        scores = dot(key[:, :HDIM], query[HDIM:]) * (scale * math.log2(math.e))
        tan_scores = dot(key, query)
        masks = [mask for source in sources for mask in allowed_keys(source)]
        masked = jnp.concatenate(
            [
                jnp.where(mask, scores[i * half : (i + 1) * half], MASKED)
                for i, mask in enumerate(masks)
            ],
            axis=0,
        )
        peak = stats[h, 0:1, :]
        new_peak = jnp.maximum(peak, jnp.max(masked, axis=0, keepdims=True))
        weights = jnp.exp2(masked - new_peak)
        rescale = jnp.exp2(peak - new_peak)
        products = weights * tan_scores
        stats[h, 0:1, :] = new_peak
        stats[h, 1:2, :] = rescale * stats[h, 1:2, :] + jnp.sum(weights, axis=0, keepdims=True)
        stats[h, 2:3, :] = rescale * stats[h, 2:3, :] + scale * jnp.sum(
            products, axis=0, keepdims=True
        )
        stats[h, 3:4, :] = rescale
        span = len(sources) * rows
        factors[0, 0:span] = weights.astype(jnp.bfloat16)
        factors[1, 0:span] = products.astype(jnp.bfloat16)

    def apply(h, sources):
        value = jnp.concatenate([vbuf[h, source] for source in sources], axis=1)
        span = len(sources) * rows
        both = dot(value, factors[0, 0:span])
        moved = dot(value[:HDIM], factors[1, 0:span])
        rescale = stats[h, 3:4, :]
        acc[h, 0:HDIM, :] = rescale * acc[h, 0:HDIM, :] + both[:HDIM]
        acc[h, HDIM:, :] = rescale * acc[h, HDIM:, :] + both[HDIM:] + scale * moved

    def finish(h):
        for slot in (1, 0):
            lanes = slice(slot * rows, (slot + 1) * rows)
            sums = stats[h, 1:2, lanes]
            inverse = jnp.where(sums > 0.0, 1.0 / jnp.where(sums > 0.0, sums, 1.0), 0.0)
            mean = stats[h, 2:3, lanes] * inverse
            primal = acc[h, 0:HDIM, lanes] * inverse
            tangent = acc[h, HDIM:, lanes] * inverse - mean * primal
            out_ref, stats_ref = ((own_o, own_stats), (o_send, s_send))[slot]
            out_ref[h, 0:HDIM, :] = primal.astype(out_ref.dtype)
            out_ref[h, HDIM:, :] = tangent.astype(out_ref.dtype)
            for i, row in enumerate((stats[h, 0:1, lanes], sums, mean)):
                stats_ref[h, i : i + 1, :] = row
            if slot == 1:
                for copy in o_copies(h):
                    copy.start()

    def merge(h):
        for copy in o_copies(h):
            copy.wait()
        peaks, sums, means = [], [], []
        for ref in (own_stats, s_recv):
            peaks.append(ref[h, 0:1, :])
            sums.append(ref[h, 1:2, :])
            means.append(ref[h, 2:3, :])
        peak = jnp.maximum(peaks[0], peaks[1])
        shares = [sums[i] * jnp.exp2(peaks[i] - peak) for i in range(2)]
        inverse = 1.0 / (shares[0] + shares[1])
        shares = [share * inverse for share in shares]
        mean = shares[0] * means[0] + shares[1] * means[1]
        primals = [own_o[h, 0:HDIM, :], o_recv[h, 0:HDIM, :].astype(jnp.float32)]
        tangents = [own_o[h, HDIM:, :], o_recv[h, HDIM:, :].astype(jnp.float32)]
        primal = shares[0] * primals[0] + shares[1] * primals[1]
        tangent = sum(
            shares[i] * (tangents[i] + (means[i] - mean) * primals[i]) for i in range(2)
        )
        gbuf[h, hd, 0:rows, :] = primal.T.astype(jnp.bfloat16)
        gbuf[h, hd, rows:, :] = tangent.T.astype(jnp.bfloat16)
        for i in range(1, n_head):
            g_copy(h, i).start()

    def project(h):
        for first in range(0, n_head, 2):
            sources = [(hd + n_head - i) % n_head for i in (first, first + 1)]
            for i in (first, first + 1):
                if i > 0:
                    g_copy(h, i).wait()
            features = jnp.concatenate([gbuf[h, source] for source in sources], axis=1)
            weight = jnp.concatenate(
                [
                    wbuf[h, pl.ds(pl.multiple_of(source * HDIM, HDIM), HDIM), :]
                    for source in sources
                ],
                axis=0,
            )
            total[...] += dot(features, weight)

    order_of = schedule(heads, depth)
    steps = len(order_of)
    finished = [order_of.index((h, depth)) for h in range(heads)]

    def place(index):
        h = d = 0
        for i, (head_at, hop_at) in enumerate(order_of):
            h = h + jnp.where(index == i, head_at, 0)
            d = d + jnp.where(index == i, hop_at, 0)
        return h, d

    def forward(h, d, piece):
        for side in range(2):
            crosses = (piece < 2) == (side == 0)

            def take(side=side, crosses=crosses):
                arrived = ring_copy(h, d - 1, piece, side)
                arrived.wait_recv()

                @pl.when(d < depth if crosses else d < depth - 1)
                def _():
                    ring_copy(h, d, piece, side).start()

                arrived.wait_send()

            if crosses:
                take()
            else:
                pl.when(d < depth)(take)

    def step(index, carry):
        h, d = place(index)
        old_h, old_d = carry
        far, near = [(z + nz - old_d) % nz], [(z + nz - old_d) % nz, (z + old_d) % nz]
        live = index < steps

        @pl.when(live)
        def _():
            forward(h, d, 0)

        @pl.when(index > 0)
        def _():
            @pl.when(old_d == 1)
            def _():
                stats[old_h, 0:1, :] = jnp.full((1, 2 * rows), NONE_SEEN, jnp.float32)
                stats[old_h, 1:3, :] = jnp.zeros((2, 2 * rows), jnp.float32)
                acc[old_h] = jnp.zeros((2 * HDIM, 2 * rows), jnp.float32)
                q_copy(old_h).wait()
                score(old_h, [z])
                apply(old_h, [z])

            @pl.when(old_d < depth)
            def _():
                score(old_h, near)

            @pl.when(old_d == depth)
            def _():
                score(old_h, far)

        @pl.when(live)
        def _():
            forward(h, d, 1)

        @pl.when(index > 0)
        def _():
            @pl.when(old_d < depth)
            def _():
                apply(old_h, near)

            @pl.when(old_d == depth)
            def _():
                apply(old_h, far)
                finish(old_h)

        @pl.when(live)
        def _():
            for piece in range(2, PIECES):
                forward(h, d, piece)

        @pl.when(index == min(finished[0] + 2, steps))
        def _():
            for i in range(1, n_head):
                w_copy(i).wait()
                w_share(i).start()

        for early in range(heads - 1):

            @pl.when(index == min(finished[early] + 2, steps))
            def _(early=early):
                merge(early)

        return h, d

    lax.fori_loop(0, steps + 1, step, (jnp.int32(0), jnp.int32(1)))
    own_w.wait()
    for i in range(1, n_head):
        w_share(i).wait()
    project(0)
    merge(heads - 1)
    for h in range(1, heads):
        project(h)
    out[...] = total[...].astype(out.dtype)


def local(
    queries,
    keys,
    values,
    tan_queries,
    tan_keys,
    tan_values,
    out_weight,
    clip_lengths,
    stretch_order,
):
    rows, width = queries.shape
    heads = width // HDIM
    n_head = lax.axis_size("head")
    nz = lax.axis_size("ctx") // 2
    depth = nz // 2
    ncol = out_weight.shape[1] // n_head
    bf16, f32 = jnp.bfloat16, jnp.float32
    weight = out_weight.reshape(heads, HDIM, out_weight.shape[1])
    dma = pltpu.SemaphoreType.DMA
    anywhere = pl.BlockSpec(memory_space=pl.ANY)
    in_vmem = pl.BlockSpec(memory_space=pltpu.VMEM)
    both = pl.pallas_call(
        functools.partial(kernel, nz, n_head),
        out_shape=pltpu.VMEM((2 * rows, ncol), bf16),
        in_specs=[anywhere] * 9,
        out_specs=in_vmem,
        scratch_shapes=[
            pltpu.SMEM(clip_lengths.shape, jnp.int32),
            pltpu.SMEM(stretch_order.shape, jnp.int32),
            pltpu.VMEM((6, rows, width), bf16),
            pltpu.VMEM((2, heads, 2 * HDIM, rows), bf16),
            pltpu.VMEM((heads, nz, rows, 2 * HDIM), bf16),
            pltpu.VMEM((heads, nz, 2 * HDIM, rows), bf16),
            pltpu.VMEM((heads, n_head * HDIM, ncol), bf16),
            pltpu.VMEM((8, 2 * rows), jnp.int32),
            pltpu.VMEM((heads, 8, 2 * rows), f32),
            pltpu.VMEM((heads, 2 * HDIM, 2 * rows), f32),
            pltpu.VMEM((2, 2 * rows, 2 * rows), bf16),
            pltpu.VMEM((heads, 2 * HDIM, rows), f32),
            pltpu.VMEM((heads, 8, rows), f32),
            pltpu.VMEM((heads, 2 * HDIM, rows), bf16),
            pltpu.VMEM((heads, 8, rows), f32),
            pltpu.VMEM((heads, 2 * HDIM, rows), bf16),
            pltpu.VMEM((heads, 8, rows), f32),
            pltpu.VMEM((heads, n_head, 2 * rows, HDIM), bf16),
            pltpu.VMEM((2 * rows, ncol), f32),
            dma((8,)),
            dma((2, PIECES, 2 * heads)),
            dma((2, PIECES, heads * depth)),
            dma((2, heads)),
            dma((4, n_head - 1)),
            dma,
            dma((2, heads)),
            dma((2, heads)),
            dma((heads, n_head - 1)),
            dma((heads, n_head - 1)),
        ],
        compiler_params=pltpu.CompilerParams(
            collective_id=0,
            has_side_effects=True,
            vmem_limit_bytes=60 * 1024 * 1024,
        ),
        cost_estimate=pl.CostEstimate(
            flops=2 * 6 * 2 * rows * nz * rows * width + 4 * rows * n_head * width * ncol,
            bytes_accessed=8 * 1024 * 1024,
            transcendentals=2 * rows * nz * rows * heads,
        ),
    )(
        queries,
        keys,
        values,
        tan_queries,
        tan_keys,
        tan_values,
        weight,
        clip_lengths,
        stretch_order,
    )
    return both[:rows], both[rows:]


def solution(mesh):
    placed = P(("dp", "ctx"), "head")
    return jax.shard_map(
        local,
        mesh=mesh,
        in_specs=(placed,) * 6 + (P("head", None), P("dp"), P("dp")),
        out_specs=(placed, placed),
        check_vma=False,
    )
```

```python
import functools
import math

import jax
import jax.numpy as jnp
from jax import lax
from jax.experimental import pallas as pl
from jax.experimental.pallas import tpu as pltpu
from jax.sharding import PartitionSpec as P

HDIM = 128
PIECES = 4
NONE_SEEN = -1e29
MASKED = -1e30


def dot(a, b):
    return lax.dot_general(a, b, (((1,), (0,)), ((), ())), preferred_element_type=jnp.float32)


def turned(block):
    return block.astype(jnp.float32).T.astype(jnp.bfloat16)


def schedule(heads, depth):
    if heads != 3 or depth != 8:
        return [(h, d) for d in range(1, depth + 1) for h in range(heads)]
    turns = [0, 1, 0, 2] * 3 + [0, 1] * 2 + [1, 2] * 3 + [2, 2]
    return [(h, turns[: i + 1].count(h)) for i, h in enumerate(turns)]


def kernel(
    nz,
    n_head,
    q_in,
    k_in,
    v_in,
    tq_in,
    tk_in,
    tv_in,
    w_in,
    lengths_in,
    order_in,
    out,
    lengths,
    order,
    stage,
    qbuf,
    kbuf,
    vbuf,
    wbuf,
    bounds,
    stats,
    acc,
    factors,
    own_o,
    own_stats,
    o_send,
    s_send,
    o_recv,
    s_recv,
    gbuf,
    total,
    stage_sem,
    ring_send,
    ring_recv,
    q_sem,
    w_sem,
    w_own_sem,
    o_sem,
    s_sem,
    g_send,
    g_recv,
):
    rows = q_in.shape[0]
    heads = q_in.shape[1] // HDIM
    half = rows // 2
    clips = lengths.shape[0]
    depth = nz // 2
    ncol = wbuf.shape[2]
    w_half = HDIM // 2
    scale = 1.0 / HDIM**0.5

    ctx = lax.axis_index("ctx")
    hd = lax.axis_index("head")
    core = lax.axis_index("dp")
    column = ctx // nz
    z = ctx % nz
    right = column * nz + (z + 1) % nz
    left = column * nz + (z + nz - 1) % nz
    partner = (ctx + nz) % (2 * nz)

    stages = [
        pltpu.make_async_copy(ref, stage.at[i], stage_sem.at[i])
        for i, ref in enumerate((k_in, tk_in, v_in, tv_in, q_in, tq_in))
    ]
    tables = [
        pltpu.make_async_copy(src, dst, stage_sem.at[6 + i])
        for i, (src, dst) in enumerate(((lengths_in, lengths), (order_in, order)))
    ]
    for copy in stages + tables:
        copy.start()
    own_w = pltpu.make_async_copy(
        w_in.at[:, :, pl.ds(pl.multiple_of(hd * ncol, 128), ncol)],
        wbuf.at[:, pl.ds(pl.multiple_of(hd * HDIM, HDIM), HDIM), :],
        w_own_sem,
    )
    own_w.start()

    barrier = pltpu.get_barrier_semaphore()
    for other in (right, left, partner):
        pl.semaphore_signal(barrier, inc=1, device_id={"ctx": other})
    for i in range(1, n_head):
        pl.semaphore_signal(barrier, inc=1, device_id={"head": (hd + i) % n_head})
    pl.semaphore_signal(barrier, inc=1, device_id={"dp": 1 - core})

    for copy in tables:
        copy.wait()
    ends = []
    running = jnp.int32(0)
    for c in range(clips):
        running = running + lengths[c]
        ends.append(running)
    lane = lax.broadcasted_iota(jnp.int32, (1, rows), 1)
    for slot, index in enumerate((ctx, partner)):
        anchor = jnp.where(
            lane < half,
            order[2 * index] * half + lane,
            order[2 * index + 1] * half + lane - half,
        )
        low = jnp.zeros_like(anchor)
        high = jnp.full_like(anchor, rows * nz * 2)
        for end in ends:
            low = jnp.where(end <= anchor, jnp.maximum(low, end), low)
            high = jnp.where(end > anchor, jnp.minimum(high, end), high)
        bounds[0:1, slot * rows : (slot + 1) * rows] = low
        bounds[1:2, slot * rows : (slot + 1) * rows] = high

    def ring_copy(h, hop, piece, side):
        source = (z + nz - hop) % nz if side == 0 else (z + hop) % nz
        step = h * depth + hop
        buf = kbuf if piece < 2 else vbuf
        size = buf.shape[2] // 2
        ref = buf.at[h, source, pl.ds((piece % 2) * size, size), :]
        return pltpu.make_async_remote_copy(
            src_ref=ref,
            dst_ref=ref,
            send_sem=ring_send.at[side, piece, h * 2 + hop % 2],
            recv_sem=ring_recv.at[side, piece, step],
            device_id={"ctx": right if side == 0 else left},
        )

    def send_own(h, pieces):
        for piece in pieces:
            for side in range(2):
                ring_copy(h, 0, piece, side).start()

    def q_copy(h):
        return pltpu.make_async_remote_copy(
            src_ref=qbuf.at[0, h],
            dst_ref=qbuf.at[1, h],
            send_sem=q_sem.at[0, h],
            recv_sem=q_sem.at[1, h],
            device_id={"ctx": partner},
        )

    def w_copy(i):
        other = (hd + i) % n_head
        return pltpu.make_async_remote_copy(
            src_ref=w_in.at[
                :,
                pl.ds(pl.multiple_of(core * w_half, w_half), w_half),
                pl.ds(pl.multiple_of(other * ncol, 128), ncol),
            ],
            dst_ref=wbuf.at[:, pl.ds(pl.multiple_of(hd * HDIM + core * w_half, w_half), w_half), :],
            send_sem=w_sem.at[0, i - 1],
            recv_sem=w_sem.at[1, i - 1],
            device_id={"head": other},
        )

    def w_share(i):
        source = (hd + n_head - i) % n_head
        ref = wbuf.at[:, pl.ds(pl.multiple_of(source * HDIM + core * w_half, w_half), w_half), :]
        return pltpu.make_async_remote_copy(
            src_ref=ref,
            dst_ref=ref,
            send_sem=w_sem.at[2, i - 1],
            recv_sem=w_sem.at[3, i - 1],
            device_id={"dp": 1 - core},
        )

    def o_copies(h):
        return [
            pltpu.make_async_remote_copy(
                src_ref=src.at[h],
                dst_ref=dst.at[h],
                send_sem=sem.at[0, h],
                recv_sem=sem.at[1, h],
                device_id={"ctx": partner},
            )
            for src, dst, sem in ((s_send, s_recv, s_sem), (o_send, o_recv, o_sem))
        ]

    def g_copy(h, i):
        return pltpu.make_async_remote_copy(
            src_ref=gbuf.at[h, hd],
            dst_ref=gbuf.at[h, hd],
            send_sem=g_send.at[h, i - 1],
            recv_sem=g_recv.at[h, i - 1],
            device_id={"head": (hd + i) % n_head},
        )

    columns = [slice(h * HDIM, (h + 1) * HDIM) for h in range(heads)]
    for copy in stages[:2]:
        copy.wait()
    for h, cols in enumerate(columns):
        kbuf[h, z, :, 0:HDIM] = stage[0, :, cols]
        kbuf[h, z, :, HDIM : 2 * HDIM] = stage[1, :, cols]
    pl.semaphore_wait(barrier, 3 + n_head)
    send_own(0, range(2))
    for copy in stages[2:4]:
        copy.wait()
    for h, cols in enumerate(columns):
        vbuf[h, z, 0:HDIM, :] = turned(stage[2, :, cols])
        vbuf[h, z, HDIM : 2 * HDIM, :] = turned(stage[3, :, cols])
    send_own(0, range(2, PIECES))
    for h in range(1, heads):
        send_own(h, range(PIECES))
    for copy in stages[4:]:
        copy.wait()
    for h, cols in enumerate(columns):
        qbuf[0, h, 0:HDIM, :] = turned(stage[5, :, cols])
        qbuf[0, h, HDIM : 2 * HDIM, :] = turned(stage[4, :, cols])
        q_copy(h).start()
    for i in range(1, n_head):
        w_copy(i).start()
    total[...] = jnp.zeros_like(total)
    s_send[...] = jnp.zeros_like(s_send)

    def allowed_keys(source):
        low, high = bounds[0:1, :], bounds[1:2, :]
        index = column * nz + source
        position = lax.broadcasted_iota(jnp.int32, (half, 2 * rows), 0)
        parts = []
        for part in range(2):
            first = order[2 * index + part] * half
            parts.append(jnp.logical_and(position >= low - first, position < high - first))
        return parts

    def score(h, sources):
        key = jnp.concatenate([kbuf[h, source] for source in sources], axis=0)
        query = jnp.concatenate([qbuf[0, h], qbuf[1, h]], axis=1)
        scores = dot(key[:, :HDIM], query[HDIM:]) * (scale * math.log2(math.e))
        tan_scores = dot(key, query)
        masks = [mask for source in sources for mask in allowed_keys(source)]
        masked = jnp.concatenate(
            [
                jnp.where(mask, scores[i * half : (i + 1) * half], MASKED)
                for i, mask in enumerate(masks)
            ],
            axis=0,
        )
        peak = stats[h, 0:1, :]
        new_peak = jnp.maximum(peak, jnp.max(masked, axis=0, keepdims=True))
        weights = jnp.exp2(masked - new_peak)
        rescale = jnp.exp2(peak - new_peak)
        products = weights * tan_scores
        stats[h, 0:1, :] = new_peak
        stats[h, 1:2, :] = rescale * stats[h, 1:2, :] + jnp.sum(weights, axis=0, keepdims=True)
        stats[h, 2:3, :] = rescale * stats[h, 2:3, :] + scale * jnp.sum(
            products, axis=0, keepdims=True
        )
        stats[h, 3:4, :] = rescale
        span = len(sources) * rows
        factors[0, 0:span] = weights.astype(jnp.bfloat16)
        factors[1, 0:span] = products.astype(jnp.bfloat16)

    def apply(h, sources):
        value = jnp.concatenate([vbuf[h, source] for source in sources], axis=1)
        span = len(sources) * rows
        both = dot(value, factors[0, 0:span])
        moved = dot(value[:HDIM], factors[1, 0:span])
        rescale = stats[h, 3:4, :]
        acc[h, 0:HDIM, :] = rescale * acc[h, 0:HDIM, :] + both[:HDIM]
        acc[h, HDIM:, :] = rescale * acc[h, HDIM:, :] + both[HDIM:] + scale * moved

    def finish(h):
        for slot in (1, 0):
            lanes = slice(slot * rows, (slot + 1) * rows)
            sums = stats[h, 1:2, lanes]
            inverse = jnp.where(sums > 0.0, 1.0 / jnp.where(sums > 0.0, sums, 1.0), 0.0)
            mean = stats[h, 2:3, lanes] * inverse
            primal = acc[h, 0:HDIM, lanes] * inverse
            tangent = acc[h, HDIM:, lanes] * inverse - mean * primal
            out_ref, stats_ref = ((own_o, own_stats), (o_send, s_send))[slot]
            out_ref[h, 0:HDIM, :] = primal.astype(out_ref.dtype)
            out_ref[h, HDIM:, :] = tangent.astype(out_ref.dtype)
            for i, row in enumerate((stats[h, 0:1, lanes], sums, mean)):
                stats_ref[h, i : i + 1, :] = row
            if slot == 1:
                for copy in o_copies(h):
                    copy.start()

    def merge(h):
        for copy in o_copies(h):
            copy.wait()
        peaks, sums, means = [], [], []
        for ref in (own_stats, s_recv):
            peaks.append(ref[h, 0:1, :])
            sums.append(ref[h, 1:2, :])
            means.append(ref[h, 2:3, :])
        peak = jnp.maximum(peaks[0], peaks[1])
        shares = [sums[i] * jnp.exp2(peaks[i] - peak) for i in range(2)]
        inverse = 1.0 / (shares[0] + shares[1])
        shares = [share * inverse for share in shares]
        mean = shares[0] * means[0] + shares[1] * means[1]
        primals = [own_o[h, 0:HDIM, :], o_recv[h, 0:HDIM, :].astype(jnp.float32)]
        tangents = [own_o[h, HDIM:, :], o_recv[h, HDIM:, :].astype(jnp.float32)]
        primal = shares[0] * primals[0] + shares[1] * primals[1]
        tangent = sum(
            shares[i] * (tangents[i] + (means[i] - mean) * primals[i]) for i in range(2)
        )
        gbuf[h, hd, 0:rows, :] = primal.T.astype(jnp.bfloat16)
        gbuf[h, hd, rows:, :] = tangent.T.astype(jnp.bfloat16)
        for i in range(1, n_head):
            g_copy(h, i).start()

    def project(h):
        for first in range(0, n_head, 2):
            sources = [(hd + n_head - i) % n_head for i in (first, first + 1)]
            for i in (first, first + 1):
                if i > 0:
                    g_copy(h, i).wait()
            features = jnp.concatenate([gbuf[h, source] for source in sources], axis=1)
            weight = jnp.concatenate(
                [
                    wbuf[h, pl.ds(pl.multiple_of(source * HDIM, HDIM), HDIM), :]
                    for source in sources
                ],
                axis=0,
            )
            total[...] += dot(features, weight)

    order_of = schedule(heads, depth)
    steps = len(order_of)
    finished = [order_of.index((h, depth)) for h in range(heads)]

    def place(index):
        h = d = 0
        for i, (head_at, hop_at) in enumerate(order_of):
            h = h + jnp.where(index == i, head_at, 0)
            d = d + jnp.where(index == i, hop_at, 0)
        return h, d

    def each_piece(d, act):
        for piece in range(PIECES):
            for side in range(2):
                crosses = (piece < 2) == (side == 0)
                if crosses:
                    act(piece, side, d < depth)
                else:
                    pl.when(d < depth)(functools.partial(act, piece, side, d < depth - 1))

    def step(index, carry):
        h, d = place(index)
        far, near = [(z + nz - d) % nz], [(z + nz - d) % nz, (z + d) % nz]

        def forward(piece, side, goes_on):
            ring_copy(h, d - 1, piece, side).wait_recv()

            @pl.when(goes_on)
            def _():
                ring_copy(h, d, piece, side).start()

        def settle(piece, side, goes_on):
            ring_copy(h, d - 1, piece, side).wait_send()

        each_piece(d, forward)

        @pl.when(d == 1)
        def _():
            stats[h, 0:1, :] = jnp.full((1, 2 * rows), NONE_SEEN, jnp.float32)
            stats[h, 1:3, :] = jnp.zeros((2, 2 * rows), jnp.float32)
            acc[h] = jnp.zeros((2 * HDIM, 2 * rows), jnp.float32)
            q_copy(h).wait()
            score(h, [z])
            apply(h, [z])

        @pl.when(d < depth)
        def _():
            score(h, near)
            apply(h, near)

        @pl.when(d == depth)
        def _():
            score(h, far)
            apply(h, far)
            finish(h)

        each_piece(d, settle)

        @pl.when(index == min(finished[0] + 2, steps - 1))
        def _():
            for i in range(1, n_head):
                w_copy(i).wait()
                w_share(i).start()

        for early in range(heads - 1):

            @pl.when(index == min(finished[early] + 1, steps - 1))
            def _(early=early):
                merge(early)

        return carry

    lax.fori_loop(0, steps, step, 0)
    own_w.wait()
    for i in range(1, n_head):
        w_share(i).wait()
    project(0)
    merge(heads - 1)
    for h in range(1, heads):
        project(h)
    out[...] = total[...].astype(out.dtype)


def local(
    queries,
    keys,
    values,
    tan_queries,
    tan_keys,
    tan_values,
    out_weight,
    clip_lengths,
    stretch_order,
):
    rows, width = queries.shape
    heads = width // HDIM
    n_head = lax.axis_size("head")
    nz = lax.axis_size("ctx") // 2
    depth = nz // 2
    ncol = out_weight.shape[1] // n_head
    bf16, f32 = jnp.bfloat16, jnp.float32
    weight = out_weight.reshape(heads, HDIM, out_weight.shape[1])
    dma = pltpu.SemaphoreType.DMA
    anywhere = pl.BlockSpec(memory_space=pl.ANY)
    in_vmem = pl.BlockSpec(memory_space=pltpu.VMEM)
    both = pl.pallas_call(
        functools.partial(kernel, nz, n_head),
        out_shape=pltpu.VMEM((2 * rows, ncol), bf16),
        in_specs=[anywhere] * 9,
        out_specs=in_vmem,
        scratch_shapes=[
            pltpu.SMEM(clip_lengths.shape, jnp.int32),
            pltpu.SMEM(stretch_order.shape, jnp.int32),
            pltpu.VMEM((6, rows, width), bf16),
            pltpu.VMEM((2, heads, 2 * HDIM, rows), bf16),
            pltpu.VMEM((heads, nz, rows, 2 * HDIM), bf16),
            pltpu.VMEM((heads, nz, 2 * HDIM, rows), bf16),
            pltpu.VMEM((heads, n_head * HDIM, ncol), bf16),
            pltpu.VMEM((8, 2 * rows), jnp.int32),
            pltpu.VMEM((heads, 8, 2 * rows), f32),
            pltpu.VMEM((heads, 2 * HDIM, 2 * rows), f32),
            pltpu.VMEM((2, 2 * rows, 2 * rows), bf16),
            pltpu.VMEM((heads, 2 * HDIM, rows), f32),
            pltpu.VMEM((heads, 8, rows), f32),
            pltpu.VMEM((heads, 2 * HDIM, rows), bf16),
            pltpu.VMEM((heads, 8, rows), f32),
            pltpu.VMEM((heads, 2 * HDIM, rows), bf16),
            pltpu.VMEM((heads, 8, rows), f32),
            pltpu.VMEM((heads, n_head, 2 * rows, HDIM), bf16),
            pltpu.VMEM((2 * rows, ncol), f32),
            dma((8,)),
            dma((2, PIECES, 2 * heads)),
            dma((2, PIECES, heads * depth)),
            dma((2, heads)),
            dma((4, n_head - 1)),
            dma,
            dma((2, heads)),
            dma((2, heads)),
            dma((heads, n_head - 1)),
            dma((heads, n_head - 1)),
        ],
        compiler_params=pltpu.CompilerParams(
            collective_id=0,
            has_side_effects=True,
            vmem_limit_bytes=60 * 1024 * 1024,
        ),
        cost_estimate=pl.CostEstimate(
            flops=2 * 6 * 2 * rows * nz * rows * width + 4 * rows * n_head * width * ncol,
            bytes_accessed=8 * 1024 * 1024,
            transcendentals=2 * rows * nz * rows * heads,
        ),
    )(
        queries,
        keys,
        values,
        tan_queries,
        tan_keys,
        tan_values,
        weight,
        clip_lengths,
        stretch_order,
    )
    return both[:rows], both[rows:]


def solution(mesh):
    placed = P(("dp", "ctx"), "head")
    return jax.shard_map(
        local,
        mesh=mesh,
        in_specs=(placed,) * 6 + (P("head", None), P("dp"), P("dp")),
        out_specs=(placed, placed),
        check_vma=False,
    )
```

```python
import functools
import math

import jax
import jax.numpy as jnp
from jax import lax
from jax.experimental import pallas as pl
from jax.experimental.pallas import tpu as pltpu
from jax.sharding import PartitionSpec as P

HDIM = 128
PIECES = 4
NONE_SEEN = -1e29
MASKED = -1e30


def dot(a, b):
    return lax.dot_general(a, b, (((1,), (0,)), ((), ())), preferred_element_type=jnp.float32)


def turned(block):
    return block.astype(jnp.float32).T.astype(jnp.bfloat16)


def schedule(heads, depth):
    if heads != 3 or depth != 8:
        return [(h, d) for d in range(1, depth + 1) for h in range(heads)]
    turns = [0, 1, 0, 2] * 3 + [0, 1] * 2 + [1, 2] * 3 + [2, 2]
    return [(h, turns[: i + 1].count(h)) for i, h in enumerate(turns)]


def kernel(
    nz,
    n_head,
    q_in,
    k_in,
    v_in,
    tq_in,
    tk_in,
    tv_in,
    w_in,
    lengths_in,
    order_in,
    out,
    lengths,
    order,
    stage,
    qbuf,
    kbuf,
    vbuf,
    wbuf,
    bounds,
    stats,
    acc,
    factors,
    own_o,
    own_stats,
    o_send,
    s_send,
    o_recv,
    s_recv,
    gbuf,
    total,
    stage_sem,
    ring_send,
    ring_recv,
    q_sem,
    w_sem,
    w_own_sem,
    o_sem,
    s_sem,
    g_send,
    g_recv,
):
    rows = q_in.shape[0]
    heads = q_in.shape[1] // HDIM
    half = rows // 2
    clips = lengths.shape[0]
    depth = nz // 2
    ncol = wbuf.shape[2]
    w_half = HDIM // 2
    scale = 1.0 / HDIM**0.5

    ctx = lax.axis_index("ctx")
    hd = lax.axis_index("head")
    core = lax.axis_index("dp")
    column = ctx // nz
    z = ctx % nz
    right = column * nz + (z + 1) % nz
    left = column * nz + (z + nz - 1) % nz
    partner = (ctx + nz) % (2 * nz)

    stages = [
        pltpu.make_async_copy(ref, stage.at[i], stage_sem.at[i])
        for i, ref in enumerate((k_in, tk_in, v_in, tv_in, q_in, tq_in))
    ]
    tables = [
        pltpu.make_async_copy(src, dst, stage_sem.at[6 + i])
        for i, (src, dst) in enumerate(((lengths_in, lengths), (order_in, order)))
    ]
    for copy in stages + tables:
        copy.start()
    own_w = pltpu.make_async_copy(
        w_in.at[:, :, pl.ds(pl.multiple_of(hd * ncol, 128), ncol)],
        wbuf.at[:, pl.ds(pl.multiple_of(hd * HDIM, HDIM), HDIM), :],
        w_own_sem,
    )
    own_w.start()

    barrier = pltpu.get_barrier_semaphore()
    for other in (right, left, partner):
        pl.semaphore_signal(barrier, inc=1, device_id={"ctx": other})
    for i in range(1, n_head):
        pl.semaphore_signal(barrier, inc=1, device_id={"head": (hd + i) % n_head})
    pl.semaphore_signal(barrier, inc=1, device_id={"dp": 1 - core})

    def ring_copy(h, hop, piece, side):
        source = (z + nz - hop) % nz if side == 0 else (z + hop) % nz
        step = h * depth + hop
        buf = kbuf if piece < 2 else vbuf
        size = buf.shape[2] // 2
        ref = buf.at[h, source, pl.ds((piece % 2) * size, size), :]
        return pltpu.make_async_remote_copy(
            src_ref=ref,
            dst_ref=ref,
            send_sem=ring_send.at[side, piece, h * 2 + hop % 2],
            recv_sem=ring_recv.at[side, piece, step],
            device_id={"ctx": right if side == 0 else left},
        )

    def send_own(h, pieces):
        for piece in pieces:
            for side in range(2):
                ring_copy(h, 0, piece, side).start()

    def q_copy(h):
        return pltpu.make_async_remote_copy(
            src_ref=qbuf.at[0, h],
            dst_ref=qbuf.at[1, h],
            send_sem=q_sem.at[0, h],
            recv_sem=q_sem.at[1, h],
            device_id={"ctx": partner},
        )

    def w_copy(i):
        other = (hd + i) % n_head
        return pltpu.make_async_remote_copy(
            src_ref=w_in.at[
                :,
                pl.ds(pl.multiple_of(core * w_half, w_half), w_half),
                pl.ds(pl.multiple_of(other * ncol, 128), ncol),
            ],
            dst_ref=wbuf.at[:, pl.ds(pl.multiple_of(hd * HDIM + core * w_half, w_half), w_half), :],
            send_sem=w_sem.at[0, i - 1],
            recv_sem=w_sem.at[1, i - 1],
            device_id={"head": other},
        )

    def w_share(i):
        source = (hd + n_head - i) % n_head
        ref = wbuf.at[:, pl.ds(pl.multiple_of(source * HDIM + core * w_half, w_half), w_half), :]
        return pltpu.make_async_remote_copy(
            src_ref=ref,
            dst_ref=ref,
            send_sem=w_sem.at[2, i - 1],
            recv_sem=w_sem.at[3, i - 1],
            device_id={"dp": 1 - core},
        )

    def o_copies(h):
        return [
            pltpu.make_async_remote_copy(
                src_ref=src.at[h],
                dst_ref=dst.at[h],
                send_sem=sem.at[0, h],
                recv_sem=sem.at[1, h],
                device_id={"ctx": partner},
            )
            for src, dst, sem in ((s_send, s_recv, s_sem), (o_send, o_recv, o_sem))
        ]

    n_y = n_head // 2
    y, x = hd // 2, hd % 2
    relayed = n_head // 2 + 1 if n_y == 4 else 0
    direct = [k for k in range(1, n_head) if k != relayed]
    direct.sort(key=lambda k: -min(k // 2, n_y - k // 2))

    def target(k):
        return (y + k // 2) % n_y * 2 + (x + k) % 2

    def source(k):
        return (y + n_y - k // 2) % n_y * 2 + (x + k) % 2

    def g_copy(h, k):
        block = hd if k != relayed else source(relayed - 1)
        return pltpu.make_async_remote_copy(
            src_ref=gbuf.at[h, block],
            dst_ref=gbuf.at[h, block],
            send_sem=g_send.at[h, k - 1],
            recv_sem=g_recv.at[h, k - 1],
            device_id={"head": target(k if k != relayed else 1)},
        )

    def relay(h):
        if relayed:
            g_copy(h, relayed - 1).wait()
            g_copy(h, relayed).start()

    columns = [slice(h * HDIM, (h + 1) * HDIM) for h in range(heads)]
    for copy in stages[:2]:
        copy.wait()
    for h, cols in enumerate(columns):
        kbuf[h, z, :, 0:HDIM] = stage[0, :, cols]
        kbuf[h, z, :, HDIM : 2 * HDIM] = stage[1, :, cols]
    pl.semaphore_wait(barrier, 3 + n_head)
    send_own(0, range(2))
    for copy in stages[2:4]:
        copy.wait()
    for h, cols in enumerate(columns):
        vbuf[h, z, 0:HDIM, :] = turned(stage[2, :, cols])
        vbuf[h, z, HDIM : 2 * HDIM, :] = turned(stage[3, :, cols])
    send_own(0, range(2, PIECES))
    for h in range(1, heads):
        send_own(h, range(PIECES))
    for copy in stages[4:]:
        copy.wait()
    for h, cols in enumerate(columns):
        qbuf[0, h, 0:HDIM, :] = turned(stage[5, :, cols])
        qbuf[0, h, HDIM : 2 * HDIM, :] = turned(stage[4, :, cols])
        q_copy(h).start()
    for i in range(1, n_head):
        w_copy(i).start()
    for copy in tables:
        copy.wait()
    ends = []
    running = jnp.int32(0)
    for c in range(clips):
        running = running + lengths[c]
        ends.append(running)
    lane = lax.broadcasted_iota(jnp.int32, (1, rows), 1)
    for slot, index in enumerate((ctx, partner)):
        anchor = jnp.where(
            lane < half,
            order[2 * index] * half + lane,
            order[2 * index + 1] * half + lane - half,
        )
        low = jnp.zeros_like(anchor)
        high = jnp.full_like(anchor, rows * nz * 2)
        for end in ends:
            low = jnp.where(end <= anchor, jnp.maximum(low, end), low)
            high = jnp.where(end > anchor, jnp.minimum(high, end), high)
        bounds[0:1, slot * rows : (slot + 1) * rows] = low
        bounds[1:2, slot * rows : (slot + 1) * rows] = high

    total[...] = jnp.zeros_like(total)
    s_send[...] = jnp.zeros_like(s_send)

    def allowed_keys(source):
        low, high = bounds[0:1, :], bounds[1:2, :]
        index = column * nz + source
        position = lax.broadcasted_iota(jnp.int32, (half, 2 * rows), 0)
        parts = []
        for part in range(2):
            first = order[2 * index + part] * half
            parts.append(jnp.logical_and(position >= low - first, position < high - first))
        return parts

    def score(h, sources):
        key = jnp.concatenate([kbuf[h, source] for source in sources], axis=0)
        query = jnp.concatenate([qbuf[0, h], qbuf[1, h]], axis=1)
        scores = dot(key[:, :HDIM], query[HDIM:]) * (scale * math.log2(math.e))
        tan_scores = dot(key, query)
        masks = [mask for source in sources for mask in allowed_keys(source)]
        masked = jnp.concatenate(
            [
                jnp.where(mask, scores[i * half : (i + 1) * half], MASKED)
                for i, mask in enumerate(masks)
            ],
            axis=0,
        )
        peak = stats[h, 0:1, :]
        new_peak = jnp.maximum(peak, jnp.max(masked, axis=0, keepdims=True))
        weights = jnp.exp2(masked - new_peak)
        rescale = jnp.exp2(peak - new_peak)
        products = weights * tan_scores
        stats[h, 0:1, :] = new_peak
        stats[h, 1:2, :] = rescale * stats[h, 1:2, :] + jnp.sum(weights, axis=0, keepdims=True)
        stats[h, 2:3, :] = rescale * stats[h, 2:3, :] + scale * jnp.sum(
            products, axis=0, keepdims=True
        )
        stats[h, 3:4, :] = rescale
        span = len(sources) * rows
        factors[0, 0:span] = weights.astype(jnp.bfloat16)
        factors[1, 0:span] = products.astype(jnp.bfloat16)

    def apply(h, sources):
        value = jnp.concatenate([vbuf[h, source] for source in sources], axis=1)
        span = len(sources) * rows
        both = dot(value, factors[0, 0:span])
        moved = dot(value[:HDIM], factors[1, 0:span])
        rescale = stats[h, 3:4, :]
        acc[h, 0:HDIM, :] = rescale * acc[h, 0:HDIM, :] + both[:HDIM]
        acc[h, HDIM:, :] = rescale * acc[h, HDIM:, :] + both[HDIM:] + scale * moved

    def finish(h):
        for slot in (1, 0):
            lanes = slice(slot * rows, (slot + 1) * rows)
            sums = stats[h, 1:2, lanes]
            inverse = jnp.where(sums > 0.0, 1.0 / jnp.where(sums > 0.0, sums, 1.0), 0.0)
            mean = stats[h, 2:3, lanes] * inverse
            primal = acc[h, 0:HDIM, lanes] * inverse
            tangent = acc[h, HDIM:, lanes] * inverse - mean * primal
            out_ref, stats_ref = ((own_o, own_stats), (o_send, s_send))[slot]
            out_ref[h, 0:HDIM, :] = primal.astype(out_ref.dtype)
            out_ref[h, HDIM:, :] = tangent.astype(out_ref.dtype)
            for i, row in enumerate((stats[h, 0:1, lanes], sums, mean)):
                stats_ref[h, i : i + 1, :] = row
            if slot == 1:
                for copy in o_copies(h):
                    copy.start()

    def merge(h):
        for copy in o_copies(h):
            copy.wait()
        peaks, sums, means = [], [], []
        for ref in (own_stats, s_recv):
            peaks.append(ref[h, 0:1, :])
            sums.append(ref[h, 1:2, :])
            means.append(ref[h, 2:3, :])
        peak = jnp.maximum(peaks[0], peaks[1])
        shares = [sums[i] * jnp.exp2(peaks[i] - peak) for i in range(2)]
        inverse = 1.0 / (shares[0] + shares[1])
        shares = [share * inverse for share in shares]
        mean = shares[0] * means[0] + shares[1] * means[1]
        primals = [own_o[h, 0:HDIM, :], o_recv[h, 0:HDIM, :].astype(jnp.float32)]
        tangents = [own_o[h, HDIM:, :], o_recv[h, HDIM:, :].astype(jnp.float32)]
        primal = shares[0] * primals[0] + shares[1] * primals[1]
        tangent = sum(
            shares[i] * (tangents[i] + (means[i] - mean) * primals[i]) for i in range(2)
        )
        gbuf[h, hd, 0:rows, :] = primal.T.astype(jnp.bfloat16)
        gbuf[h, hd, rows:, :] = tangent.T.astype(jnp.bfloat16)
        for k in direct:
            g_copy(h, k).start()

    def project(h):
        arrivals = [0] + direct[::-1] + ([relayed] if relayed else [])
        for first in range(0, n_head, 2):
            pair = arrivals[first : first + 2]
            for k in pair:
                if k > 0 and k != relayed - 1:
                    g_copy(h, k).wait()
            sources = [source(k) for k in pair]
            features = jnp.concatenate([gbuf[h, g] for g in sources], axis=1)
            weight = jnp.concatenate(
                [wbuf[h, pl.ds(pl.multiple_of(g * HDIM, HDIM), HDIM), :] for g in sources],
                axis=0,
            )
            total[...] += dot(features, weight)

    order_of = schedule(heads, depth)
    steps = len(order_of)
    finished = [order_of.index((h, depth)) for h in range(heads)]

    def place(index):
        h = d = 0
        for i, (head_at, hop_at) in enumerate(order_of):
            h = h + jnp.where(index == i, head_at, 0)
            d = d + jnp.where(index == i, hop_at, 0)
        return h, d

    def forward(h, d, piece):
        for side in range(2):
            crosses = (piece < 2) == (side == 0)

            def take(side=side, crosses=crosses):
                arrived = ring_copy(h, d - 1, piece, side)
                arrived.wait_recv()

                @pl.when(d < depth if crosses else d < depth - 1)
                def _():
                    ring_copy(h, d, piece, side).start()

                arrived.wait_send()

            if crosses:
                take()
            else:
                pl.when(d < depth)(take)

    def step(index, carry):
        h, d = place(index)
        old_h, old_d = carry
        far, near = [(z + nz - old_d) % nz], [(z + nz - old_d) % nz, (z + old_d) % nz]
        live = index < steps

        @pl.when(live)
        def _():
            forward(h, d, 0)

        @pl.when(index > 0)
        def _():
            @pl.when(old_d == 1)
            def _():
                stats[old_h, 0:1, :] = jnp.full((1, 2 * rows), NONE_SEEN, jnp.float32)
                stats[old_h, 1:3, :] = jnp.zeros((2, 2 * rows), jnp.float32)
                acc[old_h] = jnp.zeros((2 * HDIM, 2 * rows), jnp.float32)
                q_copy(old_h).wait()
                score(old_h, [z])
                apply(old_h, [z])

            @pl.when(old_d < depth)
            def _():
                score(old_h, near)

            @pl.when(old_d == depth)
            def _():
                score(old_h, far)

        @pl.when(live)
        def _():
            forward(h, d, 1)

        @pl.when(index > 0)
        def _():
            @pl.when(old_d < depth)
            def _():
                apply(old_h, near)

            @pl.when(old_d == depth)
            def _():
                apply(old_h, far)
                finish(old_h)

        @pl.when(live)
        def _():
            for piece in range(2, PIECES):
                forward(h, d, piece)

        @pl.when(index == min(finished[0] + 2, steps))
        def _():
            for i in range(1, n_head):
                w_copy(i).wait()
                w_share(i).start()

        for early in range(heads - 1):

            @pl.when(index == min(finished[early] + 2, steps))
            def _(early=early):
                merge(early)

        @pl.when(index == min(finished[0] + 5, steps))
        def _():
            relay(0)

        return h, d

    lax.fori_loop(0, steps + 1, step, (jnp.int32(0), jnp.int32(1)))
    own_w.wait()
    for i in range(1, n_head):
        w_share(i).wait()
    for h in range(1, heads - 1):
        relay(h)
    project(0)
    merge(heads - 1)
    relay(heads - 1)
    for h in range(1, heads):
        project(h)
    out[...] = total[...].astype(out.dtype)


def local(
    queries,
    keys,
    values,
    tan_queries,
    tan_keys,
    tan_values,
    out_weight,
    clip_lengths,
    stretch_order,
):
    rows, width = queries.shape
    heads = width // HDIM
    n_head = lax.axis_size("head")
    nz = lax.axis_size("ctx") // 2
    depth = nz // 2
    ncol = out_weight.shape[1] // n_head
    bf16, f32 = jnp.bfloat16, jnp.float32
    weight = out_weight.reshape(heads, HDIM, out_weight.shape[1])
    dma = pltpu.SemaphoreType.DMA
    anywhere = pl.BlockSpec(memory_space=pl.ANY)
    in_vmem = pl.BlockSpec(memory_space=pltpu.VMEM)
    both = pl.pallas_call(
        functools.partial(kernel, nz, n_head),
        out_shape=pltpu.VMEM((2 * rows, ncol), bf16),
        in_specs=[anywhere] * 9,
        out_specs=in_vmem,
        scratch_shapes=[
            pltpu.SMEM(clip_lengths.shape, jnp.int32),
            pltpu.SMEM(stretch_order.shape, jnp.int32),
            pltpu.VMEM((6, rows, width), bf16),
            pltpu.VMEM((2, heads, 2 * HDIM, rows), bf16),
            pltpu.VMEM((heads, nz, rows, 2 * HDIM), bf16),
            pltpu.VMEM((heads, nz, 2 * HDIM, rows), bf16),
            pltpu.VMEM((heads, n_head * HDIM, ncol), bf16),
            pltpu.VMEM((8, 2 * rows), jnp.int32),
            pltpu.VMEM((heads, 8, 2 * rows), f32),
            pltpu.VMEM((heads, 2 * HDIM, 2 * rows), f32),
            pltpu.VMEM((2, 2 * rows, 2 * rows), bf16),
            pltpu.VMEM((heads, 2 * HDIM, rows), f32),
            pltpu.VMEM((heads, 8, rows), f32),
            pltpu.VMEM((heads, 2 * HDIM, rows), bf16),
            pltpu.VMEM((heads, 8, rows), f32),
            pltpu.VMEM((heads, 2 * HDIM, rows), bf16),
            pltpu.VMEM((heads, 8, rows), f32),
            pltpu.VMEM((heads, n_head, 2 * rows, HDIM), bf16),
            pltpu.VMEM((2 * rows, ncol), f32),
            dma((8,)),
            dma((2, PIECES, 2 * heads)),
            dma((2, PIECES, heads * depth)),
            dma((2, heads)),
            dma((4, n_head - 1)),
            dma,
            dma((2, heads)),
            dma((2, heads)),
            dma((heads, n_head - 1)),
            dma((heads, n_head - 1)),
        ],
        compiler_params=pltpu.CompilerParams(
            collective_id=0,
            has_side_effects=True,
            vmem_limit_bytes=60 * 1024 * 1024,
        ),
        cost_estimate=pl.CostEstimate(
            flops=2 * 6 * 2 * rows * nz * rows * width + 4 * rows * n_head * width * ncol,
            bytes_accessed=8 * 1024 * 1024,
            transcendentals=2 * rows * nz * rows * heads,
        ),
    )(
        queries,
        keys,
        values,
        tan_queries,
        tan_keys,
        tan_values,
        weight,
        clip_lengths,
        stretch_order,
    )
    return both[:rows], both[rows:]


def solution(mesh):
    placed = P(("dp", "ctx"), "head")
    return jax.shard_map(
        local,
        mesh=mesh,
        in_specs=(placed,) * 6 + (P("head", None), P("dp"), P("dp")),
        out_specs=(placed, placed),
        check_vma=False,
    )
```

```python
import functools
import math

import jax
import jax.numpy as jnp
from jax import lax
from jax.experimental import pallas as pl
from jax.experimental.pallas import tpu as pltpu
from jax.sharding import PartitionSpec as P

HDIM = 128
PIECES = 4
NONE_SEEN = -1e29
MASKED = -1e30


def dot(a, b):
    return lax.dot_general(a, b, (((1,), (0,)), ((), ())), preferred_element_type=jnp.float32)


def turned(block):
    return block.astype(jnp.float32).T.astype(jnp.bfloat16)


def schedule(heads, depth):
    if heads != 3 or depth != 8:
        return [(h, d) for d in range(1, depth + 1) for h in range(heads)]
    turns = [0, 1, 0, 2] * 3 + [0, 1] * 2 + [1, 2] * 3 + [2, 2]
    return [(h, turns[: i + 1].count(h)) for i, h in enumerate(turns)]


def kernel(
    nz,
    n_head,
    q_in,
    k_in,
    v_in,
    tq_in,
    tk_in,
    tv_in,
    w_in,
    lengths_in,
    order_in,
    out,
    lengths,
    order,
    stage,
    qbuf,
    kbuf,
    vbuf,
    wbuf,
    bounds,
    stats,
    acc,
    factors,
    own_o,
    own_stats,
    o_send,
    s_send,
    o_recv,
    s_recv,
    gbuf,
    total,
    stage_sem,
    ring_send,
    ring_recv,
    q_sem,
    w_sem,
    w_own_sem,
    o_sem,
    s_sem,
    g_send,
    g_recv,
):
    rows = q_in.shape[0]
    heads = q_in.shape[1] // HDIM
    half = rows // 2
    clips = lengths.shape[0]
    depth = nz // 2
    ncol = wbuf.shape[2]
    w_half = HDIM // 2
    scale = 1.0 / HDIM**0.5

    ctx = lax.axis_index("ctx")
    hd = lax.axis_index("head")
    core = lax.axis_index("dp")
    column = ctx // nz
    z = ctx % nz
    right = column * nz + (z + 1) % nz
    left = column * nz + (z + nz - 1) % nz
    partner = (ctx + nz) % (2 * nz)

    stages = [
        pltpu.make_async_copy(ref, stage.at[i], stage_sem.at[i])
        for i, ref in enumerate((k_in, tk_in, v_in, tv_in, q_in, tq_in))
    ]
    tables = [
        pltpu.make_async_copy(src, dst, stage_sem.at[6 + i])
        for i, (src, dst) in enumerate(((lengths_in, lengths), (order_in, order)))
    ]
    for copy in stages + tables:
        copy.start()
    own_w = pltpu.make_async_copy(
        w_in.at[:, :, pl.ds(pl.multiple_of(hd * ncol, 128), ncol)],
        wbuf.at[:, pl.ds(pl.multiple_of(hd * HDIM, HDIM), HDIM), :],
        w_own_sem,
    )
    own_w.start()

    barrier = pltpu.get_barrier_semaphore()
    for other in (right, left, partner):
        pl.semaphore_signal(barrier, inc=1, device_id={"ctx": other})
    for i in range(1, n_head):
        pl.semaphore_signal(barrier, inc=1, device_id={"head": (hd + i) % n_head})
    pl.semaphore_signal(barrier, inc=1, device_id={"dp": 1 - core})

    for copy in tables:
        copy.wait()
    ends = []
    running = jnp.int32(0)
    for c in range(clips):
        running = running + lengths[c]
        ends.append(running)
    lane = lax.broadcasted_iota(jnp.int32, (1, rows), 1)
    for slot, index in enumerate((ctx, partner)):
        anchor = jnp.where(
            lane < half,
            order[2 * index] * half + lane,
            order[2 * index + 1] * half + lane - half,
        )
        low = jnp.zeros_like(anchor)
        high = jnp.full_like(anchor, rows * nz * 2)
        for end in ends:
            low = jnp.where(end <= anchor, jnp.maximum(low, end), low)
            high = jnp.where(end > anchor, jnp.minimum(high, end), high)
        bounds[0:1, slot * rows : (slot + 1) * rows] = low
        bounds[1:2, slot * rows : (slot + 1) * rows] = high

    def ring_copy(h, hop, piece, side):
        source = (z + nz - hop) % nz if side == 0 else (z + hop) % nz
        step = h * depth + hop
        buf = kbuf if piece < 2 else vbuf
        size = buf.shape[2] // 2
        ref = buf.at[h, source, pl.ds((piece % 2) * size, size), :]
        return pltpu.make_async_remote_copy(
            src_ref=ref,
            dst_ref=ref,
            send_sem=ring_send.at[side, piece, h * 2 + hop % 2],
            recv_sem=ring_recv.at[side, piece, step],
            device_id={"ctx": right if side == 0 else left},
        )

    def send_own(h, pieces):
        for piece in pieces:
            for side in range(2):
                ring_copy(h, 0, piece, side).start()

    def q_copy(h):
        return pltpu.make_async_remote_copy(
            src_ref=qbuf.at[0, h],
            dst_ref=qbuf.at[1, h],
            send_sem=q_sem.at[0, h],
            recv_sem=q_sem.at[1, h],
            device_id={"ctx": partner},
        )

    def w_copy(i):
        other = (hd + i) % n_head
        return pltpu.make_async_remote_copy(
            src_ref=w_in.at[
                :,
                pl.ds(pl.multiple_of(core * w_half, w_half), w_half),
                pl.ds(pl.multiple_of(other * ncol, 128), ncol),
            ],
            dst_ref=wbuf.at[:, pl.ds(pl.multiple_of(hd * HDIM + core * w_half, w_half), w_half), :],
            send_sem=w_sem.at[0, i - 1],
            recv_sem=w_sem.at[1, i - 1],
            device_id={"head": other},
        )

    def w_share(i):
        source = (hd + n_head - i) % n_head
        ref = wbuf.at[:, pl.ds(pl.multiple_of(source * HDIM + core * w_half, w_half), w_half), :]
        return pltpu.make_async_remote_copy(
            src_ref=ref,
            dst_ref=ref,
            send_sem=w_sem.at[2, i - 1],
            recv_sem=w_sem.at[3, i - 1],
            device_id={"dp": 1 - core},
        )

    def o_copies(h):
        return [
            pltpu.make_async_remote_copy(
                src_ref=src.at[h],
                dst_ref=dst.at[h],
                send_sem=sem.at[0, h],
                recv_sem=sem.at[1, h],
                device_id={"ctx": partner},
            )
            for src, dst, sem in ((s_send, s_recv, s_sem), (o_send, o_recv, o_sem))
        ]

    def g_copy(h, i):
        return pltpu.make_async_remote_copy(
            src_ref=gbuf.at[h, hd],
            dst_ref=gbuf.at[h, hd],
            send_sem=g_send.at[h, i - 1],
            recv_sem=g_recv.at[h, i - 1],
            device_id={"head": (hd + i) % n_head},
        )

    columns = [slice(h * HDIM, (h + 1) * HDIM) for h in range(heads)]
    for copy in stages[:2]:
        copy.wait()
    for h, cols in enumerate(columns):
        kbuf[h, z, :, 0:HDIM] = stage[0, :, cols]
        kbuf[h, z, :, HDIM : 2 * HDIM] = stage[1, :, cols]
    pl.semaphore_wait(barrier, 3 + n_head)
    send_own(0, range(2))
    for copy in stages[2:4]:
        copy.wait()
    for h, cols in enumerate(columns):
        vbuf[h, z, 0:HDIM, :] = turned(stage[2, :, cols])
        vbuf[h, z, HDIM : 2 * HDIM, :] = turned(stage[3, :, cols])
    send_own(0, range(2, PIECES))

    @pl.when(core == 0)
    def _():
        for h in range(1, heads):
            send_own(h, range(PIECES))

    for copy in stages[4:]:
        copy.wait()
    for h, cols in enumerate(columns):
        qbuf[0, h, 0:HDIM, :] = turned(stage[5, :, cols])
        qbuf[0, h, HDIM : 2 * HDIM, :] = turned(stage[4, :, cols])
        q_copy(h).start()
    for i in range(1, n_head):
        w_copy(i).start()
    total[...] = jnp.zeros_like(total)
    s_send[...] = jnp.zeros_like(s_send)

    def allowed_keys(source):
        low, high = bounds[0:1, :], bounds[1:2, :]
        index = column * nz + source
        position = lax.broadcasted_iota(jnp.int32, (half, 2 * rows), 0)
        parts = []
        for part in range(2):
            first = order[2 * index + part] * half
            parts.append(jnp.logical_and(position >= low - first, position < high - first))
        return parts

    def score(h, sources):
        key = jnp.concatenate([kbuf[h, source] for source in sources], axis=0)
        query = jnp.concatenate([qbuf[0, h], qbuf[1, h]], axis=1)
        scores = dot(key[:, :HDIM], query[HDIM:]) * (scale * math.log2(math.e))
        tan_scores = dot(key, query)
        masks = [mask for source in sources for mask in allowed_keys(source)]
        masked = jnp.concatenate(
            [
                jnp.where(mask, scores[i * half : (i + 1) * half], MASKED)
                for i, mask in enumerate(masks)
            ],
            axis=0,
        )
        peak = stats[h, 0:1, :]
        new_peak = jnp.maximum(peak, jnp.max(masked, axis=0, keepdims=True))
        weights = jnp.exp2(masked - new_peak)
        rescale = jnp.exp2(peak - new_peak)
        products = weights * tan_scores
        stats[h, 0:1, :] = new_peak
        stats[h, 1:2, :] = rescale * stats[h, 1:2, :] + jnp.sum(weights, axis=0, keepdims=True)
        stats[h, 2:3, :] = rescale * stats[h, 2:3, :] + scale * jnp.sum(
            products, axis=0, keepdims=True
        )
        stats[h, 3:4, :] = rescale
        span = len(sources) * rows
        factors[0, 0:span] = weights.astype(jnp.bfloat16)
        factors[1, 0:span] = products.astype(jnp.bfloat16)

    def apply(h, sources):
        value = jnp.concatenate([vbuf[h, source] for source in sources], axis=1)
        span = len(sources) * rows
        both = dot(value, factors[0, 0:span])
        moved = dot(value[:HDIM], factors[1, 0:span])
        rescale = stats[h, 3:4, :]
        acc[h, 0:HDIM, :] = rescale * acc[h, 0:HDIM, :] + both[:HDIM]
        acc[h, HDIM:, :] = rescale * acc[h, HDIM:, :] + both[HDIM:] + scale * moved

    def finish(h):
        for slot in (1, 0):
            lanes = slice(slot * rows, (slot + 1) * rows)
            sums = stats[h, 1:2, lanes]
            inverse = jnp.where(sums > 0.0, 1.0 / jnp.where(sums > 0.0, sums, 1.0), 0.0)
            mean = stats[h, 2:3, lanes] * inverse
            primal = acc[h, 0:HDIM, lanes] * inverse
            tangent = acc[h, HDIM:, lanes] * inverse - mean * primal
            out_ref, stats_ref = ((own_o, own_stats), (o_send, s_send))[slot]
            out_ref[h, 0:HDIM, :] = primal.astype(out_ref.dtype)
            out_ref[h, HDIM:, :] = tangent.astype(out_ref.dtype)
            for i, row in enumerate((stats[h, 0:1, lanes], sums, mean)):
                stats_ref[h, i : i + 1, :] = row
            if slot == 1:
                for copy in o_copies(h):
                    copy.start()

    def merge(h):
        for copy in o_copies(h):
            copy.wait()
        peaks, sums, means = [], [], []
        for ref in (own_stats, s_recv):
            peaks.append(ref[h, 0:1, :])
            sums.append(ref[h, 1:2, :])
            means.append(ref[h, 2:3, :])
        peak = jnp.maximum(peaks[0], peaks[1])
        shares = [sums[i] * jnp.exp2(peaks[i] - peak) for i in range(2)]
        inverse = 1.0 / (shares[0] + shares[1])
        shares = [share * inverse for share in shares]
        mean = shares[0] * means[0] + shares[1] * means[1]
        primals = [own_o[h, 0:HDIM, :], o_recv[h, 0:HDIM, :].astype(jnp.float32)]
        tangents = [own_o[h, HDIM:, :], o_recv[h, HDIM:, :].astype(jnp.float32)]
        primal = shares[0] * primals[0] + shares[1] * primals[1]
        tangent = sum(
            shares[i] * (tangents[i] + (means[i] - mean) * primals[i]) for i in range(2)
        )
        gbuf[h, hd, 0:rows, :] = primal.T.astype(jnp.bfloat16)
        gbuf[h, hd, rows:, :] = tangent.T.astype(jnp.bfloat16)
        for i in range(1, n_head):
            g_copy(h, i).start()

    def project(h):
        for first in range(0, n_head, 2):
            sources = [(hd + n_head - i) % n_head for i in (first, first + 1)]
            for i in (first, first + 1):
                if i > 0:
                    g_copy(h, i).wait()
            features = jnp.concatenate([gbuf[h, source] for source in sources], axis=1)
            weight = jnp.concatenate(
                [
                    wbuf[h, pl.ds(pl.multiple_of(source * HDIM, HDIM), HDIM), :]
                    for source in sources
                ],
                axis=0,
            )
            total[...] += dot(features, weight)

    order_of = schedule(heads, depth)
    steps = len(order_of)
    finished = [order_of.index((h, depth)) for h in range(heads)]

    def place(index):
        h = d = 0
        for i, (head_at, hop_at) in enumerate(order_of):
            h = h + jnp.where(index == i, head_at, 0)
            d = d + jnp.where(index == i, hop_at, 0)
        return h, d

    def forward(h, d, piece):
        for side in range(2):
            crosses = (piece < 2) == (side == 0)

            def take(side=side, crosses=crosses):
                arrived = ring_copy(h, d - 1, piece, side)
                arrived.wait_recv()

                @pl.when(d < depth if crosses else d < depth - 1)
                def _():
                    ring_copy(h, d, piece, side).start()

                arrived.wait_send()

            if crosses:
                take()
            else:
                pl.when(d < depth)(take)

    def step(index, carry):
        h, d = place(index)
        old_h, old_d = carry
        far, near = [(z + nz - old_d) % nz], [(z + nz - old_d) % nz, (z + old_d) % nz]
        live = index < steps

        @pl.when(live)
        def _():
            forward(h, d, 0)

        @pl.when(index > 0)
        def _():
            @pl.when(old_d == 1)
            def _():
                stats[old_h, 0:1, :] = jnp.full((1, 2 * rows), NONE_SEEN, jnp.float32)
                stats[old_h, 1:3, :] = jnp.zeros((2, 2 * rows), jnp.float32)
                acc[old_h] = jnp.zeros((2 * HDIM, 2 * rows), jnp.float32)
                q_copy(old_h).wait()
                score(old_h, [z])
                apply(old_h, [z])

            @pl.when(old_d < depth)
            def _():
                score(old_h, near)

            @pl.when(old_d == depth)
            def _():
                score(old_h, far)

        @pl.when(live)
        def _():
            forward(h, d, 1)

        @pl.when(index > 0)
        def _():
            @pl.when(old_d < depth)
            def _():
                apply(old_h, near)

            @pl.when(old_d == depth)
            def _():
                apply(old_h, far)
                finish(old_h)

        @pl.when(live)
        def _():
            for piece in range(2, PIECES):
                forward(h, d, piece)

        @pl.when(jnp.logical_and(index == 0, core != 0))
        def _():
            for other in range(1, heads):
                send_own(other, range(PIECES))

        @pl.when(index == min(finished[0] + 2, steps))
        def _():
            for i in range(1, n_head):
                w_copy(i).wait()
                w_share(i).start()

        for early in range(heads - 1):

            @pl.when(index == min(finished[early] + 2, steps))
            def _(early=early):
                merge(early)

        return h, d

    lax.fori_loop(0, steps + 1, step, (jnp.int32(0), jnp.int32(1)))
    own_w.wait()
    for i in range(1, n_head):
        w_share(i).wait()
    project(0)
    merge(heads - 1)
    for h in range(1, heads):
        project(h)
    out[...] = total[...].astype(out.dtype)


def local(
    queries,
    keys,
    values,
    tan_queries,
    tan_keys,
    tan_values,
    out_weight,
    clip_lengths,
    stretch_order,
):
    rows, width = queries.shape
    heads = width // HDIM
    n_head = lax.axis_size("head")
    nz = lax.axis_size("ctx") // 2
    depth = nz // 2
    ncol = out_weight.shape[1] // n_head
    bf16, f32 = jnp.bfloat16, jnp.float32
    weight = out_weight.reshape(heads, HDIM, out_weight.shape[1])
    dma = pltpu.SemaphoreType.DMA
    anywhere = pl.BlockSpec(memory_space=pl.ANY)
    in_vmem = pl.BlockSpec(memory_space=pltpu.VMEM)
    both = pl.pallas_call(
        functools.partial(kernel, nz, n_head),
        out_shape=pltpu.VMEM((2 * rows, ncol), bf16),
        in_specs=[anywhere] * 9,
        out_specs=in_vmem,
        scratch_shapes=[
            pltpu.SMEM(clip_lengths.shape, jnp.int32),
            pltpu.SMEM(stretch_order.shape, jnp.int32),
            pltpu.VMEM((6, rows, width), bf16),
            pltpu.VMEM((2, heads, 2 * HDIM, rows), bf16),
            pltpu.VMEM((heads, nz, rows, 2 * HDIM), bf16),
            pltpu.VMEM((heads, nz, 2 * HDIM, rows), bf16),
            pltpu.VMEM((heads, n_head * HDIM, ncol), bf16),
            pltpu.VMEM((8, 2 * rows), jnp.int32),
            pltpu.VMEM((heads, 8, 2 * rows), f32),
            pltpu.VMEM((heads, 2 * HDIM, 2 * rows), f32),
            pltpu.VMEM((2, 2 * rows, 2 * rows), bf16),
            pltpu.VMEM((heads, 2 * HDIM, rows), f32),
            pltpu.VMEM((heads, 8, rows), f32),
            pltpu.VMEM((heads, 2 * HDIM, rows), bf16),
            pltpu.VMEM((heads, 8, rows), f32),
            pltpu.VMEM((heads, 2 * HDIM, rows), bf16),
            pltpu.VMEM((heads, 8, rows), f32),
            pltpu.VMEM((heads, n_head, 2 * rows, HDIM), bf16),
            pltpu.VMEM((2 * rows, ncol), f32),
            dma((8,)),
            dma((2, PIECES, 2 * heads)),
            dma((2, PIECES, heads * depth)),
            dma((2, heads)),
            dma((4, n_head - 1)),
            dma,
            dma((2, heads)),
            dma((2, heads)),
            dma((heads, n_head - 1)),
            dma((heads, n_head - 1)),
        ],
        compiler_params=pltpu.CompilerParams(
            collective_id=0,
            has_side_effects=True,
            vmem_limit_bytes=60 * 1024 * 1024,
        ),
        cost_estimate=pl.CostEstimate(
            flops=2 * 6 * 2 * rows * nz * rows * width + 4 * rows * n_head * width * ncol,
            bytes_accessed=8 * 1024 * 1024,
            transcendentals=2 * rows * nz * rows * heads,
        ),
    )(
        queries,
        keys,
        values,
        tan_queries,
        tan_keys,
        tan_values,
        weight,
        clip_lengths,
        stretch_order,
    )
    return both[:rows], both[rows:]


def solution(mesh):
    placed = P(("dp", "ctx"), "head")
    return jax.shard_map(
        local,
        mesh=mesh,
        in_specs=(placed,) * 6 + (P("head", None), P("dp"), P("dp")),
        out_specs=(placed, placed),
        check_vma=False,
    )
```

```python
import functools
import math

import jax
import jax.numpy as jnp
from jax import lax
from jax.experimental import pallas as pl
from jax.experimental.pallas import tpu as pltpu
from jax.sharding import PartitionSpec as P

HDIM = 128
PIECES = 4
NONE_SEEN = -1e29
MASKED = -1e30


def dot(a, b):
    return lax.dot_general(a, b, (((1,), (0,)), ((), ())), preferred_element_type=jnp.float32)


def turned(block):
    return block.astype(jnp.float32).T.astype(jnp.bfloat16)


def schedule(heads, depth):
    if heads != 3 or depth != 8:
        return [(h, d) for d in range(1, depth + 1) for h in range(heads)]
    turns = [0, 1, 0, 2] * 3 + [0, 1] * 2 + [1, 2] * 3 + [2, 2]
    return [(h, turns[: i + 1].count(h)) for i, h in enumerate(turns)]


def kernel(
    nz,
    n_head,
    q_in,
    k_in,
    v_in,
    tq_in,
    tk_in,
    tv_in,
    w_in,
    lengths_in,
    order_in,
    out,
    lengths,
    order,
    stage,
    qbuf,
    kbuf,
    vbuf,
    wbuf,
    bounds,
    stats,
    acc,
    factors,
    own_o,
    own_stats,
    o_send,
    s_send,
    o_recv,
    s_recv,
    gbuf,
    total,
    stage_sem,
    ring_send,
    ring_recv,
    q_sem,
    w_sem,
    w_own_sem,
    o_sem,
    s_sem,
    g_send,
    g_recv,
):
    rows = q_in.shape[0]
    heads = q_in.shape[1] // HDIM
    half = rows // 2
    clips = lengths.shape[0]
    depth = nz // 2
    ncol = wbuf.shape[2]
    w_half = HDIM // 2
    scale = 1.0 / HDIM**0.5

    ctx = lax.axis_index("ctx")
    hd = lax.axis_index("head")
    core = lax.axis_index("dp")
    column = ctx // nz
    z = ctx % nz
    right = column * nz + (z + 1) % nz
    left = column * nz + (z + nz - 1) % nz
    partner = (ctx + nz) % (2 * nz)

    stages = [
        pltpu.make_async_copy(ref, stage.at[i], stage_sem.at[i])
        for i, ref in enumerate((k_in, tk_in, v_in, tv_in, q_in, tq_in))
    ]
    tables = [
        pltpu.make_async_copy(src, dst, stage_sem.at[6 + i])
        for i, (src, dst) in enumerate(((lengths_in, lengths), (order_in, order)))
    ]
    for copy in stages + tables:
        copy.start()
    own_w = pltpu.make_async_copy(
        w_in.at[:, :, pl.ds(pl.multiple_of(hd * ncol, 128), ncol)],
        wbuf.at[:, pl.ds(pl.multiple_of(hd * HDIM, HDIM), HDIM), :],
        w_own_sem,
    )
    own_w.start()

    barrier = pltpu.get_barrier_semaphore()
    for other in (right, left, partner):
        pl.semaphore_signal(barrier, inc=1, device_id={"ctx": other})
    for i in range(1, n_head):
        pl.semaphore_signal(barrier, inc=1, device_id={"head": (hd + i) % n_head})
    pl.semaphore_signal(barrier, inc=1, device_id={"dp": 1 - core})

    def ring_copy(h, hop, piece, side):
        source = (z + nz - hop) % nz if side == 0 else (z + hop) % nz
        step = h * depth + hop
        buf = kbuf if piece < 2 else vbuf
        size = buf.shape[2] // 2
        ref = buf.at[h, source, pl.ds((piece % 2) * size, size), :]
        return pltpu.make_async_remote_copy(
            src_ref=ref,
            dst_ref=ref,
            send_sem=ring_send.at[side, piece, h * 2 + hop % 2],
            recv_sem=ring_recv.at[side, piece, step],
            device_id={"ctx": right if side == 0 else left},
        )

    def send_own(h, pieces):
        for piece in pieces:
            for side in range(2):
                ring_copy(h, 0, piece, side).start()

    def q_copy(h):
        return pltpu.make_async_remote_copy(
            src_ref=qbuf.at[0, h],
            dst_ref=qbuf.at[1, h],
            send_sem=q_sem.at[0, h],
            recv_sem=q_sem.at[1, h],
            device_id={"ctx": partner},
        )

    def w_copy(i):
        other = (hd + i) % n_head
        return pltpu.make_async_remote_copy(
            src_ref=w_in.at[
                :,
                pl.ds(pl.multiple_of(core * w_half, w_half), w_half),
                pl.ds(pl.multiple_of(other * ncol, 128), ncol),
            ],
            dst_ref=wbuf.at[:, pl.ds(pl.multiple_of(hd * HDIM + core * w_half, w_half), w_half), :],
            send_sem=w_sem.at[0, i - 1],
            recv_sem=w_sem.at[1, i - 1],
            device_id={"head": other},
        )

    def w_share(i):
        source = (hd + n_head - i) % n_head
        ref = wbuf.at[:, pl.ds(pl.multiple_of(source * HDIM + core * w_half, w_half), w_half), :]
        return pltpu.make_async_remote_copy(
            src_ref=ref,
            dst_ref=ref,
            send_sem=w_sem.at[2, i - 1],
            recv_sem=w_sem.at[3, i - 1],
            device_id={"dp": 1 - core},
        )

    def o_copies(h):
        return [
            pltpu.make_async_remote_copy(
                src_ref=src.at[h],
                dst_ref=dst.at[h],
                send_sem=sem.at[0, h],
                recv_sem=sem.at[1, h],
                device_id={"ctx": partner},
            )
            for src, dst, sem in ((s_send, s_recv, s_sem), (o_send, o_recv, o_sem))
        ]

    def g_copy(h, i):
        return pltpu.make_async_remote_copy(
            src_ref=gbuf.at[h, hd],
            dst_ref=gbuf.at[h, hd],
            send_sem=g_send.at[h, i - 1],
            recv_sem=g_recv.at[h, i - 1],
            device_id={"head": (hd + i) % n_head},
        )

    columns = [slice(h * HDIM, (h + 1) * HDIM) for h in range(heads)]
    for copy in stages[:2]:
        copy.wait()
    for h, cols in enumerate(columns):
        kbuf[h, z, :, 0:HDIM] = stage[0, :, cols]
        kbuf[h, z, :, HDIM : 2 * HDIM] = stage[1, :, cols]
    pl.semaphore_wait(barrier, 3 + n_head)
    send_own(0, range(2))
    for copy in stages[2:4]:
        copy.wait()
    for h, cols in enumerate(columns):
        vbuf[h, z, 0:HDIM, :] = turned(stage[2, :, cols])
        vbuf[h, z, HDIM : 2 * HDIM, :] = turned(stage[3, :, cols])
    send_own(0, range(2, PIECES))

    @pl.when(core == 0)
    def _():
        for h in range(1, heads):
            send_own(h, range(PIECES))

    for copy in stages[4:]:
        copy.wait()
    for h, cols in enumerate(columns):
        qbuf[0, h, 0:HDIM, :] = turned(stage[5, :, cols])
        qbuf[0, h, HDIM : 2 * HDIM, :] = turned(stage[4, :, cols])
        q_copy(h).start()
    for i in range(1, n_head):
        w_copy(i).start()
    for copy in tables:
        copy.wait()
    ends = []
    running = jnp.int32(0)
    for c in range(clips):
        running = running + lengths[c]
        ends.append(running)
    lane = lax.broadcasted_iota(jnp.int32, (1, rows), 1)
    for slot, index in enumerate((ctx, partner)):
        anchor = jnp.where(
            lane < half,
            order[2 * index] * half + lane,
            order[2 * index + 1] * half + lane - half,
        )
        low = jnp.zeros_like(anchor)
        high = jnp.full_like(anchor, rows * nz * 2)
        for end in ends:
            low = jnp.where(end <= anchor, jnp.maximum(low, end), low)
            high = jnp.where(end > anchor, jnp.minimum(high, end), high)
        bounds[0:1, slot * rows : (slot + 1) * rows] = low
        bounds[1:2, slot * rows : (slot + 1) * rows] = high

    total[...] = jnp.zeros_like(total)
    s_send[...] = jnp.zeros_like(s_send)

    def allowed_keys(source):
        low, high = bounds[0:1, :], bounds[1:2, :]
        index = column * nz + source
        position = lax.broadcasted_iota(jnp.int32, (half, 2 * rows), 0)
        parts = []
        for part in range(2):
            first = order[2 * index + part] * half
            parts.append(jnp.logical_and(position >= low - first, position < high - first))
        return parts

    def score(h, sources):
        key = jnp.concatenate([kbuf[h, source] for source in sources], axis=0)
        query = jnp.concatenate([qbuf[0, h], qbuf[1, h]], axis=1)
        scores = dot(key[:, :HDIM], query[HDIM:]) * (scale * math.log2(math.e))
        tan_scores = dot(key, query)
        masks = [mask for source in sources for mask in allowed_keys(source)]
        masked = jnp.concatenate(
            [
                jnp.where(mask, scores[i * half : (i + 1) * half], MASKED)
                for i, mask in enumerate(masks)
            ],
            axis=0,
        )
        peak = stats[h, 0:1, :]
        new_peak = jnp.maximum(peak, jnp.max(masked, axis=0, keepdims=True))
        weights = jnp.exp2(masked - new_peak)
        rescale = jnp.exp2(peak - new_peak)
        products = weights * tan_scores
        stats[h, 0:1, :] = new_peak
        stats[h, 1:2, :] = rescale * stats[h, 1:2, :] + jnp.sum(weights, axis=0, keepdims=True)
        stats[h, 2:3, :] = rescale * stats[h, 2:3, :] + scale * jnp.sum(
            products, axis=0, keepdims=True
        )
        stats[h, 3:4, :] = rescale
        span = len(sources) * rows
        factors[0, 0:span] = weights.astype(jnp.bfloat16)
        factors[1, 0:span] = products.astype(jnp.bfloat16)

    def apply(h, sources):
        value = jnp.concatenate([vbuf[h, source] for source in sources], axis=1)
        span = len(sources) * rows
        both = dot(value, factors[0, 0:span])
        moved = dot(value[:HDIM], factors[1, 0:span])
        rescale = stats[h, 3:4, :]
        acc[h, 0:HDIM, :] = rescale * acc[h, 0:HDIM, :] + both[:HDIM]
        acc[h, HDIM:, :] = rescale * acc[h, HDIM:, :] + both[HDIM:] + scale * moved

    def finish(h):
        for slot in (1, 0):
            lanes = slice(slot * rows, (slot + 1) * rows)
            sums = stats[h, 1:2, lanes]
            inverse = jnp.where(sums > 0.0, 1.0 / jnp.where(sums > 0.0, sums, 1.0), 0.0)
            mean = stats[h, 2:3, lanes] * inverse
            primal = acc[h, 0:HDIM, lanes] * inverse
            tangent = acc[h, HDIM:, lanes] * inverse - mean * primal
            out_ref, stats_ref = ((own_o, own_stats), (o_send, s_send))[slot]
            out_ref[h, 0:HDIM, :] = primal.astype(out_ref.dtype)
            out_ref[h, HDIM:, :] = tangent.astype(out_ref.dtype)
            for i, row in enumerate((stats[h, 0:1, lanes], sums, mean)):
                stats_ref[h, i : i + 1, :] = row
            if slot == 1:
                for copy in o_copies(h):
                    copy.start()

    def merge(h):
        for copy in o_copies(h):
            copy.wait()
        peaks, sums, means = [], [], []
        for ref in (own_stats, s_recv):
            peaks.append(ref[h, 0:1, :])
            sums.append(ref[h, 1:2, :])
            means.append(ref[h, 2:3, :])
        peak = jnp.maximum(peaks[0], peaks[1])
        shares = [sums[i] * jnp.exp2(peaks[i] - peak) for i in range(2)]
        inverse = 1.0 / (shares[0] + shares[1])
        shares = [share * inverse for share in shares]
        mean = shares[0] * means[0] + shares[1] * means[1]
        primals = [own_o[h, 0:HDIM, :], o_recv[h, 0:HDIM, :].astype(jnp.float32)]
        tangents = [own_o[h, HDIM:, :], o_recv[h, HDIM:, :].astype(jnp.float32)]
        primal = shares[0] * primals[0] + shares[1] * primals[1]
        tangent = sum(
            shares[i] * (tangents[i] + (means[i] - mean) * primals[i]) for i in range(2)
        )
        gbuf[h, hd, 0:rows, :] = primal.T.astype(jnp.bfloat16)
        gbuf[h, hd, rows:, :] = tangent.T.astype(jnp.bfloat16)
        for i in range(1, n_head):
            g_copy(h, i).start()

    def project(h):
        for first in range(0, n_head, 2):
            sources = [(hd + n_head - i) % n_head for i in (first, first + 1)]
            for i in (first, first + 1):
                if i > 0:
                    g_copy(h, i).wait()
            features = jnp.concatenate([gbuf[h, source] for source in sources], axis=1)
            weight = jnp.concatenate(
                [
                    wbuf[h, pl.ds(pl.multiple_of(source * HDIM, HDIM), HDIM), :]
                    for source in sources
                ],
                axis=0,
            )
            total[...] += dot(features, weight)

    order_of = schedule(heads, depth)
    steps = len(order_of)
    finished = [order_of.index((h, depth)) for h in range(heads)]

    def place(index):
        h = d = 0
        for i, (head_at, hop_at) in enumerate(order_of):
            h = h + jnp.where(index == i, head_at, 0)
            d = d + jnp.where(index == i, hop_at, 0)
        return h, d

    def forward(h, d, piece):
        for side in range(2):
            crosses = (piece < 2) == (side == 0)

            def take(side=side, crosses=crosses):
                arrived = ring_copy(h, d - 1, piece, side)
                arrived.wait_recv()

                @pl.when(d < depth if crosses else d < depth - 1)
                def _():
                    ring_copy(h, d, piece, side).start()

                arrived.wait_send()

            if crosses:
                take()
            else:
                pl.when(d < depth)(take)

    def step(index, carry):
        h, d = place(index)
        old_h, old_d = carry
        far, near = [(z + nz - old_d) % nz], [(z + nz - old_d) % nz, (z + old_d) % nz]
        live = index < steps

        @pl.when(live)
        def _():
            forward(h, d, 0)

        @pl.when(index > 0)
        def _():
            @pl.when(old_d == 1)
            def _():
                stats[old_h, 0:1, :] = jnp.full((1, 2 * rows), NONE_SEEN, jnp.float32)
                stats[old_h, 1:3, :] = jnp.zeros((2, 2 * rows), jnp.float32)
                acc[old_h] = jnp.zeros((2 * HDIM, 2 * rows), jnp.float32)
                q_copy(old_h).wait()
                score(old_h, [z])
                apply(old_h, [z])

            @pl.when(old_d < depth)
            def _():
                score(old_h, near)

            @pl.when(old_d == depth)
            def _():
                score(old_h, far)

        @pl.when(live)
        def _():
            forward(h, d, 1)

        @pl.when(index > 0)
        def _():
            @pl.when(old_d < depth)
            def _():
                apply(old_h, near)

            @pl.when(old_d == depth)
            def _():
                apply(old_h, far)
                finish(old_h)

        @pl.when(live)
        def _():
            for piece in range(2, PIECES):
                forward(h, d, piece)

        for other in range(1, heads):

            @pl.when(jnp.logical_and(index == order_of.index((other, 1)) - 1, core != 0))
            def _(other=other):
                send_own(other, range(PIECES))

        @pl.when(index == min(finished[0] + 2, steps))
        def _():
            for i in range(1, n_head):
                w_copy(i).wait()
                w_share(i).start()

        for early in range(heads - 1):

            @pl.when(index == min(finished[early] + 2, steps))
            def _(early=early):
                merge(early)

        return h, d

    lax.fori_loop(0, steps + 1, step, (jnp.int32(0), jnp.int32(1)))
    own_w.wait()
    for i in range(1, n_head):
        w_share(i).wait()
    project(0)
    merge(heads - 1)
    for h in range(1, heads):
        project(h)
    out[...] = total[...].astype(out.dtype)


def local(
    queries,
    keys,
    values,
    tan_queries,
    tan_keys,
    tan_values,
    out_weight,
    clip_lengths,
    stretch_order,
):
    rows, width = queries.shape
    heads = width // HDIM
    n_head = lax.axis_size("head")
    nz = lax.axis_size("ctx") // 2
    depth = nz // 2
    ncol = out_weight.shape[1] // n_head
    bf16, f32 = jnp.bfloat16, jnp.float32
    weight = out_weight.reshape(heads, HDIM, out_weight.shape[1])
    dma = pltpu.SemaphoreType.DMA
    anywhere = pl.BlockSpec(memory_space=pl.ANY)
    in_vmem = pl.BlockSpec(memory_space=pltpu.VMEM)
    both = pl.pallas_call(
        functools.partial(kernel, nz, n_head),
        out_shape=pltpu.VMEM((2 * rows, ncol), bf16),
        in_specs=[anywhere] * 9,
        out_specs=in_vmem,
        scratch_shapes=[
            pltpu.SMEM(clip_lengths.shape, jnp.int32),
            pltpu.SMEM(stretch_order.shape, jnp.int32),
            pltpu.VMEM((6, rows, width), bf16),
            pltpu.VMEM((2, heads, 2 * HDIM, rows), bf16),
            pltpu.VMEM((heads, nz, rows, 2 * HDIM), bf16),
            pltpu.VMEM((heads, nz, 2 * HDIM, rows), bf16),
            pltpu.VMEM((heads, n_head * HDIM, ncol), bf16),
            pltpu.VMEM((8, 2 * rows), jnp.int32),
            pltpu.VMEM((heads, 8, 2 * rows), f32),
            pltpu.VMEM((heads, 2 * HDIM, 2 * rows), f32),
            pltpu.VMEM((2, 2 * rows, 2 * rows), bf16),
            pltpu.VMEM((heads, 2 * HDIM, rows), f32),
            pltpu.VMEM((heads, 8, rows), f32),
            pltpu.VMEM((heads, 2 * HDIM, rows), bf16),
            pltpu.VMEM((heads, 8, rows), f32),
            pltpu.VMEM((heads, 2 * HDIM, rows), bf16),
            pltpu.VMEM((heads, 8, rows), f32),
            pltpu.VMEM((heads, n_head, 2 * rows, HDIM), bf16),
            pltpu.VMEM((2 * rows, ncol), f32),
            dma((8,)),
            dma((2, PIECES, 2 * heads)),
            dma((2, PIECES, heads * depth)),
            dma((2, heads)),
            dma((4, n_head - 1)),
            dma,
            dma((2, heads)),
            dma((2, heads)),
            dma((heads, n_head - 1)),
            dma((heads, n_head - 1)),
        ],
        compiler_params=pltpu.CompilerParams(
            collective_id=0,
            has_side_effects=True,
            vmem_limit_bytes=60 * 1024 * 1024,
        ),
        cost_estimate=pl.CostEstimate(
            flops=2 * 6 * 2 * rows * nz * rows * width + 4 * rows * n_head * width * ncol,
            bytes_accessed=8 * 1024 * 1024,
            transcendentals=2 * rows * nz * rows * heads,
        ),
    )(
        queries,
        keys,
        values,
        tan_queries,
        tan_keys,
        tan_values,
        weight,
        clip_lengths,
        stretch_order,
    )
    return both[:rows], both[rows:]


def solution(mesh):
    placed = P(("dp", "ctx"), "head")
    return jax.shard_map(
        local,
        mesh=mesh,
        in_specs=(placed,) * 6 + (P("head", None), P("dp"), P("dp")),
        out_specs=(placed, placed),
        check_vma=False,
    )
```
